512 devices in a mesh: view: 8 (over x, y_hi), row: 16 (over z, core), mat: 4 (over y_lo).
Axes of the slice: x: 4, y: 8 (y_hi: 2, y_lo: 4; y = y_hi * 4 + y_lo), z: 8, core: 2. Of those that a mesh axis runs over, the one named last changes fastest.
Arguments:
- volume: float32 [512, 3, 2048], P(('row', 'mat')), may hold values from 0 to 1
- projector: bfloat16 [32, 1024, 2048], P(('view', 'mat')), may hold values from -0.125 to 0.125
- counts: bfloat16 [32, 512, 4, 1024], P(('view', 'mat'), 'row'), may hold values from 0.049804688 to 1
- atten: float32 [4, 3], replicated, may hold values from 0.1 to 1
- newton: bfloat16 [512, 3, 3, 2048], P(('row', 'mat')), may hold values from -0.25 to 0.80078125, as said below
Outputs:
- updated: float32 [512, 3, 2048], P(('row', 'mat'))
The draws below stay inside these ranges and needn't reach their ends.
Inputs may be any that keep to these rules, and one draw needn't show every extreme that they name: newton is symmetric in its two material dimensions; after rounding to bfloat16 its diagonal lies in 0.2 to 0.80078125 and each off-diagonal entry is at most about 0.3 times the root of the two diagonal entries in magnitude.
All inputs are finite; a program needn't handle non-finite values.
Results may differ from the reference program's by a relative error of at most 0.0028.
The reference program's roundings to bfloat16 on the way (of `x_half` and `resid`) count: a program that leaves them out, or rounds other values in their place, can miss the bound.
Values may be sent and summed in bfloat16 or wider, within the bound.
No kernel may reach another device: no remote copies, remote signals or barrier semaphores. Data moves between devices by JAX's collectives and lax.ppermute only.
A program may use at most 64 MiB of HBM per device.

```python
import math
import jax
import jax.numpy as jnp
from jax import lax

M = 3
B = 4
U = 1024
PX = 1024
PY = 2
PIX = 2048
VIEWS = 32
Z = 512


def draw_newton(key, part):
    first_key, second_key = jax.random.split(jax.random.fold_in(key, 17))
    diag = jnp.exp(jax.random.uniform(first_key, (Z, M, PIX), jnp.float32, jnp.log(0.2), jnp.log(0.8)))
    couple = jax.random.uniform(second_key, (Z, M, M, PIX), jnp.float32, -1.0, 1.0)
    couple = 0.5 * (couple + jnp.swapaxes(couple, 1, 2))
    root = jnp.sqrt(diag)
    scaled = 0.3 * couple * root[:, :, None, :] * root[:, None, :, :]
    ident = jnp.eye(M, dtype=jnp.float32)[None, :, :, None]
    whole = scaled * (1.0 - ident) + ident * diag[:, :, None, :]
    return whole.astype(jnp.bfloat16)


def level_of(key, extent, cuts, least, high):
    gain = 1.0
    for dim, shards_of in cuts:
        draws = jax.random.uniform(jax.random.fold_in(jax.random.fold_in(key, 6), dim), (shards_of,), jnp.float32, least / len(cuts), high / len(cuts))
        gain = gain * jnp.repeat(jnp.exp(draws), extent[dim] // shards_of).reshape((-1,) + (1,) * (len(extent) - 1 - dim))
    return gain


def gaussian(own_key, dims, scale, limit, shards=(), held_as=jnp.bfloat16):
    result = scale * jax.random.normal(own_key, dims, jnp.float32)
    if shards:
        result = result * level_of(own_key, dims, shards, -0.22, 0.18)
    return jnp.clip(result, -limit, limit).astype(held_as)


def setup_inputs(seed: int = 0) -> dict:
    splits = jax.random.split(jax.random.key(seed), 6)
    volume = jnp.clip(1.0 * jax.random.uniform(splits[0], (Z, M, PIX), jnp.float32) ** level_of(splits[0], (Z, M, PIX), ((0, 64),), -0.2, 0.2), 0.0, 1.0)
    projector = gaussian(splits[1], (VIEWS, U, PIX), PIX ** -0.5, 0.125, ((0, 32),))
    counts = jnp.clip(0.049804688 + 0.9501953 * jax.random.uniform(splits[2], (VIEWS, Z, B, U), jnp.float32) ** level_of(splits[2], (VIEWS, Z, B, U), ((0, 32), (1, 16)), -0.2, 0.2), 0.049804688, 1.0).astype(jnp.bfloat16)
    atten = jnp.clip(jnp.exp(jax.random.uniform(splits[3], (B, M), jnp.float32, math.log(0.1), math.log(1.0))), 0.1, 1.0)
    newton = draw_newton(jax.random.fold_in(splits[5], 71), 0)
    return dict(volume=volume, projector=projector, counts=counts, atten=atten, newton=newton)


HIGH = lax.Precision.HIGHEST

def reference(volume, projector, counts, atten, newton):
    x_half = volume.astype(jnp.bfloat16).astype(jnp.float32)

    def one_view(total, material_pair_index):
        pixel_block_slice, measured_photon_counts = material_pair_index
        blockf = pixel_block_slice.astype(jnp.float32)
        line = jnp.einsum('zmp,up->zmu', x_half, blockf, precision=HIGH)
        expected_counts_model = jnp.exp(-jnp.einsum('bm,zmu->zbu', atten, line, precision=HIGH))
        forward_difference = measured_photon_counts.astype(jnp.float32) - expected_counts_model
        resid = jnp.einsum('bm,zbu->zmu', atten, forward_difference, precision=HIGH)
        resid = resid.astype(jnp.bfloat16).astype(jnp.float32)
        total = total + jnp.einsum('zmu,up->zmp', resid, blockf, precision=HIGH)
        return (total, None)
    start = jnp.zeros((Z, M, PIX), jnp.float32)
    total, unused = lax.scan(one_view, start, (projector, counts))
    grad = total * float(VIEWS) ** (-0.5)
    field = volume.reshape(Z, M, PY, PX)
    pad_z = jnp.pad(field, ((0, 1), (0, 0), (0, 0), (0, 0)))
    pad_y = jnp.pad(field, ((0, 0), (0, 0), (0, 1), (0, 0)))
    pad_x = jnp.pad(field, ((0, 0), (0, 0), (0, 0), (0, 1)))
    diff_z = pad_z[1:] - pad_z[:-1]
    diff_y = pad_y[:, :, 1:] - pad_y[:, :, :-1]
    diff_x = pad_x[:, :, :, 1:] - pad_x[:, :, :, :-1]
    scale = jnp.sqrt(0.25 + lax.optimization_barrier(jnp.sum(diff_z * diff_z + diff_y * diff_y + diff_x * diff_x, axis=1, keepdims=True)))
    flux_z = diff_z / scale
    flux_y = diff_y / scale
    flux_x = diff_x / scale
    prev_z = jnp.pad(flux_z, ((1, 0), (0, 0), (0, 0), (0, 0)))[:-1]
    prev_y = jnp.pad(flux_y, ((0, 0), (0, 0), (1, 0), (0, 0)))[:, :, :-1]
    prev_x = jnp.pad(flux_x, ((0, 0), (0, 0), (0, 0), (1, 0)))[:, :, :, :-1]
    smooth = prev_z - flux_z + (prev_y - flux_y) + (prev_x - flux_x)
    smooth = smooth.reshape(Z, M, PIX)
    step_dir = grad + 0.5 * smooth
    hess = newton.astype(jnp.float32)
    return volume - lax.optimization_barrier(jnp.sum(hess * step_dir[:, None], axis=2))
```

```python
import functools

import jax
import jax.numpy as jnp
from jax import lax
from jax.experimental import pallas as pl
from jax.experimental.pallas import tpu as pltpu
from jax.sharding import PartitionSpec as P

PX = 1024
BF16 = jnp.bfloat16
F32 = jnp.float32
VMEM = pl.BlockSpec(memory_space=pltpu.VMEM)
SMEM = pl.BlockSpec(memory_space=pltpu.SMEM)
LIMIT = 40 * 1024 * 1024


def project_kernel(mats, bins, slabs, atten_ref, x_ref, proj_ref, counts_ref, out_ref, resid_ref):
    rows, pix = x_ref.shape
    cols = proj_ref.shape[0]
    per_slab = rows // slabs
    depth = per_slab // mats
    wide = 256
    for at in range(0, cols, wide):
        line = lax.dot_general(
            x_ref[...], proj_ref[at : at + wide, :], (((1,), (1,)), ((), ())), preferred_element_type=F32
        )
        blocks = []
        for slab in range(slabs):
            lines = [line[slab * per_slab + m * depth :][:depth] for m in range(mats)]
            parts = [None] * mats
            for b in range(bins):
                power = atten_ref[b, 0] * lines[0]
                for m in range(1, mats):
                    power = power + atten_ref[b, m] * lines[m]
                seen = counts_ref[b, slab * depth : (slab + 1) * depth, at : at + wide]
                diff = seen - jnp.exp(-power)
                for m in range(mats):
                    term = atten_ref[b, m] * diff
                    parts[m] = term if parts[m] is None else parts[m] + term
            blocks += parts
        resid_ref[:, at : at + wide] = jnp.concatenate(blocks, 0).astype(BF16)
    owners = out_ref.shape[0]
    span = pix // owners
    for owner in range(owners):
        back = jnp.dot(
            resid_ref[...], proj_ref[:, owner * span : (owner + 1) * span], preferred_element_type=F32
        )
        for slab in range(slabs):
            out_ref[owner, slab] = back[slab * per_slab : (slab + 1) * per_slab].astype(BF16)


def project(atten, x_all, projector, counts, owners, slabs, mats):
    rows, pix = x_all.shape
    cols = projector.shape[0]
    return pl.pallas_call(
        functools.partial(project_kernel, mats, counts.shape[0], slabs),
        out_shape=jax.ShapeDtypeStruct((owners, slabs, rows // slabs, pix // owners), BF16),
        in_specs=[SMEM, VMEM, VMEM, VMEM],
        out_specs=VMEM,
        scratch_shapes=[pltpu.VMEM((rows, cols), BF16)],
        compiler_params=pltpu.CompilerParams(vmem_limit_bytes=LIMIT),
        cost_estimate=pl.CostEstimate(
            flops=4 * rows * cols * pix, bytes_accessed=2 * cols * pix, transcendentals=rows * cols
        ),
    )(atten, x_all, projector, counts)


def next_pixel(field):
    column = lax.broadcasted_iota(jnp.int32, field.shape, 1) % PX
    return jnp.where(column == PX - 1, 0.0, pltpu.roll(field, field.shape[1] - 1, 1))


def next_row(field):
    return jnp.concatenate([field[:, PX:], jnp.zeros((field.shape[0], PX), F32)], 1)


def prev_pixel(flux):
    column = lax.broadcasted_iota(jnp.int32, flux.shape, 1) % PX
    return jnp.where(column == 0, 0.0, pltpu.roll(flux, 1, 1))


def prev_row(flux):
    return jnp.concatenate([jnp.zeros((flux.shape[0], PX), F32), flux[:, :-PX]], 1)


def smooth_kernel(where_ref, vol_ref, x_ref, edge_ref, out_ref):
    mats, depth, pix = vol_ref.shape
    slabs = x_ref.shape[0] // (mats * depth)
    slab, first = where_ref[0], where_ref[1]
    row = lax.broadcasted_iota(jnp.int32, (depth, pix), 0)
    vol, above, below = [], [], []
    for m in range(mats):
        vol.append(vol_ref[m])
        up = down = edge_ref[m : m + 1]
        for other in range(1, slabs):
            at = (other * mats + m) * depth
            up = jnp.where(slab == other - 1, x_ref[at : at + depth].astype(F32)[:1], up)
            at = ((other - 1) * mats + m) * depth
            down = jnp.where(slab == other, x_ref[at : at + depth].astype(F32)[-1:], down)
        above.append(jnp.where(row == depth - 1, up, pltpu.roll(vol[m], depth - 1, 0)))
        below.append(down)
    square = jnp.full((depth, pix), 0.25, F32)
    square_below = jnp.full((1, pix), 0.25, F32)
    diffs, steps = [], []
    for m in range(mats):
        dz, dy, dx = above[m] - vol[m], next_row(vol[m]) - vol[m], next_pixel(vol[m]) - vol[m]
        square = square + (dz * dz + dy * dy + dx * dx)
        diffs.append((dz, dy, dx))
        dz, dy, dx = vol[m][:1] - below[m], next_row(below[m]) - below[m], next_pixel(below[m]) - below[m]
        square_below = square_below + (dz * dz + dy * dy + dx * dx)
        steps.append(dz)
    scale = lax.rsqrt(square)
    scale_below = jnp.where(first == 1, 0.0, lax.rsqrt(square_below))
    for m in range(mats):
        qz, qy, qx = (d * scale for d in diffs[m])
        prev_z = jnp.where(row == 0, steps[m] * scale_below, pltpu.roll(qz, 1, 0))
        out_ref[m] = prev_z - qz + (prev_row(qy) - qy) + (prev_pixel(qx) - qx)


def smooth(where, volume, x_all, edge):
    return pl.pallas_call(
        smooth_kernel,
        out_shape=jax.ShapeDtypeStruct(volume.shape, F32),
        in_specs=[SMEM, VMEM, VMEM, VMEM],
        out_specs=VMEM,
        compiler_params=pltpu.CompilerParams(vmem_limit_bytes=LIMIT),
        cost_estimate=pl.CostEstimate(
            flops=40 * volume.size, bytes_accessed=12 * volume.size, transcendentals=volume.size
        ),
    )(where, volume, x_all, edge)


def total_kernel(factor, part_ref, out_ref):
    total = jnp.sum(part_ref[...].astype(F32), axis=0) * factor
    total = total.astype(BF16)
    for copy in range(out_ref.shape[0]):
        out_ref[copy] = total


def total_copies(parts, factor, copies):
    return pl.pallas_call(
        functools.partial(total_kernel, factor),
        out_shape=jax.ShapeDtypeStruct((copies,) + parts.shape[1:], BF16),
        in_specs=[VMEM],
        out_specs=VMEM,
        compiler_params=pltpu.CompilerParams(vmem_limit_bytes=LIMIT),
    )(parts)


def step_kernel(grad_ref, smooth_ref, newton_ref, vol_ref, out_ref):
    mats, depth, pix = vol_ref.shape
    span = grad_ref.shape[2]
    for owner in range(grad_ref.shape[0]):
        own = slice(owner * span, (owner + 1) * span)
        grad = grad_ref[owner].astype(F32)
        steps = [grad[k * depth : (k + 1) * depth] + 0.5 * smooth_ref[k, :, own] for k in range(mats)]
        for m in range(mats):
            moved = newton_ref[m, 0, :, own].astype(F32) * steps[0]
            for k in range(1, mats):
                moved = moved + newton_ref[m, k, :, own].astype(F32) * steps[k]
            out_ref[m, :, own] = vol_ref[m, :, own] - moved


def newton_step(grad, smoothed, newton, volume):
    return pl.pallas_call(
        step_kernel,
        out_shape=jax.ShapeDtypeStruct(volume.shape, F32),
        in_specs=[VMEM] * 4,
        out_specs=VMEM,
        compiler_params=pltpu.CompilerParams(vmem_limit_bytes=LIMIT),
    )(grad, smoothed, newton, volume)


def body(volume, projector, counts, atten, newton):
    depth, mats, pix = volume.shape
    owners, slabs, groups = (lax.axis_size(name) for name in ("view", "mat", "row"))
    views_all = projector.shape[0] * owners * slabs
    slab, group = lax.axis_index("mat"), lax.axis_index("row")
    vol = volume.transpose(1, 0, 2)
    x_all = lax.all_gather(vol.astype(BF16).reshape(mats * depth, pix), "mat", axis=0, tiled=True)
    counts_binned = counts[0].astype(F32).transpose(1, 0, 2)
    parts = project(atten, x_all, projector[0], counts_binned, owners, slabs, mats)
    parts = parts.reshape(owners * slabs, mats * depth, pix // owners)
    parts = lax.all_to_all(parts, ("view", "mat"), 0, 0, tiled=True)
    mine = total_copies(parts, float(views_all) ** (-0.5), owners)
    grad = lax.all_to_all(mine, "view", 0, 0, tiled=True)
    edge = jnp.where(slab == 0, vol[:, 0], vol[:, -1])
    pairs = []
    for g in range(groups - 1):
        last, start = g * slabs + slabs - 1, (g + 1) * slabs
        pairs += [(last, start), (start, last)]
    edge = lax.ppermute(edge, ("row", "mat"), pairs)
    is_first = jnp.logical_and(slab == 0, group == 0).astype(jnp.int32)
    smoothed = smooth(jnp.stack([slab, is_first]).astype(jnp.int32), vol, x_all, edge)
    updated = newton_step(grad, smoothed, newton.transpose(1, 2, 0, 3), vol)
    return updated.transpose(1, 0, 2)


def solution(mesh):
    in_specs = (
        P(("row", "mat"), None, None),
        P(("view", "mat"), None, None),
        P(("view", "mat"), "row", None, None),
        P(),
        P(("row", "mat"), None, None, None),
    )
    out_specs = P(("row", "mat"), None, None)
    return jax.shard_map(body, mesh=mesh, in_specs=in_specs, out_specs=out_specs, check_vma=False)
```

```python
import functools

import jax
import jax.numpy as jnp
from jax import lax
from jax.experimental import pallas as pl
from jax.experimental.pallas import tpu as pltpu
from jax.sharding import PartitionSpec as P

PX = 1024
BF16 = jnp.bfloat16
F32 = jnp.float32
VMEM = pl.BlockSpec(memory_space=pltpu.VMEM)
SMEM = pl.BlockSpec(memory_space=pltpu.SMEM)
SMALL = 8 * 1024 * 1024
LARGE = 52 * 1024 * 1024


def spread_kernel(vol_ref, out_ref):
    mats, depth, _ = vol_ref.shape
    rounded = jnp.concatenate([vol_ref[m] for m in range(mats)], 0).astype(BF16)
    for copy in range(out_ref.shape[0]):
        out_ref[copy] = rounded


def spread(volume, copies):
    mats, depth, pix = volume.shape
    return pl.pallas_call(
        spread_kernel,
        out_shape=jax.ShapeDtypeStruct((copies, mats * depth, pix), BF16),
        in_specs=[VMEM],
        out_specs=VMEM,
        compiler_params=pltpu.CompilerParams(vmem_limit_bytes=SMALL),
    )(volume)


def tiles_kernel(atten_ref, tiles_ref):
    bins, mats = atten_ref.shape
    for b in range(bins):
        for m in range(mats):
            tiles_ref[b * mats + m] = jnp.full(tiles_ref.shape[1:], atten_ref[b, m], F32)


def attenuation_tiles(atten):
    return pl.pallas_call(
        tiles_kernel,
        out_shape=jax.ShapeDtypeStruct((atten.size, 8, 128), F32),
        in_specs=[SMEM],
        out_specs=VMEM,
        compiler_params=pltpu.CompilerParams(vmem_limit_bytes=SMALL),
    )(atten)


def wide_tile(tile, wide):
    return jnp.concatenate([tile] * (wide // tile.shape[1]), 1)


def project_kernel(mats, bins, slabs, tiles_ref, x_ref, proj_ref, counts_ref, out_ref, resid_ref, near_ref, sems):
    rows, pix = x_ref.shape
    cols = proj_ref.shape[0]
    per_slab = rows // slabs
    depth = per_slab // mats
    wide = cols // sems.shape[0]
    copies_in = [
        pltpu.make_async_copy(
            proj_ref.at[at : at + wide], near_ref.at[at : at + wide], sems.at[at // wide]
        )
        for at in range(0, cols, wide)
    ]
    for copy_in in copies_in:
        copy_in.start()
    atten = [[wide_tile(tiles_ref[b * mats + m], wide) for m in range(mats)] for b in range(bins)]
    for at in range(0, cols, wide):
        copies_in[at // wide].wait()
        line = lax.dot_general(
            x_ref[...], near_ref[at : at + wide, :], (((1,), (1,)), ((), ())), preferred_element_type=F32
        )
        blocks = []
        for slab in range(slabs):
            lines = [line[slab * per_slab + m * depth :][:depth] for m in range(mats)]
            parts = [None] * mats
            for b in range(bins):
                power = atten[b][0] * lines[0]
                for m in range(1, mats):
                    power = power + atten[b][m] * lines[m]
                seen = counts_ref[b, slab * depth : (slab + 1) * depth, at : at + wide]
                diff = seen - jnp.exp(-power)
                for m in range(mats):
                    term = atten[b][m] * diff
                    parts[m] = term if parts[m] is None else parts[m] + term
            blocks += parts
        resid_ref[:, at : at + wide] = jnp.concatenate(blocks, 0).astype(BF16)
    owners, copies, _, _, span = out_ref.shape
    for owner in range(owners):
        back = jnp.dot(
            resid_ref[...], near_ref[:, owner * span : (owner + 1) * span], preferred_element_type=F32
        )
        for slab in range(slabs):
            part = back[slab * per_slab : (slab + 1) * per_slab].astype(BF16)
            for copy in range(copies):
                out_ref[owner, copy, slab] = part


def project(tiles, x_all, projector, counts, owners, copies, slabs, mats):
    rows, pix = x_all.shape
    cols = projector.shape[0]
    return pl.pallas_call(
        functools.partial(project_kernel, mats, counts.shape[0], slabs),
        out_shape=jax.ShapeDtypeStruct((owners, copies, slabs, rows // slabs, pix // owners), BF16),
        in_specs=[VMEM, VMEM, pl.BlockSpec(memory_space=pltpu.HBM), VMEM],
        out_specs=VMEM,
        scratch_shapes=[
            pltpu.VMEM((rows, cols), BF16),
            pltpu.VMEM((cols, pix), BF16),
            pltpu.SemaphoreType.DMA((4,)),
        ],
        compiler_params=pltpu.CompilerParams(vmem_limit_bytes=LARGE),
        cost_estimate=pl.CostEstimate(
            flops=4 * rows * cols * pix, bytes_accessed=2 * cols * pix, transcendentals=rows * cols
        ),
    )(tiles, x_all, projector, counts)


def next_pixel(field):
    column = lax.broadcasted_iota(jnp.int32, field.shape, 1) % PX
    return jnp.where(column == PX - 1, 0.0, pltpu.roll(field, field.shape[1] - 1, 1))


def next_row(field):
    return jnp.concatenate([field[:, PX:], jnp.zeros((field.shape[0], PX), F32)], 1)


def prev_pixel(flux):
    column = lax.broadcasted_iota(jnp.int32, flux.shape, 1) % PX
    return jnp.where(column == 0, 0.0, pltpu.roll(flux, 1, 1))


def prev_row(flux):
    return jnp.concatenate([jnp.zeros((flux.shape[0], PX), F32), flux[:, :-PX]], 1)


def smooth_kernel(where_ref, vol_ref, x_ref, edge_ref, out_ref):
    mats, depth, pix = vol_ref.shape
    slabs = x_ref.shape[0] // (mats * depth)
    slab, first = where_ref[0], where_ref[1]
    row = lax.broadcasted_iota(jnp.int32, (depth, pix), 0)
    vol, above, below = [], [], []
    for m in range(mats):
        vol.append(vol_ref[m])
        up = down = edge_ref[m : m + 1]
        for other in range(1, slabs):
            at = (other * mats + m) * depth
            up = jnp.where(slab == other - 1, x_ref[at : at + depth].astype(F32)[:1], up)
            at = ((other - 1) * mats + m) * depth
            down = jnp.where(slab == other, x_ref[at : at + depth].astype(F32)[-1:], down)
        above.append(jnp.where(row == depth - 1, up, pltpu.roll(vol[m], depth - 1, 0)))
        below.append(down)
    square = jnp.full((depth, pix), 0.25, F32)
    square_below = jnp.full((1, pix), 0.25, F32)
    diffs, steps = [], []
    for m in range(mats):
        dz, dy, dx = above[m] - vol[m], next_row(vol[m]) - vol[m], next_pixel(vol[m]) - vol[m]
        square = square + (dz * dz + dy * dy + dx * dx)
        diffs.append((dz, dy, dx))
        dz, dy, dx = vol[m][:1] - below[m], next_row(below[m]) - below[m], next_pixel(below[m]) - below[m]
        square_below = square_below + (dz * dz + dy * dy + dx * dx)
        steps.append(dz)
    scale = lax.rsqrt(square)
    scale_below = jnp.where(first == 1, 0.0, lax.rsqrt(square_below))
    for m in range(mats):
        qz, qy, qx = (d * scale for d in diffs[m])
        prev_z = jnp.where(row == 0, steps[m] * scale_below, pltpu.roll(qz, 1, 0))
        out_ref[m] = prev_z - qz + (prev_row(qy) - qy) + (prev_pixel(qx) - qx)


def smooth(where, volume, x_all, edge):
    return pl.pallas_call(
        smooth_kernel,
        out_shape=jax.ShapeDtypeStruct(volume.shape, F32),
        in_specs=[SMEM, VMEM, VMEM, VMEM],
        out_specs=VMEM,
        compiler_params=pltpu.CompilerParams(vmem_limit_bytes=SMALL),
        cost_estimate=pl.CostEstimate(
            flops=40 * volume.size, bytes_accessed=12 * volume.size, transcendentals=volume.size
        ),
    )(where, volume, x_all, edge)


def total_kernel(factor, part_ref, out_ref):
    total = jnp.sum(part_ref[...].astype(F32), axis=0) * factor
    total = total.astype(BF16)
    for copy in range(out_ref.shape[0]):
        out_ref[copy] = total


def total_copies(parts, factor, copies):
    return pl.pallas_call(
        functools.partial(total_kernel, factor),
        out_shape=jax.ShapeDtypeStruct((copies,) + parts.shape[1:], BF16),
        in_specs=[VMEM],
        out_specs=VMEM,
        compiler_params=pltpu.CompilerParams(vmem_limit_bytes=SMALL),
    )(parts)


def step_kernel(grad_ref, smooth_ref, newton_ref, vol_ref, out_ref):
    mats, depth, pix = vol_ref.shape
    span = grad_ref.shape[2]
    for owner in range(grad_ref.shape[0]):
        own = slice(owner * span, (owner + 1) * span)
        grad = grad_ref[owner].astype(F32)
        steps = [grad[k * depth : (k + 1) * depth] + 0.5 * smooth_ref[k, :, own] for k in range(mats)]
        for m in range(mats):
            moved = newton_ref[m, 0, :, own].astype(F32) * steps[0]
            for k in range(1, mats):
                moved = moved + newton_ref[m, k, :, own].astype(F32) * steps[k]
            out_ref[m, :, own] = vol_ref[m, :, own] - moved


def newton_step(grad, smoothed, newton, volume):
    return pl.pallas_call(
        step_kernel,
        out_shape=jax.ShapeDtypeStruct(volume.shape, F32),
        in_specs=[VMEM] * 4,
        out_specs=VMEM,
        compiler_params=pltpu.CompilerParams(vmem_limit_bytes=SMALL),
    )(grad, smoothed, newton, volume)


def body(volume, projector, counts, atten, newton):
    depth, mats, pix = volume.shape
    owners, copies, slabs, groups = (lax.axis_size(name) for name in ("x", "half", "mat", "row"))
    views_all = projector.shape[0] * owners * copies * slabs
    slab, group = lax.axis_index("mat"), lax.axis_index("row")
    rows = mats * depth
    vol = volume.transpose(1, 0, 2)
    x_all = lax.all_to_all(spread(vol, slabs), "mat", 0, 0, tiled=True)
    x_all = x_all.reshape(slabs * rows, pix)
    counts_binned = counts[0].astype(F32).transpose(1, 0, 2)
    parts = project(attenuation_tiles(atten), x_all, projector[0], counts_binned, owners, copies, slabs, mats)
    parts = parts.reshape(owners * copies * slabs, rows, pix // owners)
    parts = lax.all_to_all(parts, ("x", "half", "mat"), 0, 0, tiled=True)
    mine = total_copies(parts, float(views_all) ** (-0.5), owners)
    grad = lax.all_to_all(mine, "x", 0, 0, tiled=True)
    edge = jnp.where(slab == 0, vol[:, 0], vol[:, -1])
    pairs = []
    for g in range(groups - 1):
        last, start = g * slabs + slabs - 1, (g + 1) * slabs
        pairs += [(last, start), (start, last)]
    edge = lax.ppermute(edge, ("row", "mat"), pairs)
    is_first = jnp.logical_and(slab == 0, group == 0).astype(jnp.int32)
    smoothed = smooth(jnp.stack([slab, is_first]).astype(jnp.int32), vol, x_all, edge)
    updated = newton_step(grad, smoothed, newton.transpose(1, 2, 0, 3), vol)
    return updated.transpose(1, 0, 2)


def solution(mesh):
    shape = mesh.devices.shape
    mesh = jax.sharding.Mesh(
        mesh.devices.reshape(shape[0] // 2, 2, *shape[1:]), ("x", "half", "row", "mat")
    )
    view = ("x", "half", "mat")
    in_specs = (
        P(("row", "mat"), None, None),
        P(view, None, None),
        P(view, "row", None, None),
        P(),
        P(("row", "mat"), None, None, None),
    )
    out_specs = P(("row", "mat"), None, None)
    return jax.shard_map(body, mesh=mesh, in_specs=in_specs, out_specs=out_specs, check_vma=False)
```

```python
import functools

import jax
import jax.numpy as jnp
from jax import lax
from jax.experimental import pallas as pl
from jax.experimental.pallas import tpu as pltpu
from jax.sharding import PartitionSpec as P

PX = 1024
BF16 = jnp.bfloat16
F32 = jnp.float32
VMEM = pl.BlockSpec(memory_space=pltpu.VMEM)
SMEM = pl.BlockSpec(memory_space=pltpu.SMEM)
SMALL = 8 * 1024 * 1024
MEDIUM = 49 * 1024 * 1024
LARGE = 47 * 1024 * 1024


def spread_kernel(vol_ref, out_ref):
    mats, depth, _ = vol_ref.shape
    rounded = jnp.concatenate([vol_ref[m] for m in range(mats)], 0).astype(BF16)
    for copy in range(out_ref.shape[0]):
        out_ref[copy] = rounded


def spread(volume, copies):
    mats, depth, pix = volume.shape
    return pl.pallas_call(
        spread_kernel,
        out_shape=jax.ShapeDtypeStruct((copies, mats * depth, pix), BF16),
        in_specs=[VMEM],
        out_specs=VMEM,
        compiler_params=pltpu.CompilerParams(vmem_limit_bytes=SMALL),
    )(volume)


def stage_kernel(atten_ref, proj_ref, counts_ref, near_ref, binned_ref, tiles_ref, sem):
    copy = pltpu.make_async_copy(proj_ref.at[: near_ref.shape[0]], near_ref, sem)
    copy.start()
    bins, mats = atten_ref.shape
    for b in range(bins):
        binned_ref[b] = counts_ref[:, b, :].astype(F32)
    for b in range(bins):
        for m in range(mats):
            tiles_ref[b * mats + m] = jnp.full(tiles_ref.shape[1:], atten_ref[b, m], F32)
    copy.wait()


def stage(atten, projector, counts, held):
    slices, bins, cols = counts.shape
    return pl.pallas_call(
        stage_kernel,
        out_shape=[
            jax.ShapeDtypeStruct((held, projector.shape[1]), BF16),
            jax.ShapeDtypeStruct((bins, slices, cols), F32),
            jax.ShapeDtypeStruct((atten.size, 8, 128), F32),
        ],
        in_specs=[SMEM, pl.BlockSpec(memory_space=pltpu.HBM), VMEM],
        out_specs=[VMEM] * 3,
        scratch_shapes=[pltpu.SemaphoreType.DMA(())],
        compiler_params=pltpu.CompilerParams(vmem_limit_bytes=LARGE),
        cost_estimate=pl.CostEstimate(flops=0, bytes_accessed=4 * projector.size, transcendentals=0),
    )(atten, projector, counts)


def wide_tile(tile, wide):
    return jnp.concatenate([tile] * (wide // tile.shape[1]), 1)


def project_kernel(mats, bins, slabs, tiles_ref, x_ref, near_ref, proj_ref, counts_ref, out_ref, resid_ref, rest_ref, sems):
    rows, pix = x_ref.shape
    cols, held = proj_ref.shape[0], near_ref.shape[0]
    wide = 256
    copies = [
        pltpu.make_async_copy(
            proj_ref.at[at : at + wide], rest_ref.at[at - held : at - held + wide], sems.at[i]
        )
        for i, at in enumerate(range(held, cols, wide))
    ]
    for copy in copies:
        copy.start()
    per_slab = rows // slabs
    depth = per_slab // mats
    atten = [[wide_tile(tiles_ref[b * mats + m], wide) for m in range(mats)] for b in range(bins)]
    for at in range(0, cols, wide):
        if at >= held:
            copies[(at - held) // wide].wait()
        block = near_ref[at : at + wide] if at < held else rest_ref[at - held : at - held + wide]
        line = lax.dot_general(
            x_ref[...], block, (((1,), (1,)), ((), ())), preferred_element_type=F32
        )
        blocks = []
        for slab in range(slabs):
            lines = [line[slab * per_slab + m * depth :][:depth] for m in range(mats)]
            parts = [None] * mats
            for b in range(bins):
                power = atten[b][0] * lines[0]
                for m in range(1, mats):
                    power = power + atten[b][m] * lines[m]
                seen = counts_ref[b, slab * depth : (slab + 1) * depth, at : at + wide]
                diff = seen - jnp.exp(-power)
                for m in range(mats):
                    term = atten[b][m] * diff
                    parts[m] = term if parts[m] is None else parts[m] + term
            blocks += parts
        resid_ref[:, at : at + wide] = jnp.concatenate(blocks, 0).astype(BF16)
    owners, _, _, span = out_ref.shape
    for owner in range(owners):
        own = slice(owner * span, (owner + 1) * span)
        back = jnp.dot(resid_ref[:, :held], near_ref[:, own], preferred_element_type=F32)
        back = back + jnp.dot(resid_ref[:, held:], rest_ref[:, own], preferred_element_type=F32)
        for slab in range(slabs):
            out_ref[owner, slab] = back[slab * per_slab : (slab + 1) * per_slab].astype(BF16)


def project(tiles, x_all, near, projector, counts, owners, slabs, mats):
    rows, pix = x_all.shape
    cols = counts.shape[2]
    return pl.pallas_call(
        functools.partial(project_kernel, mats, counts.shape[0], slabs),
        out_shape=jax.ShapeDtypeStruct((owners, slabs, rows // slabs, pix // owners), BF16),
        in_specs=[VMEM, VMEM, VMEM, pl.BlockSpec(memory_space=pltpu.HBM), VMEM],
        out_specs=VMEM,
        scratch_shapes=[
            pltpu.VMEM((rows, cols), BF16),
            pltpu.VMEM((cols - near.shape[0], pix), BF16),
            pltpu.SemaphoreType.DMA(((cols - near.shape[0]) // 256,)),
        ],
        compiler_params=pltpu.CompilerParams(vmem_limit_bytes=MEDIUM),
        cost_estimate=pl.CostEstimate(
            flops=4 * rows * cols * pix, bytes_accessed=2 * cols * pix, transcendentals=rows * cols
        ),
    )(tiles, x_all, near, projector, counts)


def next_pixel(field):
    column = lax.broadcasted_iota(jnp.int32, field.shape, 1) % PX
    return jnp.where(column == PX - 1, 0.0, pltpu.roll(field, field.shape[1] - 1, 1))


def next_row(field):
    return jnp.concatenate([field[:, PX:], jnp.zeros((field.shape[0], PX), F32)], 1)


def prev_pixel(flux):
    column = lax.broadcasted_iota(jnp.int32, flux.shape, 1) % PX
    return jnp.where(column == 0, 0.0, pltpu.roll(flux, 1, 1))


def prev_row(flux):
    return jnp.concatenate([jnp.zeros((flux.shape[0], PX), F32), flux[:, :-PX]], 1)


def smooth_kernel(where_ref, vol_ref, x_ref, edge_ref, out_ref):
    mats, depth, pix = vol_ref.shape
    slabs = x_ref.shape[0] // (mats * depth)
    slab, first = where_ref[0], where_ref[1]
    row = lax.broadcasted_iota(jnp.int32, (depth, pix), 0)
    vol, above, below = [], [], []
    for m in range(mats):
        vol.append(vol_ref[m])
        up = down = edge_ref[m : m + 1]
        for other in range(1, slabs):
            at = (other * mats + m) * depth
            up = jnp.where(slab == other - 1, x_ref[at : at + depth].astype(F32)[:1], up)
            at = ((other - 1) * mats + m) * depth
            down = jnp.where(slab == other, x_ref[at : at + depth].astype(F32)[-1:], down)
        above.append(jnp.where(row == depth - 1, up, pltpu.roll(vol[m], depth - 1, 0)))
        below.append(down)
    square = jnp.full((depth, pix), 0.25, F32)
    square_below = jnp.full((1, pix), 0.25, F32)
    diffs, steps = [], []
    for m in range(mats):
        dz, dy, dx = above[m] - vol[m], next_row(vol[m]) - vol[m], next_pixel(vol[m]) - vol[m]
        square = square + (dz * dz + dy * dy + dx * dx)
        diffs.append((dz, dy, dx))
        dz, dy, dx = vol[m][:1] - below[m], next_row(below[m]) - below[m], next_pixel(below[m]) - below[m]
        square_below = square_below + (dz * dz + dy * dy + dx * dx)
        steps.append(dz)
    scale = lax.rsqrt(square)
    scale_below = jnp.where(first == 1, 0.0, lax.rsqrt(square_below))
    for m in range(mats):
        qz, qy, qx = (d * scale for d in diffs[m])
        prev_z = jnp.where(row == 0, steps[m] * scale_below, pltpu.roll(qz, 1, 0))
        out_ref[m] = prev_z - qz + (prev_row(qy) - qy) + (prev_pixel(qx) - qx)


def smooth(where, volume, x_all, edge):
    return pl.pallas_call(
        smooth_kernel,
        out_shape=jax.ShapeDtypeStruct(volume.shape, F32),
        in_specs=[SMEM, VMEM, VMEM, VMEM],
        out_specs=VMEM,
        compiler_params=pltpu.CompilerParams(vmem_limit_bytes=SMALL),
        cost_estimate=pl.CostEstimate(
            flops=40 * volume.size, bytes_accessed=12 * volume.size, transcendentals=volume.size
        ),
    )(where, volume, x_all, edge)


def total_kernel(factor, part_ref, out_ref):
    total = jnp.sum(part_ref[...].astype(F32), axis=0) * factor
    total = total.astype(BF16)
    for copy in range(out_ref.shape[0]):
        out_ref[copy] = total


def total_copies(parts, factor, copies):
    return pl.pallas_call(
        functools.partial(total_kernel, factor),
        out_shape=jax.ShapeDtypeStruct((copies,) + parts.shape[1:], BF16),
        in_specs=[VMEM],
        out_specs=VMEM,
        compiler_params=pltpu.CompilerParams(vmem_limit_bytes=SMALL),
    )(parts)


def step_kernel(grad_ref, smooth_ref, newton_ref, vol_ref, out_ref):
    mats, depth, pix = vol_ref.shape
    span = grad_ref.shape[2]
    for owner in range(grad_ref.shape[0]):
        own = slice(owner * span, (owner + 1) * span)
        grad = grad_ref[owner].astype(F32)
        steps = [grad[k * depth : (k + 1) * depth] + 0.5 * smooth_ref[k, :, own] for k in range(mats)]
        for m in range(mats):
            moved = newton_ref[m, 0, :, own].astype(F32) * steps[0]
            for k in range(1, mats):
                moved = moved + newton_ref[m, k, :, own].astype(F32) * steps[k]
            out_ref[m, :, own] = vol_ref[m, :, own] - moved


def newton_step(grad, smoothed, newton, volume):
    return pl.pallas_call(
        step_kernel,
        out_shape=jax.ShapeDtypeStruct(volume.shape, F32),
        in_specs=[VMEM] * 4,
        out_specs=VMEM,
        compiler_params=pltpu.CompilerParams(vmem_limit_bytes=SMALL),
    )(grad, smoothed, newton, volume)


def body(volume, projector, counts, atten, newton):
    depth, mats, pix = volume.shape
    owners, copies, slabs, groups = (lax.axis_size(name) for name in ("x", "half", "mat", "row"))
    views_all = projector.shape[0] * owners * copies * slabs
    slab, group = lax.axis_index("mat"), lax.axis_index("row")
    rows = mats * depth
    vol = volume.transpose(1, 0, 2)
    x_all = lax.all_to_all(spread(vol, slabs), "mat", 0, 0, tiled=True)
    x_all = x_all.reshape(slabs * rows, pix)
    near, binned, tiles = stage(atten, projector[0], counts[0], projector.shape[1] // 2)
    parts = project(tiles, x_all, near, projector[0], binned, owners, slabs, mats)
    parts = lax.all_to_all(parts, "x", 0, 0, tiled=True)
    parts = total_copies(parts, 1.0, copies).reshape(copies * slabs, rows, pix // owners)
    parts = lax.all_to_all(parts, ("half", "mat"), 0, 0, tiled=True)
    mine = total_copies(parts, float(views_all) ** (-0.5), owners)
    grad = lax.all_to_all(mine, "x", 0, 0, tiled=True)
    edge = jnp.where(slab == 0, vol[:, 0], vol[:, -1])
    pairs = []
    for g in range(groups - 1):
        last, start = g * slabs + slabs - 1, (g + 1) * slabs
        pairs += [(last, start), (start, last)]
    edge = lax.ppermute(edge, ("row", "mat"), pairs)
    is_first = jnp.logical_and(slab == 0, group == 0).astype(jnp.int32)
    smoothed = smooth(jnp.stack([slab, is_first]).astype(jnp.int32), vol, x_all, edge)
    updated = newton_step(grad, smoothed, newton.transpose(1, 2, 0, 3), vol)
    return updated.transpose(1, 0, 2)


def solution(mesh):
    shape = mesh.devices.shape
    mesh = jax.sharding.Mesh(
        mesh.devices.reshape(shape[0] // 2, 2, *shape[1:]), ("x", "half", "row", "mat")
    )
    view = ("x", "half", "mat")
    in_specs = (
        P(("row", "mat"), None, None),
        P(view, None, None),
        P(view, "row", None, None),
        P(),
        P(("row", "mat"), None, None, None),
    )
    out_specs = P(("row", "mat"), None, None)
    return jax.shard_map(body, mesh=mesh, in_specs=in_specs, out_specs=out_specs, check_vma=False)
```

```python
import functools

import jax
import jax.numpy as jnp
from jax import lax
from jax.experimental import pallas as pl
from jax.experimental.pallas import tpu as pltpu
from jax.sharding import PartitionSpec as P

PX = 1024
BF16 = jnp.bfloat16
F32 = jnp.float32
VMEM = pl.BlockSpec(memory_space=pltpu.VMEM)
SMEM = pl.BlockSpec(memory_space=pltpu.SMEM)
SMALL = 8 * 1024 * 1024
MEDIUM = 49 * 1024 * 1024
LARGE = 50 * 1024 * 1024


def spread_kernel(vol_ref, out_ref):
    mats, depth, _ = vol_ref.shape
    rounded = jnp.concatenate([vol_ref[m] for m in range(mats)], 0).astype(BF16)
    for copy in range(out_ref.shape[0]):
        out_ref[copy] = rounded


def spread(volume, copies):
    mats, depth, pix = volume.shape
    return pl.pallas_call(
        spread_kernel,
        out_shape=jax.ShapeDtypeStruct((copies, mats * depth, pix), BF16),
        in_specs=[VMEM],
        out_specs=VMEM,
        compiler_params=pltpu.CompilerParams(vmem_limit_bytes=SMALL),
    )(volume)


def stage_kernel(atten_ref, proj_ref, counts_ref, near_ref, binned_ref, tiles_ref, sem):
    copy = pltpu.make_async_copy(proj_ref.at[: near_ref.shape[0]], near_ref, sem)
    copy.start()
    bins, mats = atten_ref.shape
    for b in range(bins):
        binned_ref[b] = counts_ref[:, b, :].astype(F32)
    for b in range(bins):
        for m in range(mats):
            tiles_ref[b * mats + m] = jnp.full(tiles_ref.shape[1:], atten_ref[b, m], F32)
    copy.wait()


def stage(atten, projector, counts, held):
    slices, bins, cols = counts.shape
    return pl.pallas_call(
        stage_kernel,
        out_shape=[
            jax.ShapeDtypeStruct((held, projector.shape[1]), BF16),
            jax.ShapeDtypeStruct((bins, slices, cols), F32),
            jax.ShapeDtypeStruct((atten.size, 8, 128), F32),
        ],
        in_specs=[SMEM, pl.BlockSpec(memory_space=pltpu.HBM), VMEM],
        out_specs=[VMEM] * 3,
        scratch_shapes=[pltpu.SemaphoreType.DMA(())],
        compiler_params=pltpu.CompilerParams(vmem_limit_bytes=LARGE),
        cost_estimate=pl.CostEstimate(flops=0, bytes_accessed=4 * projector.size, transcendentals=0),
    )(atten, projector, counts)


def wide_tile(tile, wide):
    return jnp.concatenate([tile] * (wide // tile.shape[1]), 1)


def project_kernel(mats, bins, slabs, tiles_ref, x_ref, near_ref, proj_ref, counts_ref, out_ref, resid_ref, rest_ref, sems):
    rows, pix = x_ref.shape
    cols, held = proj_ref.shape[0], near_ref.shape[0]
    wide = 256
    copies = [
        pltpu.make_async_copy(
            proj_ref.at[at : at + wide], rest_ref.at[at - held : at - held + wide], sems.at[i]
        )
        for i, at in enumerate(range(held, cols, wide))
    ]
    for copy in copies:
        copy.start()
    per_slab = rows // slabs
    depth = per_slab // mats
    atten = [[wide_tile(tiles_ref[b * mats + m], wide) for m in range(mats)] for b in range(bins)]
    for at in range(0, cols, wide):
        if at >= held:
            copies[(at - held) // wide].wait()
        block = near_ref[at : at + wide] if at < held else rest_ref[at - held : at - held + wide]
        line = lax.dot_general(
            x_ref[...], block, (((1,), (1,)), ((), ())), preferred_element_type=F32
        )
        blocks = []
        for slab in range(slabs):
            lines = [line[slab * per_slab + m * depth :][:depth] for m in range(mats)]
            parts = [None] * mats
            for b in range(bins):
                power = atten[b][0] * lines[0]
                for m in range(1, mats):
                    power = power + atten[b][m] * lines[m]
                seen = counts_ref[b, slab * depth : (slab + 1) * depth, at : at + wide]
                diff = seen - jnp.exp(-power)
                for m in range(mats):
                    term = atten[b][m] * diff
                    parts[m] = term if parts[m] is None else parts[m] + term
            blocks += parts
        resid_ref[:, at : at + wide] = jnp.concatenate(blocks, 0).astype(BF16)
    owners, _, _, span = out_ref.shape
    for owner in range(owners):
        own = slice(owner * span, (owner + 1) * span)
        back = jnp.dot(resid_ref[:, :held], near_ref[:, own], preferred_element_type=F32)
        back = back + jnp.dot(resid_ref[:, held:], rest_ref[:, own], preferred_element_type=F32)
        for slab in range(slabs):
            out_ref[owner, slab] = back[slab * per_slab : (slab + 1) * per_slab].astype(BF16)


def project(tiles, x_all, near, projector, counts, owners, slabs, mats):
    rows, pix = x_all.shape
    cols = counts.shape[2]
    return pl.pallas_call(
        functools.partial(project_kernel, mats, counts.shape[0], slabs),
        out_shape=jax.ShapeDtypeStruct((owners, slabs, rows // slabs, pix // owners), BF16),
        in_specs=[VMEM, VMEM, VMEM, pl.BlockSpec(memory_space=pltpu.HBM), VMEM],
        out_specs=VMEM,
        scratch_shapes=[
            pltpu.VMEM((rows, cols), BF16),
            pltpu.VMEM((cols - near.shape[0], pix), BF16),
            pltpu.SemaphoreType.DMA(((cols - near.shape[0]) // 256,)),
        ],
        compiler_params=pltpu.CompilerParams(vmem_limit_bytes=MEDIUM),
        cost_estimate=pl.CostEstimate(
            flops=4 * rows * cols * pix, bytes_accessed=2 * cols * pix, transcendentals=rows * cols
        ),
    )(tiles, x_all, near, projector, counts)


def next_pixel(field):
    column = lax.broadcasted_iota(jnp.int32, field.shape, 1) % PX
    return jnp.where(column == PX - 1, 0.0, pltpu.roll(field, field.shape[1] - 1, 1))


def next_row(field):
    return jnp.concatenate([field[:, PX:], jnp.zeros((field.shape[0], PX), F32)], 1)


def prev_pixel(flux):
    column = lax.broadcasted_iota(jnp.int32, flux.shape, 1) % PX
    return jnp.where(column == 0, 0.0, pltpu.roll(flux, 1, 1))


def prev_row(flux):
    return jnp.concatenate([jnp.zeros((flux.shape[0], PX), F32), flux[:, :-PX]], 1)


def smooth_kernel(where_ref, vol_ref, x_ref, edge_ref, out_ref):
    mats, depth, pix = vol_ref.shape
    slabs = x_ref.shape[0] // (mats * depth)
    slab, first = where_ref[0], where_ref[1]
    row = lax.broadcasted_iota(jnp.int32, (depth, pix), 0)
    vol, above, below = [], [], []
    for m in range(mats):
        vol.append(vol_ref[m])
        up = down = edge_ref[m : m + 1]
        for other in range(1, slabs):
            at = (other * mats + m) * depth
            up = jnp.where(slab == other - 1, x_ref[at : at + depth].astype(F32)[:1], up)
            at = ((other - 1) * mats + m) * depth
            down = jnp.where(slab == other, x_ref[at : at + depth].astype(F32)[-1:], down)
        above.append(jnp.where(row == depth - 1, up, pltpu.roll(vol[m], depth - 1, 0)))
        below.append(down)
    square = jnp.full((depth, pix), 0.25, F32)
    square_below = jnp.full((1, pix), 0.25, F32)
    diffs, steps = [], []
    for m in range(mats):
        dz, dy, dx = above[m] - vol[m], next_row(vol[m]) - vol[m], next_pixel(vol[m]) - vol[m]
        square = square + (dz * dz + dy * dy + dx * dx)
        diffs.append((dz, dy, dx))
        dz, dy, dx = vol[m][:1] - below[m], next_row(below[m]) - below[m], next_pixel(below[m]) - below[m]
        square_below = square_below + (dz * dz + dy * dy + dx * dx)
        steps.append(dz)
    scale = lax.rsqrt(square)
    scale_below = jnp.where(first == 1, 0.0, lax.rsqrt(square_below))
    for m in range(mats):
        qz, qy, qx = (d * scale for d in diffs[m])
        prev_z = jnp.where(row == 0, steps[m] * scale_below, pltpu.roll(qz, 1, 0))
        out_ref[m] = prev_z - qz + (prev_row(qy) - qy) + (prev_pixel(qx) - qx)


def smooth(where, volume, x_all, edge):
    return pl.pallas_call(
        smooth_kernel,
        out_shape=jax.ShapeDtypeStruct(volume.shape, F32),
        in_specs=[SMEM, VMEM, VMEM, VMEM],
        out_specs=VMEM,
        compiler_params=pltpu.CompilerParams(vmem_limit_bytes=SMALL),
        cost_estimate=pl.CostEstimate(
            flops=40 * volume.size, bytes_accessed=12 * volume.size, transcendentals=volume.size
        ),
    )(where, volume, x_all, edge)


def total_kernel(factor, part_ref, out_ref):
    total = jnp.sum(part_ref[...].astype(F32), axis=0) * factor
    total = total.astype(BF16)
    for copy in range(out_ref.shape[0]):
        out_ref[copy] = total


def total_copies(parts, factor, copies):
    return pl.pallas_call(
        functools.partial(total_kernel, factor),
        out_shape=jax.ShapeDtypeStruct((copies,) + parts.shape[1:], BF16),
        in_specs=[VMEM],
        out_specs=VMEM,
        compiler_params=pltpu.CompilerParams(vmem_limit_bytes=SMALL),
    )(parts)


def step_kernel(grad_ref, smooth_ref, newton_ref, vol_ref, out_ref):
    mats, depth, pix = vol_ref.shape
    owners, copies, _, span = grad_ref.shape
    for owner in range(owners):
        own = slice(owner * span, (owner + 1) * span)
        grad = grad_ref[owner, 0].astype(F32)
        for copy in range(1, copies):
            grad = grad + grad_ref[owner, copy].astype(F32)
        steps = [grad[k * depth : (k + 1) * depth] + 0.5 * smooth_ref[k, :, own] for k in range(mats)]
        for m in range(mats):
            moved = newton_ref[m, 0, :, own].astype(F32) * steps[0]
            for k in range(1, mats):
                moved = moved + newton_ref[m, k, :, own].astype(F32) * steps[k]
            out_ref[m, :, own] = vol_ref[m, :, own] - moved


def newton_step(grad, smoothed, newton, volume):
    return pl.pallas_call(
        step_kernel,
        out_shape=jax.ShapeDtypeStruct(volume.shape, F32),
        in_specs=[VMEM] * 4,
        out_specs=VMEM,
        compiler_params=pltpu.CompilerParams(vmem_limit_bytes=SMALL),
    )(grad, smoothed, newton, volume)


def body(volume, projector, counts, atten, newton):
    depth, mats, pix = volume.shape
    owners, copies, slabs, groups = (lax.axis_size(name) for name in ("x", "half", "mat", "row"))
    views_all = projector.shape[0] * owners * copies * slabs
    slab, group = lax.axis_index("mat"), lax.axis_index("row")
    rows = mats * depth
    vol = volume.transpose(1, 0, 2)
    x_all = lax.all_to_all(spread(vol, slabs), "mat", 0, 0, tiled=True)
    x_all = x_all.reshape(slabs * rows, pix)
    edge = jnp.where(slab == 0, vol[:, 0], vol[:, -1])
    pairs = []
    for g in range(groups - 1):
        last, start = g * slabs + slabs - 1, (g + 1) * slabs
        pairs += [(last, start), (start, last)]
    edge = lax.ppermute(edge, ("row", "mat"), pairs)
    near, binned, tiles = stage(atten, projector[0], counts[0], projector.shape[1] // 2)
    x_all, edge, near = lax.optimization_barrier((x_all, edge, near))
    parts = project(tiles, x_all, near, projector[0], binned, owners, slabs, mats)
    parts = parts.reshape(owners * slabs, rows, pix // owners)
    parts = lax.all_to_all(parts, ("x", "mat"), 0, 0, tiled=True)
    mine = total_copies(parts, float(views_all) ** (-0.5), owners * copies)
    grad = lax.all_to_all(mine, ("x", "half"), 0, 0, tiled=True)
    grad = grad.reshape(owners, copies, rows, pix // owners)
    is_first = jnp.logical_and(slab == 0, group == 0).astype(jnp.int32)
    smoothed = smooth(jnp.stack([slab, is_first]).astype(jnp.int32), vol, x_all, edge)
    updated = newton_step(grad, smoothed, newton.transpose(1, 2, 0, 3), vol)
    return updated.transpose(1, 0, 2)


def solution(mesh):
    shape = mesh.devices.shape
    mesh = jax.sharding.Mesh(
        mesh.devices.reshape(shape[0] // 2, 2, *shape[1:]), ("x", "half", "row", "mat")
    )
    view = ("x", "half", "mat")
    in_specs = (
        P(("row", "mat"), None, None),
        P(view, None, None),
        P(view, "row", None, None),
        P(),
        P(("row", "mat"), None, None, None),
    )
    out_specs = P(("row", "mat"), None, None)
    return jax.shard_map(body, mesh=mesh, in_specs=in_specs, out_specs=out_specs, check_vma=False)
```

```python
import functools

import jax
import jax.numpy as jnp
from jax import lax
from jax.experimental import pallas as pl
from jax.experimental.pallas import tpu as pltpu
from jax.sharding import PartitionSpec as P

PX = 1024
BF16 = jnp.bfloat16
F32 = jnp.float32
VMEM = pl.BlockSpec(memory_space=pltpu.VMEM)
SMEM = pl.BlockSpec(memory_space=pltpu.SMEM)
HBM = pl.BlockSpec(memory_space=pltpu.HBM)
SMALL = 8 * 1024 * 1024
MEDIUM = 49 * 1024 * 1024
LARGE = 50 * 1024 * 1024
HUGE = 58 * 1024 * 1024


def spread_kernel(vol_ref, out_ref, near_ref, rounded_ref, sems):
    copy_in = pltpu.make_async_copy(vol_ref, near_ref, sems.at[0])
    copy_in.start()
    copy_in.wait()
    mats = near_ref.shape[0]
    rounded_ref[...] = jnp.concatenate([near_ref[m] for m in range(mats)], 0).astype(BF16)
    copies = [
        pltpu.make_async_copy(rounded_ref, out_ref.at[copy], sems.at[copy + 1])
        for copy in range(out_ref.shape[0])
    ]
    for copy in copies:
        copy.start()
    for copy in copies:
        copy.wait()


def spread(volume, copies):
    mats, depth, pix = volume.shape
    return pl.pallas_call(
        spread_kernel,
        out_shape=jax.ShapeDtypeStruct((copies, mats * depth, pix), BF16),
        in_specs=[HBM],
        out_specs=HBM,
        scratch_shapes=[
            pltpu.VMEM(volume.shape, F32),
            pltpu.VMEM((mats * depth, pix), BF16),
            pltpu.SemaphoreType.DMA((copies + 1,)),
        ],
        compiler_params=pltpu.CompilerParams(vmem_limit_bytes=HUGE),
    )(volume)


def stage_kernel(
    atten_ref, proj_ref, counts_ref, near_ref, binned_ref, tiles_ref, atten_near, counts_near, sems
):
    copy_atten = pltpu.make_async_copy(atten_ref, atten_near, sems.at[0])
    copy_counts = pltpu.make_async_copy(counts_ref, counts_near, sems.at[1])
    copy_proj = pltpu.make_async_copy(proj_ref.at[: near_ref.shape[0]], near_ref, sems.at[2])
    copy_atten.start()
    copy_counts.start()
    copy_proj.start()
    bins, mats = atten_ref.shape
    copy_atten.wait()
    for b in range(bins):
        for m in range(mats):
            tiles_ref[b * mats + m] = jnp.full(tiles_ref.shape[1:], atten_near[b, m], F32)
    copy_counts.wait()
    for b in range(bins):
        binned_ref[b] = counts_near[:, b, :].astype(F32)
    copy_proj.wait()


def stage(atten, projector, counts, held):
    slices, bins, cols = counts.shape
    return pl.pallas_call(
        stage_kernel,
        out_shape=[
            jax.ShapeDtypeStruct((held, projector.shape[1]), BF16),
            jax.ShapeDtypeStruct((bins, slices, cols), F32),
            jax.ShapeDtypeStruct((atten.size, 8, 128), F32),
        ],
        in_specs=[HBM, HBM, HBM],
        out_specs=[VMEM] * 3,
        scratch_shapes=[
            pltpu.SMEM(atten.shape, F32),
            pltpu.VMEM(counts.shape, BF16),
            pltpu.SemaphoreType.DMA((3,)),
        ],
        compiler_params=pltpu.CompilerParams(vmem_limit_bytes=LARGE),
        cost_estimate=pl.CostEstimate(flops=0, bytes_accessed=4 * projector.size, transcendentals=0),
    )(atten, projector, counts)


def wide_tile(tile, wide):
    return jnp.concatenate([tile] * (wide // tile.shape[1]), 1)


def project_kernel(mats, bins, slabs, tiles_ref, x_ref, near_ref, proj_ref, counts_ref, out_ref, resid_ref, rest_ref, sems):
    rows, pix = x_ref.shape
    cols, held = proj_ref.shape[0], near_ref.shape[0]
    wide = 256
    copies = [
        pltpu.make_async_copy(
            proj_ref.at[at : at + wide], rest_ref.at[at - held : at - held + wide], sems.at[i]
        )
        for i, at in enumerate(range(held, cols, wide))
    ]
    for copy in copies:
        copy.start()
    per_slab = rows // slabs
    depth = per_slab // mats
    atten = [[wide_tile(tiles_ref[b * mats + m], wide) for m in range(mats)] for b in range(bins)]
    for at in range(0, cols, wide):
        if at >= held:
            copies[(at - held) // wide].wait()
        block = near_ref[at : at + wide] if at < held else rest_ref[at - held : at - held + wide]
        line = lax.dot_general(
            x_ref[...], block, (((1,), (1,)), ((), ())), preferred_element_type=F32
        )
        blocks = []
        for slab in range(slabs):
            lines = [line[slab * per_slab + m * depth :][:depth] for m in range(mats)]
            parts = [None] * mats
            for b in range(bins):
                power = atten[b][0] * lines[0]
                for m in range(1, mats):
                    power = power + atten[b][m] * lines[m]
                seen = counts_ref[b, slab * depth : (slab + 1) * depth, at : at + wide]
                diff = seen - jnp.exp(-power)
                for m in range(mats):
                    term = atten[b][m] * diff
                    parts[m] = term if parts[m] is None else parts[m] + term
            blocks += parts
        resid_ref[:, at : at + wide] = jnp.concatenate(blocks, 0).astype(BF16)
    owners, _, _, span = out_ref.shape
    for owner in range(owners):
        own = slice(owner * span, (owner + 1) * span)
        back = jnp.dot(resid_ref[:, :held], near_ref[:, own], preferred_element_type=F32)
        back = back + jnp.dot(resid_ref[:, held:], rest_ref[:, own], preferred_element_type=F32)
        for slab in range(slabs):
            out_ref[owner, slab] = back[slab * per_slab : (slab + 1) * per_slab].astype(BF16)


def project(tiles, x_all, near, projector, counts, owners, slabs, mats):
    rows, pix = x_all.shape
    cols = counts.shape[2]
    return pl.pallas_call(
        functools.partial(project_kernel, mats, counts.shape[0], slabs),
        out_shape=jax.ShapeDtypeStruct((owners, slabs, rows // slabs, pix // owners), BF16),
        in_specs=[VMEM, VMEM, VMEM, HBM, VMEM],
        out_specs=VMEM,
        scratch_shapes=[
            pltpu.VMEM((rows, cols), BF16),
            pltpu.VMEM((cols - near.shape[0], pix), BF16),
            pltpu.SemaphoreType.DMA(((cols - near.shape[0]) // 256,)),
        ],
        compiler_params=pltpu.CompilerParams(vmem_limit_bytes=MEDIUM),
        cost_estimate=pl.CostEstimate(
            flops=4 * rows * cols * pix, bytes_accessed=2 * cols * pix, transcendentals=rows * cols
        ),
    )(tiles, x_all, near, projector, counts)


def next_pixel(field):
    column = lax.broadcasted_iota(jnp.int32, field.shape, 1) % PX
    return jnp.where(column == PX - 1, 0.0, pltpu.roll(field, field.shape[1] - 1, 1))


def next_row(field):
    return jnp.concatenate([field[:, PX:], jnp.zeros((field.shape[0], PX), F32)], 1)


def prev_pixel(flux):
    column = lax.broadcasted_iota(jnp.int32, flux.shape, 1) % PX
    return jnp.where(column == 0, 0.0, pltpu.roll(flux, 1, 1))


def prev_row(flux):
    return jnp.concatenate([jnp.zeros((flux.shape[0], PX), F32), flux[:, :-PX]], 1)


def smooth_kernel(where_ref, vol_ref, x_ref, edge_ref, out_ref):
    mats, depth, pix = vol_ref.shape
    slabs = x_ref.shape[0] // (mats * depth)
    slab, first = where_ref[0], where_ref[1]
    row = lax.broadcasted_iota(jnp.int32, (depth, pix), 0)
    vol, above, below = [], [], []
    for m in range(mats):
        vol.append(vol_ref[m])
        up = down = edge_ref[m : m + 1]
        for other in range(1, slabs):
            at = (other * mats + m) * depth
            up = jnp.where(slab == other - 1, x_ref[at : at + depth].astype(F32)[:1], up)
            at = ((other - 1) * mats + m) * depth
            down = jnp.where(slab == other, x_ref[at : at + depth].astype(F32)[-1:], down)
        above.append(jnp.where(row == depth - 1, up, pltpu.roll(vol[m], depth - 1, 0)))
        below.append(down)
    square = jnp.full((depth, pix), 0.25, F32)
    square_below = jnp.full((1, pix), 0.25, F32)
    diffs, steps = [], []
    for m in range(mats):
        dz, dy, dx = above[m] - vol[m], next_row(vol[m]) - vol[m], next_pixel(vol[m]) - vol[m]
        square = square + (dz * dz + dy * dy + dx * dx)
        diffs.append((dz, dy, dx))
        dz, dy, dx = vol[m][:1] - below[m], next_row(below[m]) - below[m], next_pixel(below[m]) - below[m]
        square_below = square_below + (dz * dz + dy * dy + dx * dx)
        steps.append(dz)
    scale = lax.rsqrt(square)
    scale_below = jnp.where(first == 1, 0.0, lax.rsqrt(square_below))
    for m in range(mats):
        qz, qy, qx = (d * scale for d in diffs[m])
        prev_z = jnp.where(row == 0, steps[m] * scale_below, pltpu.roll(qz, 1, 0))
        out_ref[m] = prev_z - qz + (prev_row(qy) - qy) + (prev_pixel(qx) - qx)


def smooth(where, volume, x_all, edge):
    return pl.pallas_call(
        smooth_kernel,
        out_shape=jax.ShapeDtypeStruct(volume.shape, F32),
        in_specs=[SMEM, VMEM, VMEM, VMEM],
        out_specs=VMEM,
        compiler_params=pltpu.CompilerParams(vmem_limit_bytes=SMALL),
        cost_estimate=pl.CostEstimate(
            flops=40 * volume.size, bytes_accessed=12 * volume.size, transcendentals=volume.size
        ),
    )(where, volume, x_all, edge)


def total_kernel(factor, part_ref, out_ref):
    total = jnp.sum(part_ref[...].astype(F32), axis=0) * factor
    total = total.astype(BF16)
    for copy in range(out_ref.shape[0]):
        out_ref[copy] = total


def total_copies(parts, factor, copies):
    return pl.pallas_call(
        functools.partial(total_kernel, factor),
        out_shape=jax.ShapeDtypeStruct((copies,) + parts.shape[1:], BF16),
        in_specs=[VMEM],
        out_specs=VMEM,
        compiler_params=pltpu.CompilerParams(vmem_limit_bytes=SMALL),
    )(parts)


def step_kernel(grad_ref, smooth_ref, newton_ref, vol_ref, out_ref):
    mats, depth, pix = vol_ref.shape
    owners, copies, _, span = grad_ref.shape
    for owner in range(owners):
        own = slice(owner * span, (owner + 1) * span)
        grad = grad_ref[owner, 0].astype(F32)
        for copy in range(1, copies):
            grad = grad + grad_ref[owner, copy].astype(F32)
        steps = [grad[k * depth : (k + 1) * depth] + 0.5 * smooth_ref[k, :, own] for k in range(mats)]
        for m in range(mats):
            moved = newton_ref[m, 0, :, own].astype(F32) * steps[0]
            for k in range(1, mats):
                moved = moved + newton_ref[m, k, :, own].astype(F32) * steps[k]
            out_ref[m, :, own] = vol_ref[m, :, own] - moved


def newton_step(grad, smoothed, newton, volume):
    return pl.pallas_call(
        step_kernel,
        out_shape=jax.ShapeDtypeStruct(volume.shape, F32),
        in_specs=[VMEM] * 4,
        out_specs=VMEM,
        compiler_params=pltpu.CompilerParams(vmem_limit_bytes=SMALL),
    )(grad, smoothed, newton, volume)


def body(volume, projector, counts, atten, newton):
    depth, mats, pix = volume.shape
    owners, copies, slabs, groups = (lax.axis_size(name) for name in ("x", "half", "mat", "row"))
    views_all = projector.shape[0] * owners * copies * slabs
    slab, group = lax.axis_index("mat"), lax.axis_index("row")
    rows = mats * depth
    vol = volume.transpose(1, 0, 2)
    x_all = lax.all_to_all(spread(vol, slabs), "mat", 0, 0, tiled=True)
    x_all = x_all.reshape(slabs * rows, pix)
    near, binned, tiles = stage(atten, projector[0], counts[0], projector.shape[1] // 2)
    parts = project(tiles, x_all, near, projector[0], binned, owners, slabs, mats)
    parts = parts.reshape(owners * slabs, rows, pix // owners)
    edge = jnp.where(slab == 0, vol[:, 0], vol[:, -1])
    pairs = []
    for g in range(groups - 1):
        last, start = g * slabs + slabs - 1, (g + 1) * slabs
        pairs += [(last, start), (start, last)]
    parts, edge = lax.optimization_barrier((parts, edge))
    parts = lax.all_to_all(parts, ("x", "mat"), 0, 0, tiled=True)
    edge = lax.ppermute(edge, ("row", "mat"), pairs)
    parts, edge = lax.optimization_barrier((parts, edge))
    mine = total_copies(parts, float(views_all) ** (-0.5), owners * copies)
    grad = lax.all_to_all(mine, ("x", "half"), 0, 0, tiled=True)
    grad = grad.reshape(owners, copies, rows, pix // owners)
    is_first = jnp.logical_and(slab == 0, group == 0).astype(jnp.int32)
    smoothed = smooth(jnp.stack([slab, is_first]).astype(jnp.int32), vol, x_all, edge)
    updated = newton_step(grad, smoothed, newton.transpose(1, 2, 0, 3), vol)
    return updated.transpose(1, 0, 2)


def solution(mesh):
    shape = mesh.devices.shape
    mesh = jax.sharding.Mesh(
        mesh.devices.reshape(shape[0] // 2, 2, *shape[1:]), ("x", "half", "row", "mat")
    )
    view = ("x", "half", "mat")
    in_specs = (
        P(("row", "mat"), None, None),
        P(view, None, None),
        P(view, "row", None, None),
        P(),
        P(("row", "mat"), None, None, None),
    )
    out_specs = P(("row", "mat"), None, None)
    return jax.shard_map(body, mesh=mesh, in_specs=in_specs, out_specs=out_specs, check_vma=False)
```

```python
import functools

import jax
import jax.numpy as jnp
from jax import lax
from jax.experimental import pallas as pl
from jax.experimental.pallas import tpu as pltpu
from jax.sharding import PartitionSpec as P

PX = 1024
BF16 = jnp.bfloat16
F32 = jnp.float32
VMEM = pl.BlockSpec(memory_space=pltpu.VMEM)
SMEM = pl.BlockSpec(memory_space=pltpu.SMEM)
HBM = pl.BlockSpec(memory_space=pltpu.HBM)
SMALL = 8 * 1024 * 1024
MEDIUM = 49 * 1024 * 1024
LARGE = 50 * 1024 * 1024
HUGE = 58 * 1024 * 1024


def spread_kernel(vol_ref, out_ref, near_ref, rounded_ref, sems):
    copy_in = pltpu.make_async_copy(vol_ref, near_ref, sems.at[0])
    copy_in.start()
    copy_in.wait()
    mats = near_ref.shape[0]
    rounded_ref[...] = jnp.concatenate([near_ref[m] for m in range(mats)], 0).astype(BF16)
    copies = [
        pltpu.make_async_copy(rounded_ref, out_ref.at[copy], sems.at[copy + 1])
        for copy in range(out_ref.shape[0])
    ]
    for copy in copies:
        copy.start()
    for copy in copies:
        copy.wait()


def spread(volume, copies):
    mats, depth, pix = volume.shape
    return pl.pallas_call(
        spread_kernel,
        out_shape=jax.ShapeDtypeStruct((copies, mats * depth, pix), BF16),
        in_specs=[HBM],
        out_specs=HBM,
        scratch_shapes=[
            pltpu.VMEM(volume.shape, F32),
            pltpu.VMEM((mats * depth, pix), BF16),
            pltpu.SemaphoreType.DMA((copies + 1,)),
        ],
        compiler_params=pltpu.CompilerParams(vmem_limit_bytes=HUGE),
    )(volume)


def stage_kernel(
    atten_ref, proj_ref, counts_ref, near_ref, binned_ref, tiles_ref, atten_near, counts_near, sems
):
    copy_atten = pltpu.make_async_copy(atten_ref, atten_near, sems.at[0])
    copy_counts = pltpu.make_async_copy(counts_ref, counts_near, sems.at[1])
    copy_proj = pltpu.make_async_copy(proj_ref.at[: near_ref.shape[0]], near_ref, sems.at[2])
    copy_atten.start()
    copy_counts.start()
    copy_proj.start()
    bins, mats = atten_ref.shape
    copy_atten.wait()
    for b in range(bins):
        for m in range(mats):
            tiles_ref[b * mats + m] = jnp.full(tiles_ref.shape[1:], atten_near[b, m], F32)
    copy_counts.wait()
    for b in range(bins):
        binned_ref[b] = counts_near[:, b, :].astype(F32)
    copy_proj.wait()


def stage(atten, projector, counts, held):
    slices, bins, cols = counts.shape
    return pl.pallas_call(
        stage_kernel,
        out_shape=[
            jax.ShapeDtypeStruct((held, projector.shape[1]), BF16),
            jax.ShapeDtypeStruct((bins, slices, cols), F32),
            jax.ShapeDtypeStruct((atten.size, 8, 128), F32),
        ],
        in_specs=[HBM, HBM, HBM],
        out_specs=[VMEM] * 3,
        scratch_shapes=[
            pltpu.SMEM(atten.shape, F32),
            pltpu.VMEM(counts.shape, BF16),
            pltpu.SemaphoreType.DMA((3,)),
        ],
        compiler_params=pltpu.CompilerParams(vmem_limit_bytes=LARGE),
        cost_estimate=pl.CostEstimate(flops=0, bytes_accessed=4 * projector.size, transcendentals=0),
    )(atten, projector, counts)


def wide_tile(tile, wide):
    return jnp.concatenate([tile] * (wide // tile.shape[1]), 1)


def project_kernel(mats, bins, slabs, tiles_ref, x_ref, near_ref, proj_ref, counts_ref, out_ref, resid_ref, rest_ref, block_ref, sems, out_sems):
    rows, pix = x_ref.shape
    cols, held = proj_ref.shape[0], near_ref.shape[0]
    wide = 256
    copies = [
        pltpu.make_async_copy(
            proj_ref.at[at : at + wide], rest_ref.at[at - held : at - held + wide], sems.at[i]
        )
        for i, at in enumerate(range(held, cols, wide))
    ]
    for copy in copies:
        copy.start()
    per_slab = rows // slabs
    depth = per_slab // mats
    atten = [[wide_tile(tiles_ref[b * mats + m], wide) for m in range(mats)] for b in range(bins)]
    for at in range(0, cols, wide):
        if at >= held:
            copies[(at - held) // wide].wait()
        block = near_ref[at : at + wide] if at < held else rest_ref[at - held : at - held + wide]
        line = lax.dot_general(
            x_ref[...], block, (((1,), (1,)), ((), ())), preferred_element_type=F32
        )
        blocks = []
        for slab in range(slabs):
            lines = [line[slab * per_slab + m * depth :][:depth] for m in range(mats)]
            parts = [None] * mats
            for b in range(bins):
                power = atten[b][0] * lines[0]
                for m in range(1, mats):
                    power = power + atten[b][m] * lines[m]
                seen = counts_ref[b, slab * depth : (slab + 1) * depth, at : at + wide]
                diff = seen - jnp.exp(-power)
                for m in range(mats):
                    term = atten[b][m] * diff
                    parts[m] = term if parts[m] is None else parts[m] + term
            blocks += parts
        resid_ref[:, at : at + wide] = jnp.concatenate(blocks, 0).astype(BF16)
    owners, sides, pairs, _, span = out_ref.shape
    copies_out = []
    for owner in range(owners):
        own = slice(owner * span, (owner + 1) * span)
        back = jnp.dot(resid_ref[:, :held], near_ref[:, own], preferred_element_type=F32)
        back = back + jnp.dot(resid_ref[:, held:], rest_ref[:, own], preferred_element_type=F32)
        for slab in range(slabs):
            block_ref[owner, slab % sides, slab // sides] = back[
                slab * per_slab : (slab + 1) * per_slab
            ].astype(BF16)
        copies_out.append(
            pltpu.make_async_copy(block_ref.at[owner], out_ref.at[owner], out_sems.at[owner])
        )
        copies_out[-1].start()
    for copy in copies_out:
        copy.wait()


def project(tiles, x_all, near, projector, counts, owners, sides, slabs, mats):
    rows, pix = x_all.shape
    cols = counts.shape[2]
    out = (owners, sides, slabs // sides, rows // slabs, pix // owners)
    return pl.pallas_call(
        functools.partial(project_kernel, mats, counts.shape[0], slabs),
        out_shape=jax.ShapeDtypeStruct(out, BF16),
        in_specs=[VMEM, VMEM, VMEM, HBM, VMEM],
        out_specs=HBM,
        scratch_shapes=[
            pltpu.VMEM((rows, cols), BF16),
            pltpu.VMEM((cols - near.shape[0], pix), BF16),
            pltpu.VMEM(out, BF16),
            pltpu.SemaphoreType.DMA(((cols - near.shape[0]) // 256,)),
            pltpu.SemaphoreType.DMA((owners,)),
        ],
        compiler_params=pltpu.CompilerParams(vmem_limit_bytes=MEDIUM),
        cost_estimate=pl.CostEstimate(
            flops=4 * rows * cols * pix, bytes_accessed=2 * cols * pix, transcendentals=rows * cols
        ),
    )(tiles, x_all, near, projector, counts)


def next_pixel(field):
    column = lax.broadcasted_iota(jnp.int32, field.shape, 1) % PX
    return jnp.where(column == PX - 1, 0.0, pltpu.roll(field, field.shape[1] - 1, 1))


def next_row(field):
    return jnp.concatenate([field[:, PX:], jnp.zeros((field.shape[0], PX), F32)], 1)


def prev_pixel(flux):
    column = lax.broadcasted_iota(jnp.int32, flux.shape, 1) % PX
    return jnp.where(column == 0, 0.0, pltpu.roll(flux, 1, 1))


def prev_row(flux):
    return jnp.concatenate([jnp.zeros((flux.shape[0], PX), F32), flux[:, :-PX]], 1)


def smooth_kernel(where_ref, vol_ref, x_ref, edge_ref, out_ref):
    mats, depth, pix = vol_ref.shape
    slabs = x_ref.shape[0] // (mats * depth)
    slab, first = where_ref[0], where_ref[1]
    row = lax.broadcasted_iota(jnp.int32, (depth, pix), 0)
    vol, above, below = [], [], []
    for m in range(mats):
        vol.append(vol_ref[m])
        up = down = edge_ref[m : m + 1]
        for other in range(1, slabs):
            at = (other * mats + m) * depth
            up = jnp.where(slab == other - 1, x_ref[at : at + depth].astype(F32)[:1], up)
            at = ((other - 1) * mats + m) * depth
            down = jnp.where(slab == other, x_ref[at : at + depth].astype(F32)[-1:], down)
        above.append(jnp.where(row == depth - 1, up, pltpu.roll(vol[m], depth - 1, 0)))
        below.append(down)
    square = jnp.full((depth, pix), 0.25, F32)
    square_below = jnp.full((1, pix), 0.25, F32)
    diffs, steps = [], []
    for m in range(mats):
        dz, dy, dx = above[m] - vol[m], next_row(vol[m]) - vol[m], next_pixel(vol[m]) - vol[m]
        square = square + (dz * dz + dy * dy + dx * dx)
        diffs.append((dz, dy, dx))
        dz, dy, dx = vol[m][:1] - below[m], next_row(below[m]) - below[m], next_pixel(below[m]) - below[m]
        square_below = square_below + (dz * dz + dy * dy + dx * dx)
        steps.append(dz)
    scale = lax.rsqrt(square)
    scale_below = jnp.where(first == 1, 0.0, lax.rsqrt(square_below))
    for m in range(mats):
        qz, qy, qx = (d * scale for d in diffs[m])
        prev_z = jnp.where(row == 0, steps[m] * scale_below, pltpu.roll(qz, 1, 0))
        out_ref[m] = prev_z - qz + (prev_row(qy) - qy) + (prev_pixel(qx) - qx)


def smooth(where, volume, x_all, edge):
    return pl.pallas_call(
        smooth_kernel,
        out_shape=jax.ShapeDtypeStruct(volume.shape, F32),
        in_specs=[SMEM, VMEM, VMEM, VMEM],
        out_specs=VMEM,
        compiler_params=pltpu.CompilerParams(vmem_limit_bytes=SMALL),
        cost_estimate=pl.CostEstimate(
            flops=40 * volume.size, bytes_accessed=12 * volume.size, transcendentals=volume.size
        ),
    )(where, volume, x_all, edge)


def total_kernel(factor, part_ref, out_ref):
    total = jnp.sum(part_ref[...].astype(F32), axis=0) * factor
    total = total.astype(BF16)
    for copy in range(out_ref.shape[0]):
        out_ref[copy] = total


def total_copies(parts, factor, copies):
    return pl.pallas_call(
        functools.partial(total_kernel, factor),
        out_shape=jax.ShapeDtypeStruct((copies,) + parts.shape[1:], BF16),
        in_specs=[VMEM],
        out_specs=VMEM,
        compiler_params=pltpu.CompilerParams(vmem_limit_bytes=SMALL),
    )(parts)


def step_kernel(grad_ref, smooth_ref, newton_ref, vol_ref, out_ref):
    mats, depth, pix = vol_ref.shape
    owners, copies, _, span = grad_ref.shape
    for owner in range(owners):
        own = slice(owner * span, (owner + 1) * span)
        grad = grad_ref[owner, 0].astype(F32)
        for copy in range(1, copies):
            grad = grad + grad_ref[owner, copy].astype(F32)
        steps = [grad[k * depth : (k + 1) * depth] + 0.5 * smooth_ref[k, :, own] for k in range(mats)]
        for m in range(mats):
            moved = newton_ref[m, 0, :, own].astype(F32) * steps[0]
            for k in range(1, mats):
                moved = moved + newton_ref[m, k, :, own].astype(F32) * steps[k]
            out_ref[m, :, own] = vol_ref[m, :, own] - moved


def newton_step(grad, smoothed, newton, volume):
    return pl.pallas_call(
        step_kernel,
        out_shape=jax.ShapeDtypeStruct(volume.shape, F32),
        in_specs=[VMEM] * 4,
        out_specs=VMEM,
        compiler_params=pltpu.CompilerParams(vmem_limit_bytes=SMALL),
    )(grad, smoothed, newton, volume)


def body(volume, projector, counts, atten, newton):
    depth, mats, pix = volume.shape
    owners, halves, groups, pairs, sides = (
        lax.axis_size(name) for name in ("x", "half", "row", "pair", "side")
    )
    slabs = pairs * sides
    views_all = projector.shape[0] * owners * halves * slabs
    slab, group = lax.axis_index(("pair", "side")), lax.axis_index("row")
    rows, span = mats * depth, pix // owners
    vol = volume.transpose(1, 0, 2)
    x_all = lax.all_to_all(spread(vol, slabs), ("pair", "side"), 0, 0, tiled=True)
    x_all = x_all.reshape(slabs * rows, pix)
    near, binned, tiles = stage(atten, projector[0], counts[0], projector.shape[1] // 2)
    parts = project(tiles, x_all, near, projector[0], binned, owners, sides, slabs, mats)
    parts = parts.reshape(owners * sides, pairs, rows, span)
    edge = jnp.where(slab == 0, vol[:, 0], vol[:, -1])
    ends = []
    for g in range(groups - 1):
        last, start = g * slabs + slabs - 1, (g + 1) * slabs
        ends += [(last, start), (start, last)]
    parts, edge = lax.optimization_barrier((parts, edge))
    parts = lax.all_to_all(parts, ("x", "side"), 0, 0, tiled=True)
    edge = lax.ppermute(edge, ("row", "pair", "side"), ends)
    parts, edge = lax.optimization_barrier((parts, edge))
    mine = total_copies(parts, float(views_all) ** (-0.5), owners * halves)
    mine = mine.reshape(owners * halves * pairs, rows, span)
    grad = lax.all_to_all(mine, ("x", "half", "pair"), 0, 0, tiled=True)
    grad = grad.reshape(owners, halves * pairs, rows, span)
    is_first = jnp.logical_and(slab == 0, group == 0).astype(jnp.int32)
    smoothed = smooth(jnp.stack([slab, is_first]).astype(jnp.int32), vol, x_all, edge)
    updated = newton_step(grad, smoothed, newton.transpose(1, 2, 0, 3), vol)
    return updated.transpose(1, 0, 2)


def solution(mesh):
    views, groups, slabs = mesh.devices.shape
    mesh = jax.sharding.Mesh(
        mesh.devices.reshape(views // 2, 2, groups, slabs // 2, 2),
        ("x", "half", "row", "pair", "side"),
    )
    view, slice_axes = ("x", "half", "pair", "side"), ("row", "pair", "side")
    in_specs = (
        P(slice_axes, None, None),
        P(view, None, None),
        P(view, "row", None, None),
        P(),
        P(slice_axes, None, None, None),
    )
    out_specs = P(slice_axes, None, None)
    return jax.shard_map(body, mesh=mesh, in_specs=in_specs, out_specs=out_specs, check_vma=False)
```

```python
import functools

import jax
import jax.numpy as jnp
from jax import lax
from jax.experimental import pallas as pl
from jax.experimental.pallas import tpu as pltpu
from jax.sharding import PartitionSpec as P

PX = 1024
BF16 = jnp.bfloat16
F32 = jnp.float32
VMEM = pl.BlockSpec(memory_space=pltpu.VMEM)
SMEM = pl.BlockSpec(memory_space=pltpu.SMEM)
HBM = pl.BlockSpec(memory_space=pltpu.HBM)
SMALL = 8 * 1024 * 1024
MEDIUM = 49 * 1024 * 1024
LARGE = 50 * 1024 * 1024
HUGE = 58 * 1024 * 1024


def spread_kernel(vol_ref, out_ref, near_ref, rounded_ref, sems):
    copy_in = pltpu.make_async_copy(vol_ref, near_ref, sems.at[0])
    copy_in.start()
    copy_in.wait()
    mats = near_ref.shape[0]
    rounded_ref[...] = jnp.concatenate([near_ref[m] for m in range(mats)], 0).astype(BF16)
    copies = [
        pltpu.make_async_copy(rounded_ref, out_ref.at[copy], sems.at[copy + 1])
        for copy in range(out_ref.shape[0])
    ]
    for copy in copies:
        copy.start()
    for copy in copies:
        copy.wait()


def spread(volume, copies):
    mats, depth, pix = volume.shape
    return pl.pallas_call(
        spread_kernel,
        out_shape=jax.ShapeDtypeStruct((copies, mats * depth, pix), BF16),
        in_specs=[HBM],
        out_specs=HBM,
        scratch_shapes=[
            pltpu.VMEM(volume.shape, F32),
            pltpu.VMEM((mats * depth, pix), BF16),
            pltpu.SemaphoreType.DMA((copies + 1,)),
        ],
        compiler_params=pltpu.CompilerParams(vmem_limit_bytes=HUGE),
    )(volume)


def stage_kernel(
    atten_ref, proj_ref, counts_ref, near_ref, binned_ref, tiles_ref, atten_near, counts_near, sems
):
    copy_atten = pltpu.make_async_copy(atten_ref, atten_near, sems.at[0])
    copy_counts = pltpu.make_async_copy(counts_ref, counts_near, sems.at[1])
    copy_proj = pltpu.make_async_copy(proj_ref.at[: near_ref.shape[0]], near_ref, sems.at[2])
    copy_atten.start()
    copy_counts.start()
    copy_proj.start()
    bins, mats = atten_ref.shape
    copy_atten.wait()
    for b in range(bins):
        for m in range(mats):
            tiles_ref[b * mats + m] = jnp.full(tiles_ref.shape[1:], atten_near[b, m], F32)
    copy_counts.wait()
    for b in range(bins):
        binned_ref[b] = counts_near[:, b, :].astype(F32)
    copy_proj.wait()


def stage(atten, projector, counts, held):
    slices, bins, cols = counts.shape
    return pl.pallas_call(
        stage_kernel,
        out_shape=[
            jax.ShapeDtypeStruct((held, projector.shape[1]), BF16),
            jax.ShapeDtypeStruct((bins, slices, cols), F32),
            jax.ShapeDtypeStruct((atten.size, 8, 128), F32),
        ],
        in_specs=[HBM, HBM, HBM],
        out_specs=[VMEM] * 3,
        scratch_shapes=[
            pltpu.SMEM(atten.shape, F32),
            pltpu.VMEM(counts.shape, BF16),
            pltpu.SemaphoreType.DMA((3,)),
        ],
        compiler_params=pltpu.CompilerParams(vmem_limit_bytes=LARGE),
        cost_estimate=pl.CostEstimate(flops=0, bytes_accessed=4 * projector.size, transcendentals=0),
    )(atten, projector, counts)


def wide_tile(tile, wide):
    return jnp.concatenate([tile] * (wide // tile.shape[1]), 1)


def project_kernel(mats, bins, slabs, tiles_ref, x_ref, near_ref, proj_ref, counts_ref, out_ref, resid_ref, rest_ref, block_ref, sems, out_sems):
    rows, pix = x_ref.shape
    cols, held = proj_ref.shape[0], near_ref.shape[0]
    wide = 256
    copies = [
        pltpu.make_async_copy(
            proj_ref.at[at : at + wide], rest_ref.at[at - held : at - held + wide], sems.at[i]
        )
        for i, at in enumerate(range(held, cols, wide))
    ]
    for copy in copies:
        copy.start()
    per_slab = rows // slabs
    depth = per_slab // mats
    atten = [[wide_tile(tiles_ref[b * mats + m], wide) for m in range(mats)] for b in range(bins)]
    for at in range(0, cols, wide):
        if at >= held:
            copies[(at - held) // wide].wait()
        block = near_ref[at : at + wide] if at < held else rest_ref[at - held : at - held + wide]
        line = lax.dot_general(
            x_ref[...], block, (((1,), (1,)), ((), ())), preferred_element_type=F32
        )
        blocks = []
        for slab in range(slabs):
            lines = [line[slab * per_slab + m * depth :][:depth] for m in range(mats)]
            parts = [None] * mats
            for b in range(bins):
                power = atten[b][0] * lines[0]
                for m in range(1, mats):
                    power = power + atten[b][m] * lines[m]
                seen = counts_ref[b, slab * depth : (slab + 1) * depth, at : at + wide]
                diff = seen - jnp.exp(-power)
                for m in range(mats):
                    term = atten[b][m] * diff
                    parts[m] = term if parts[m] is None else parts[m] + term
            blocks += parts
        resid_ref[:, at : at + wide] = jnp.concatenate(blocks, 0).astype(BF16)
    owners, sides, pairs, _, span = out_ref.shape
    copies_out = []
    for owner in range(owners):
        own = slice(owner * span, (owner + 1) * span)
        back = jnp.dot(resid_ref[:, :held], near_ref[:, own], preferred_element_type=F32)
        back = back + jnp.dot(resid_ref[:, held:], rest_ref[:, own], preferred_element_type=F32)
        for slab in range(slabs):
            block_ref[owner, slab % sides, slab // sides] = back[
                slab * per_slab : (slab + 1) * per_slab
            ].astype(BF16)
        copies_out.append(
            pltpu.make_async_copy(block_ref.at[owner], out_ref.at[owner], out_sems.at[owner])
        )
        copies_out[-1].start()
    for copy in copies_out:
        copy.wait()


def project(tiles, x_all, near, projector, counts, owners, sides, slabs, mats):
    rows, pix = x_all.shape
    cols = counts.shape[2]
    out = (owners, sides, slabs // sides, rows // slabs, pix // owners)
    return pl.pallas_call(
        functools.partial(project_kernel, mats, counts.shape[0], slabs),
        out_shape=jax.ShapeDtypeStruct(out, BF16),
        in_specs=[VMEM, VMEM, VMEM, HBM, VMEM],
        out_specs=HBM,
        scratch_shapes=[
            pltpu.VMEM((rows, cols), BF16),
            pltpu.VMEM((cols - near.shape[0], pix), BF16),
            pltpu.VMEM(out, BF16),
            pltpu.SemaphoreType.DMA(((cols - near.shape[0]) // 256,)),
            pltpu.SemaphoreType.DMA((owners,)),
        ],
        compiler_params=pltpu.CompilerParams(vmem_limit_bytes=MEDIUM),
        cost_estimate=pl.CostEstimate(
            flops=4 * rows * cols * pix, bytes_accessed=2 * cols * pix, transcendentals=rows * cols
        ),
    )(tiles, x_all, near, projector, counts)


def next_pixel(field):
    column = lax.broadcasted_iota(jnp.int32, field.shape, 1) % PX
    return jnp.where(column == PX - 1, 0.0, pltpu.roll(field, field.shape[1] - 1, 1))


def next_row(field):
    return jnp.concatenate([field[:, PX:], jnp.zeros((field.shape[0], PX), F32)], 1)


def prev_pixel(flux):
    column = lax.broadcasted_iota(jnp.int32, flux.shape, 1) % PX
    return jnp.where(column == 0, 0.0, pltpu.roll(flux, 1, 1))


def prev_row(flux):
    return jnp.concatenate([jnp.zeros((flux.shape[0], PX), F32), flux[:, :-PX]], 1)


def smooth_kernel(where_ref, vol_ref, x_ref, edge_ref, out_ref):
    mats, depth, pix = vol_ref.shape
    slabs = x_ref.shape[0] // (mats * depth)
    slab, first = where_ref[0], where_ref[1]
    row = lax.broadcasted_iota(jnp.int32, (depth, pix), 0)
    vol, above, below = [], [], []
    for m in range(mats):
        vol.append(vol_ref[m])
        up = down = edge_ref[m : m + 1]
        for other in range(1, slabs):
            at = (other * mats + m) * depth
            up = jnp.where(slab == other - 1, x_ref[at : at + depth].astype(F32)[:1], up)
            at = ((other - 1) * mats + m) * depth
            down = jnp.where(slab == other, x_ref[at : at + depth].astype(F32)[-1:], down)
        above.append(jnp.where(row == depth - 1, up, pltpu.roll(vol[m], depth - 1, 0)))
        below.append(down)
    square = jnp.full((depth, pix), 0.25, F32)
    square_below = jnp.full((1, pix), 0.25, F32)
    diffs, steps = [], []
    for m in range(mats):
        dz, dy, dx = above[m] - vol[m], next_row(vol[m]) - vol[m], next_pixel(vol[m]) - vol[m]
        square = square + (dz * dz + dy * dy + dx * dx)
        diffs.append((dz, dy, dx))
        dz, dy, dx = vol[m][:1] - below[m], next_row(below[m]) - below[m], next_pixel(below[m]) - below[m]
        square_below = square_below + (dz * dz + dy * dy + dx * dx)
        steps.append(dz)
    scale = lax.rsqrt(square)
    scale_below = jnp.where(first == 1, 0.0, lax.rsqrt(square_below))
    for m in range(mats):
        qz, qy, qx = (d * scale for d in diffs[m])
        prev_z = jnp.where(row == 0, steps[m] * scale_below, pltpu.roll(qz, 1, 0))
        out_ref[m] = prev_z - qz + (prev_row(qy) - qy) + (prev_pixel(qx) - qx)


def smooth(where, volume, x_all, edge):
    return pl.pallas_call(
        smooth_kernel,
        out_shape=jax.ShapeDtypeStruct(volume.shape, F32),
        in_specs=[SMEM, VMEM, VMEM, VMEM],
        out_specs=VMEM,
        compiler_params=pltpu.CompilerParams(vmem_limit_bytes=SMALL),
        cost_estimate=pl.CostEstimate(
            flops=40 * volume.size, bytes_accessed=12 * volume.size, transcendentals=volume.size
        ),
    )(where, volume, x_all, edge)


def total_kernel(factor, part_ref, out_ref):
    total = jnp.sum(part_ref[...].astype(F32), axis=0) * factor
    total = total.astype(BF16)
    for copy in range(out_ref.shape[0]):
        out_ref[copy] = total


def total_copies(parts, factor, copies):
    return pl.pallas_call(
        functools.partial(total_kernel, factor),
        out_shape=jax.ShapeDtypeStruct((copies,) + parts.shape[1:], BF16),
        in_specs=[VMEM],
        out_specs=VMEM,
        compiler_params=pltpu.CompilerParams(vmem_limit_bytes=SMALL),
    )(parts)


def step_kernel(grad_ref, smooth_ref, newton_ref, vol_ref, out_ref):
    mats, depth, pix = vol_ref.shape
    owners, copies, _, span = grad_ref.shape
    for owner in range(owners):
        own = slice(owner * span, (owner + 1) * span)
        grad = grad_ref[owner, 0].astype(F32)
        for copy in range(1, copies):
            grad = grad + grad_ref[owner, copy].astype(F32)
        steps = [grad[k * depth : (k + 1) * depth] + 0.5 * smooth_ref[k, :, own] for k in range(mats)]
        for m in range(mats):
            moved = newton_ref[m, 0, :, own].astype(F32) * steps[0]
            for k in range(1, mats):
                moved = moved + newton_ref[m, k, :, own].astype(F32) * steps[k]
            out_ref[m, :, own] = vol_ref[m, :, own] - moved


def newton_step(grad, smoothed, newton, volume):
    return pl.pallas_call(
        step_kernel,
        out_shape=jax.ShapeDtypeStruct(volume.shape, F32),
        in_specs=[VMEM] * 4,
        out_specs=VMEM,
        compiler_params=pltpu.CompilerParams(vmem_limit_bytes=SMALL),
    )(grad, smoothed, newton, volume)


def body(volume, projector, counts, atten, newton):
    depth, mats, pix = volume.shape
    owners, halves, groups, pairs, sides = (
        lax.axis_size(name) for name in ("x", "half", "row", "pair", "side")
    )
    slabs = pairs * sides
    views_all = projector.shape[0] * owners * halves * slabs
    slab, group = lax.axis_index(("pair", "side")), lax.axis_index("row")
    rows, span = mats * depth, pix // owners
    vol = volume.transpose(1, 0, 2)
    x_all = lax.all_to_all(spread(vol, slabs), ("pair", "side"), 0, 0, tiled=True)
    x_all = x_all.reshape(slabs * rows, pix)
    near, binned, tiles = stage(atten, projector[0], counts[0], projector.shape[1] // 2)
    parts = project(tiles, x_all, near, projector[0], binned, owners, sides, slabs, mats)
    parts = parts.reshape(owners * sides, pairs, rows, span)
    edge = jnp.where(slab == 0, vol[:, 0], vol[:, -1])
    ends = []
    for g in range(groups - 1):
        last, start = g * slabs + slabs - 1, (g + 1) * slabs
        ends += [(last, start), (start, last)]
    parts = lax.all_to_all(parts, ("x", "side"), 0, 0, tiled=True)
    mine = total_copies(parts, float(views_all) ** (-0.5), owners * halves)
    mine, edge = lax.optimization_barrier((mine, edge))
    edge = lax.ppermute(edge, ("row", "pair", "side"), ends)
    mine = mine.reshape(owners * halves * pairs, rows, span)
    grad = lax.all_to_all(mine, ("x", "half", "pair"), 0, 0, tiled=True)
    grad = grad.reshape(owners, halves * pairs, rows, span)
    is_first = jnp.logical_and(slab == 0, group == 0).astype(jnp.int32)
    smoothed = smooth(jnp.stack([slab, is_first]).astype(jnp.int32), vol, x_all, edge)
    updated = newton_step(grad, smoothed, newton.transpose(1, 2, 0, 3), vol)
    return updated.transpose(1, 0, 2)


def solution(mesh):
    views, groups, slabs = mesh.devices.shape
    mesh = jax.sharding.Mesh(
        mesh.devices.reshape(views // 2, 2, groups, slabs // 2, 2),
        ("x", "half", "row", "pair", "side"),
    )
    view, slice_axes = ("x", "half", "pair", "side"), ("row", "pair", "side")
    in_specs = (
        P(slice_axes, None, None),
        P(view, None, None),
        P(view, "row", None, None),
        P(),
        P(slice_axes, None, None, None),
    )
    out_specs = P(slice_axes, None, None)
    return jax.shard_map(body, mesh=mesh, in_specs=in_specs, out_specs=out_specs, check_vma=False)
```

```python
import functools

import jax
import jax.numpy as jnp
from jax import lax
from jax.experimental import pallas as pl
from jax.experimental.pallas import tpu as pltpu
from jax.sharding import PartitionSpec as P

PX = 1024
BF16 = jnp.bfloat16
F32 = jnp.float32
VMEM = pl.BlockSpec(memory_space=pltpu.VMEM)
SMEM = pl.BlockSpec(memory_space=pltpu.SMEM)
HBM = pl.BlockSpec(memory_space=pltpu.HBM)
SMALL = 8 * 1024 * 1024
MEDIUM = 49 * 1024 * 1024
LARGE = 50 * 1024 * 1024
HUGE = 58 * 1024 * 1024


def spread_kernel(vol_ref, out_ref, near_ref, rounded_ref, sems):
    copy_in = pltpu.make_async_copy(vol_ref, near_ref, sems.at[0])
    copy_in.start()
    copy_in.wait()
    mats = near_ref.shape[0]
    rounded_ref[...] = jnp.concatenate([near_ref[m] for m in range(mats)], 0).astype(BF16)
    copies = [
        pltpu.make_async_copy(rounded_ref, out_ref.at[copy], sems.at[copy + 1])
        for copy in range(out_ref.shape[0])
    ]
    for copy in copies:
        copy.start()
    for copy in copies:
        copy.wait()


def spread(volume, copies):
    mats, depth, pix = volume.shape
    return pl.pallas_call(
        spread_kernel,
        out_shape=jax.ShapeDtypeStruct((copies, mats * depth, pix), BF16),
        in_specs=[HBM],
        out_specs=HBM,
        scratch_shapes=[
            pltpu.VMEM(volume.shape, F32),
            pltpu.VMEM((mats * depth, pix), BF16),
            pltpu.SemaphoreType.DMA((copies + 1,)),
        ],
        compiler_params=pltpu.CompilerParams(vmem_limit_bytes=HUGE),
    )(volume)


def stage_kernel(
    atten_ref, proj_ref, counts_ref, near_ref, binned_ref, tiles_ref, atten_near, counts_near, sems
):
    copy_atten = pltpu.make_async_copy(atten_ref, atten_near, sems.at[0])
    copy_counts = pltpu.make_async_copy(counts_ref, counts_near, sems.at[1])
    copy_proj = pltpu.make_async_copy(proj_ref.at[: near_ref.shape[0]], near_ref, sems.at[2])
    copy_atten.start()
    copy_counts.start()
    copy_proj.start()
    bins, mats = atten_ref.shape
    copy_atten.wait()
    for b in range(bins):
        for m in range(mats):
            tiles_ref[b * mats + m] = jnp.full(tiles_ref.shape[1:], atten_near[b, m], F32)
    copy_counts.wait()
    for b in range(bins):
        binned_ref[b] = counts_near[:, b, :].astype(F32)
    copy_proj.wait()


def stage(atten, projector, counts, held):
    slices, bins, cols = counts.shape
    return pl.pallas_call(
        stage_kernel,
        out_shape=[
            jax.ShapeDtypeStruct((held, projector.shape[1]), BF16),
            jax.ShapeDtypeStruct((bins, slices, cols), F32),
            jax.ShapeDtypeStruct((atten.size, 8, 128), F32),
        ],
        in_specs=[HBM, HBM, HBM],
        out_specs=[VMEM] * 3,
        scratch_shapes=[
            pltpu.SMEM(atten.shape, F32),
            pltpu.VMEM(counts.shape, BF16),
            pltpu.SemaphoreType.DMA((3,)),
        ],
        compiler_params=pltpu.CompilerParams(vmem_limit_bytes=LARGE),
        cost_estimate=pl.CostEstimate(flops=0, bytes_accessed=4 * projector.size, transcendentals=0),
    )(atten, projector, counts)


def wide_tile(tile, wide):
    return jnp.concatenate([tile] * (wide // tile.shape[1]), 1)


def project_kernel(mats, bins, slabs, tiles_ref, x_ref, near_ref, proj_ref, counts_ref, out_ref, resid_ref, rest_ref, sems):
    rows, pix = x_ref.shape
    cols, held = proj_ref.shape[0], near_ref.shape[0]
    wide = 256
    copies = [
        pltpu.make_async_copy(
            proj_ref.at[at : at + wide], rest_ref.at[at - held : at - held + wide], sems.at[i]
        )
        for i, at in enumerate(range(held, cols, wide))
    ]
    for copy in copies:
        copy.start()
    per_slab = rows // slabs
    depth = per_slab // mats
    atten = [[wide_tile(tiles_ref[b * mats + m], wide) for m in range(mats)] for b in range(bins)]
    for at in range(0, cols, wide):
        if at >= held:
            copies[(at - held) // wide].wait()
        block = near_ref[at : at + wide] if at < held else rest_ref[at - held : at - held + wide]
        line = lax.dot_general(
            x_ref[...], block, (((1,), (1,)), ((), ())), preferred_element_type=F32
        )
        blocks = []
        for slab in range(slabs):
            lines = [line[slab * per_slab + m * depth :][:depth] for m in range(mats)]
            parts = [None] * mats
            for b in range(bins):
                power = atten[b][0] * lines[0]
                for m in range(1, mats):
                    power = power + atten[b][m] * lines[m]
                seen = counts_ref[b, slab * depth : (slab + 1) * depth, at : at + wide]
                diff = seen - jnp.exp(-power)
                for m in range(mats):
                    term = atten[b][m] * diff
                    parts[m] = term if parts[m] is None else parts[m] + term
            blocks += parts
        resid_ref[:, at : at + wide] = jnp.concatenate(blocks, 0).astype(BF16)
    owners, sides, _, _, span = out_ref.shape
    for owner in range(owners):
        own = slice(owner * span, (owner + 1) * span)
        back = jnp.dot(resid_ref[:, :held], near_ref[:, own], preferred_element_type=F32)
        back = back + jnp.dot(resid_ref[:, held:], rest_ref[:, own], preferred_element_type=F32)
        for slab in range(slabs):
            out_ref[owner, slab % sides, slab // sides] = back[
                slab * per_slab : (slab + 1) * per_slab
            ].astype(BF16)


def project(tiles, x_all, near, projector, counts, owners, sides, slabs, mats):
    rows, pix = x_all.shape
    cols = counts.shape[2]
    out = (owners, sides, slabs // sides, rows // slabs, pix // owners)
    return pl.pallas_call(
        functools.partial(project_kernel, mats, counts.shape[0], slabs),
        out_shape=jax.ShapeDtypeStruct(out, BF16),
        in_specs=[VMEM, VMEM, VMEM, HBM, VMEM],
        out_specs=VMEM,
        scratch_shapes=[
            pltpu.VMEM((rows, cols), BF16),
            pltpu.VMEM((cols - near.shape[0], pix), BF16),
            pltpu.SemaphoreType.DMA(((cols - near.shape[0]) // 256,)),
        ],
        compiler_params=pltpu.CompilerParams(vmem_limit_bytes=MEDIUM),
        cost_estimate=pl.CostEstimate(
            flops=4 * rows * cols * pix, bytes_accessed=2 * cols * pix, transcendentals=rows * cols
        ),
    )(tiles, x_all, near, projector, counts)


def next_pixel(field):
    column = lax.broadcasted_iota(jnp.int32, field.shape, 1) % PX
    return jnp.where(column == PX - 1, 0.0, pltpu.roll(field, field.shape[1] - 1, 1))


def next_row(field):
    return jnp.concatenate([field[:, PX:], jnp.zeros((field.shape[0], PX), F32)], 1)


def prev_pixel(flux):
    column = lax.broadcasted_iota(jnp.int32, flux.shape, 1) % PX
    return jnp.where(column == 0, 0.0, pltpu.roll(flux, 1, 1))


def prev_row(flux):
    return jnp.concatenate([jnp.zeros((flux.shape[0], PX), F32), flux[:, :-PX]], 1)


def smooth_kernel(where_ref, vol_ref, x_ref, edge_ref, out_ref):
    mats, depth, pix = vol_ref.shape
    slabs = x_ref.shape[0] // (mats * depth)
    slab, first = where_ref[0], where_ref[1]
    row = lax.broadcasted_iota(jnp.int32, (depth, pix), 0)
    vol, above, below = [], [], []
    for m in range(mats):
        vol.append(vol_ref[m])
        up = down = edge_ref[m : m + 1]
        for other in range(1, slabs):
            at = (other * mats + m) * depth
            up = jnp.where(slab == other - 1, x_ref[at : at + depth].astype(F32)[:1], up)
            at = ((other - 1) * mats + m) * depth
            down = jnp.where(slab == other, x_ref[at : at + depth].astype(F32)[-1:], down)
        above.append(jnp.where(row == depth - 1, up, pltpu.roll(vol[m], depth - 1, 0)))
        below.append(down)
    square = jnp.full((depth, pix), 0.25, F32)
    square_below = jnp.full((1, pix), 0.25, F32)
    diffs, steps = [], []
    for m in range(mats):
        dz, dy, dx = above[m] - vol[m], next_row(vol[m]) - vol[m], next_pixel(vol[m]) - vol[m]
        square = square + (dz * dz + dy * dy + dx * dx)
        diffs.append((dz, dy, dx))
        dz, dy, dx = vol[m][:1] - below[m], next_row(below[m]) - below[m], next_pixel(below[m]) - below[m]
        square_below = square_below + (dz * dz + dy * dy + dx * dx)
        steps.append(dz)
    scale = lax.rsqrt(square)
    scale_below = jnp.where(first == 1, 0.0, lax.rsqrt(square_below))
    for m in range(mats):
        qz, qy, qx = (d * scale for d in diffs[m])
        prev_z = jnp.where(row == 0, steps[m] * scale_below, pltpu.roll(qz, 1, 0))
        out_ref[m] = prev_z - qz + (prev_row(qy) - qy) + (prev_pixel(qx) - qx)


def smooth(where, volume, x_all, edge):
    return pl.pallas_call(
        smooth_kernel,
        out_shape=jax.ShapeDtypeStruct(volume.shape, F32),
        in_specs=[SMEM, VMEM, VMEM, VMEM],
        out_specs=VMEM,
        compiler_params=pltpu.CompilerParams(vmem_limit_bytes=SMALL),
        cost_estimate=pl.CostEstimate(
            flops=40 * volume.size, bytes_accessed=12 * volume.size, transcendentals=volume.size
        ),
    )(where, volume, x_all, edge)


def total_kernel(factor, part_ref, out_ref):
    total = jnp.sum(part_ref[...].astype(F32), axis=0) * factor
    total = total.astype(BF16)
    for copy in range(out_ref.shape[0]):
        out_ref[copy] = total


def total_copies(parts, factor, copies):
    return pl.pallas_call(
        functools.partial(total_kernel, factor),
        out_shape=jax.ShapeDtypeStruct((copies,) + parts.shape[1:], BF16),
        in_specs=[VMEM],
        out_specs=VMEM,
        compiler_params=pltpu.CompilerParams(vmem_limit_bytes=SMALL),
    )(parts)


def step_kernel(grad_ref, smooth_ref, newton_ref, vol_ref, out_ref):
    mats, depth, pix = vol_ref.shape
    owners, copies, _, span = grad_ref.shape
    for owner in range(owners):
        own = slice(owner * span, (owner + 1) * span)
        grad = grad_ref[owner, 0].astype(F32)
        for copy in range(1, copies):
            grad = grad + grad_ref[owner, copy].astype(F32)
        steps = [grad[k * depth : (k + 1) * depth] + 0.5 * smooth_ref[k, :, own] for k in range(mats)]
        for m in range(mats):
            moved = newton_ref[m, 0, :, own].astype(F32) * steps[0]
            for k in range(1, mats):
                moved = moved + newton_ref[m, k, :, own].astype(F32) * steps[k]
            out_ref[m, :, own] = vol_ref[m, :, own] - moved


def newton_step(grad, smoothed, newton, volume):
    return pl.pallas_call(
        step_kernel,
        out_shape=jax.ShapeDtypeStruct(volume.shape, F32),
        in_specs=[VMEM] * 4,
        out_specs=VMEM,
        compiler_params=pltpu.CompilerParams(vmem_limit_bytes=SMALL),
    )(grad, smoothed, newton, volume)


def body(volume, projector, counts, atten, newton):
    depth, mats, pix = volume.shape
    owners, halves, groups, pairs, sides = (
        lax.axis_size(name) for name in ("x", "half", "row", "pair", "side")
    )
    slabs = pairs * sides
    views_all = projector.shape[0] * owners * halves * slabs
    slab, group = lax.axis_index(("pair", "side")), lax.axis_index("row")
    rows, span = mats * depth, pix // owners
    vol = volume.transpose(1, 0, 2)
    x_all = lax.all_to_all(spread(vol, slabs), ("pair", "side"), 0, 0, tiled=True)
    x_all = x_all.reshape(slabs * rows, pix)
    where = jnp.stack([slab, jnp.logical_and(slab == 0, group == 0)]).astype(jnp.int32)
    x_all, where, slab = lax.optimization_barrier((x_all, where, slab))
    near, binned, tiles = stage(atten, projector[0], counts[0], projector.shape[1] // 2)
    parts = project(tiles, x_all, near, projector[0], binned, owners, sides, slabs, mats)
    parts = parts.reshape(owners * sides, pairs, rows, span)
    parts = lax.all_to_all(parts, ("x", "side"), 0, 0, tiled=True)
    sums = total_copies(parts, 1.0, halves).reshape(halves * pairs, rows, span)
    sums, vol = lax.optimization_barrier((sums, vol))
    edge = jnp.where(slab == 0, vol[:, 0], vol[:, -1])
    ends = []
    for g in range(groups - 1):
        last, start = g * slabs + slabs - 1, (g + 1) * slabs
        ends += [(last, start), (start, last)]
    edge = lax.ppermute(edge, ("row", "pair", "side"), ends)
    sums = lax.all_to_all(sums, ("half", "pair"), 0, 0, tiled=True)
    sums, edge = lax.optimization_barrier((sums, edge))
    mine = total_copies(sums, float(views_all) ** (-0.5), owners)
    grad = lax.all_to_all(mine, "x", 0, 0, tiled=True)
    grad = grad.reshape(owners, 1, rows, span)
    smoothed = smooth(where, vol, x_all, edge)
    updated = newton_step(grad, smoothed, newton.transpose(1, 2, 0, 3), vol)
    return updated.transpose(1, 0, 2)


def solution(mesh):
    views, groups, slabs = mesh.devices.shape
    mesh = jax.sharding.Mesh(
        mesh.devices.reshape(views // 2, 2, groups, slabs // 2, 2),
        ("x", "half", "row", "pair", "side"),
    )
    view, slice_axes = ("x", "half", "pair", "side"), ("row", "pair", "side")
    in_specs = (
        P(slice_axes, None, None),
        P(view, None, None),
        P(view, "row", None, None),
        P(),
        P(slice_axes, None, None, None),
    )
    out_specs = P(slice_axes, None, None)
    return jax.shard_map(body, mesh=mesh, in_specs=in_specs, out_specs=out_specs, check_vma=False)
```

```python
import functools

import jax
import jax.numpy as jnp
from jax import lax
from jax.experimental import pallas as pl
from jax.experimental.pallas import tpu as pltpu
from jax.sharding import PartitionSpec as P

PX = 1024
BF16 = jnp.bfloat16
F32 = jnp.float32
VMEM = pl.BlockSpec(memory_space=pltpu.VMEM)
SMEM = pl.BlockSpec(memory_space=pltpu.SMEM)
HBM = pl.BlockSpec(memory_space=pltpu.HBM)
SMALL = 8 * 1024 * 1024
MEDIUM = 49 * 1024 * 1024
LARGE = 50 * 1024 * 1024
HUGE = 58 * 1024 * 1024


def spread_kernel(vol_ref, out_ref, near_ref, rounded_ref, sems):
    copy_in = pltpu.make_async_copy(vol_ref, near_ref, sems.at[0])
    copy_in.start()
    copy_in.wait()
    mats = near_ref.shape[0]
    rounded_ref[...] = jnp.concatenate([near_ref[m] for m in range(mats)], 0).astype(BF16)
    copies = [
        pltpu.make_async_copy(rounded_ref, out_ref.at[copy], sems.at[copy + 1])
        for copy in range(out_ref.shape[0])
    ]
    for copy in copies:
        copy.start()
    for copy in copies:
        copy.wait()


def spread(volume, copies):
    mats, depth, pix = volume.shape
    return pl.pallas_call(
        spread_kernel,
        out_shape=jax.ShapeDtypeStruct((copies, mats * depth, pix), BF16),
        in_specs=[HBM],
        out_specs=HBM,
        scratch_shapes=[
            pltpu.VMEM(volume.shape, F32),
            pltpu.VMEM((mats * depth, pix), BF16),
            pltpu.SemaphoreType.DMA((copies + 1,)),
        ],
        compiler_params=pltpu.CompilerParams(vmem_limit_bytes=HUGE),
    )(volume)


def stage_kernel(
    atten_ref, proj_ref, counts_ref, near_ref, binned_ref, tiles_ref, atten_near, counts_near, sems
):
    copy_atten = pltpu.make_async_copy(atten_ref, atten_near, sems.at[0])
    copy_counts = pltpu.make_async_copy(counts_ref, counts_near, sems.at[1])
    copy_proj = pltpu.make_async_copy(proj_ref.at[: near_ref.shape[0]], near_ref, sems.at[2])
    copy_atten.start()
    copy_counts.start()
    copy_proj.start()
    bins, mats = atten_ref.shape
    copy_atten.wait()
    for b in range(bins):
        for m in range(mats):
            tiles_ref[b * mats + m] = jnp.full(tiles_ref.shape[1:], atten_near[b, m], F32)
    copy_counts.wait()
    for b in range(bins):
        binned_ref[b] = counts_near[:, b, :].astype(F32)
    copy_proj.wait()


def stage(atten, projector, counts, held):
    slices, bins, cols = counts.shape
    return pl.pallas_call(
        stage_kernel,
        out_shape=[
            jax.ShapeDtypeStruct((held, projector.shape[1]), BF16),
            jax.ShapeDtypeStruct((bins, slices, cols), F32),
            jax.ShapeDtypeStruct((atten.size, 8, 128), F32),
        ],
        in_specs=[HBM, HBM, HBM],
        out_specs=[VMEM] * 3,
        scratch_shapes=[
            pltpu.SMEM(atten.shape, F32),
            pltpu.VMEM(counts.shape, BF16),
            pltpu.SemaphoreType.DMA((3,)),
        ],
        compiler_params=pltpu.CompilerParams(vmem_limit_bytes=LARGE),
        cost_estimate=pl.CostEstimate(flops=0, bytes_accessed=4 * projector.size, transcendentals=0),
    )(atten, projector, counts)


def wide_tile(tile, wide):
    return jnp.concatenate([tile] * (wide // tile.shape[1]), 1)


def project_kernel(mats, bins, slabs, tiles_ref, x_ref, near_ref, proj_ref, counts_ref, out_ref, resid_ref, rest_ref, sems):
    rows, pix = x_ref.shape
    cols, held = proj_ref.shape[0], near_ref.shape[0]
    wide = 256
    copies = [
        pltpu.make_async_copy(
            proj_ref.at[at : at + wide], rest_ref.at[at - held : at - held + wide], sems.at[i]
        )
        for i, at in enumerate(range(held, cols, wide))
    ]
    for copy in copies:
        copy.start()
    per_slab = rows // slabs
    depth = per_slab // mats
    atten = [[wide_tile(tiles_ref[b * mats + m], wide) for m in range(mats)] for b in range(bins)]
    for at in range(0, cols, wide):
        if at >= held:
            copies[(at - held) // wide].wait()
        block = near_ref[at : at + wide] if at < held else rest_ref[at - held : at - held + wide]
        line = lax.dot_general(
            x_ref[...], block, (((1,), (1,)), ((), ())), preferred_element_type=F32
        )
        blocks = []
        for slab in range(slabs):
            lines = [line[slab * per_slab + m * depth :][:depth] for m in range(mats)]
            parts = [None] * mats
            for b in range(bins):
                power = atten[b][0] * lines[0]
                for m in range(1, mats):
                    power = power + atten[b][m] * lines[m]
                seen = counts_ref[b, slab * depth : (slab + 1) * depth, at : at + wide]
                diff = seen - jnp.exp(-power)
                for m in range(mats):
                    term = atten[b][m] * diff
                    parts[m] = term if parts[m] is None else parts[m] + term
            blocks += parts
        resid_ref[:, at : at + wide] = jnp.concatenate(blocks, 0).astype(BF16)
    owners, sides, _, _, span = out_ref.shape
    for owner in range(owners):
        own = slice(owner * span, (owner + 1) * span)
        back = jnp.dot(resid_ref[:, :held], near_ref[:, own], preferred_element_type=F32)
        back = back + jnp.dot(resid_ref[:, held:], rest_ref[:, own], preferred_element_type=F32)
        for slab in range(slabs):
            out_ref[owner, slab % sides, slab // sides] = back[
                slab * per_slab : (slab + 1) * per_slab
            ].astype(BF16)


def project(tiles, x_all, near, projector, counts, owners, sides, slabs, mats):
    rows, pix = x_all.shape
    cols = counts.shape[2]
    out = (owners, sides, slabs // sides, rows // slabs, pix // owners)
    return pl.pallas_call(
        functools.partial(project_kernel, mats, counts.shape[0], slabs),
        out_shape=jax.ShapeDtypeStruct(out, BF16),
        in_specs=[VMEM, VMEM, VMEM, HBM, VMEM],
        out_specs=VMEM,
        scratch_shapes=[
            pltpu.VMEM((rows, cols), BF16),
            pltpu.VMEM((cols - near.shape[0], pix), BF16),
            pltpu.SemaphoreType.DMA(((cols - near.shape[0]) // 256,)),
        ],
        compiler_params=pltpu.CompilerParams(vmem_limit_bytes=MEDIUM),
        cost_estimate=pl.CostEstimate(
            flops=4 * rows * cols * pix, bytes_accessed=2 * cols * pix, transcendentals=rows * cols
        ),
    )(tiles, x_all, near, projector, counts)


def next_pixel(field):
    column = lax.broadcasted_iota(jnp.int32, field.shape, 1) % PX
    return jnp.where(column == PX - 1, 0.0, pltpu.roll(field, field.shape[1] - 1, 1))


def next_row(field):
    return jnp.concatenate([field[:, PX:], jnp.zeros((field.shape[0], PX), F32)], 1)


def prev_pixel(flux):
    column = lax.broadcasted_iota(jnp.int32, flux.shape, 1) % PX
    return jnp.where(column == 0, 0.0, pltpu.roll(flux, 1, 1))


def prev_row(flux):
    return jnp.concatenate([jnp.zeros((flux.shape[0], PX), F32), flux[:, :-PX]], 1)


def slab_index():
    return lax.axis_index("pair") * lax.axis_size("side") + lax.axis_index("side")


def smooth_kernel(vol_ref, x_ref, edge_ref, out_ref):
    mats, depth, pix = vol_ref.shape
    slabs = x_ref.shape[0] // (mats * depth)
    slab = slab_index()
    first = jnp.logical_and(slab == 0, lax.axis_index("row") == 0)
    row = lax.broadcasted_iota(jnp.int32, (depth, pix), 0)
    vol, above, below = [], [], []
    for m in range(mats):
        vol.append(vol_ref[m])
        up = down = edge_ref[m : m + 1]
        for other in range(1, slabs):
            at = (other * mats + m) * depth
            up = jnp.where(slab == other - 1, x_ref[at : at + depth].astype(F32)[:1], up)
            at = ((other - 1) * mats + m) * depth
            down = jnp.where(slab == other, x_ref[at : at + depth].astype(F32)[-1:], down)
        above.append(jnp.where(row == depth - 1, up, pltpu.roll(vol[m], depth - 1, 0)))
        below.append(down)
    square = jnp.full((depth, pix), 0.25, F32)
    square_below = jnp.full((1, pix), 0.25, F32)
    diffs, steps = [], []
    for m in range(mats):
        dz, dy, dx = above[m] - vol[m], next_row(vol[m]) - vol[m], next_pixel(vol[m]) - vol[m]
        square = square + (dz * dz + dy * dy + dx * dx)
        diffs.append((dz, dy, dx))
        dz, dy, dx = vol[m][:1] - below[m], next_row(below[m]) - below[m], next_pixel(below[m]) - below[m]
        square_below = square_below + (dz * dz + dy * dy + dx * dx)
        steps.append(dz)
    scale = lax.rsqrt(square)
    scale_below = jnp.where(first, 0.0, lax.rsqrt(square_below))
    for m in range(mats):
        qz, qy, qx = (d * scale for d in diffs[m])
        prev_z = jnp.where(row == 0, steps[m] * scale_below, pltpu.roll(qz, 1, 0))
        out_ref[m] = prev_z - qz + (prev_row(qy) - qy) + (prev_pixel(qx) - qx)


def smooth(volume, x_all, edge):
    return pl.pallas_call(
        smooth_kernel,
        out_shape=jax.ShapeDtypeStruct(volume.shape, F32),
        in_specs=[VMEM, VMEM, VMEM],
        out_specs=VMEM,
        compiler_params=pltpu.CompilerParams(vmem_limit_bytes=SMALL),
        cost_estimate=pl.CostEstimate(
            flops=40 * volume.size, bytes_accessed=12 * volume.size, transcendentals=volume.size
        ),
    )(volume, x_all, edge)


def total_kernel(factor, part_ref, vol_ref, out_ref, edge_ref):
    total = jnp.sum(part_ref[...].astype(F32), axis=0) * factor
    total = total.astype(BF16)
    for copy in range(out_ref.shape[0]):
        out_ref[copy] = total
    slab = slab_index()
    for m in range(vol_ref.shape[0]):
        slab_m = vol_ref[m]
        edge_ref[m : m + 1] = jnp.where(slab == 0, slab_m[:1], slab_m[-1:])


def total_copies(parts, volume, factor, copies):
    mats, _, pix = volume.shape
    return pl.pallas_call(
        functools.partial(total_kernel, factor),
        out_shape=[
            jax.ShapeDtypeStruct((copies,) + parts.shape[1:], BF16),
            jax.ShapeDtypeStruct((mats, pix), F32),
        ],
        in_specs=[VMEM, VMEM],
        out_specs=[VMEM, VMEM],
        compiler_params=pltpu.CompilerParams(vmem_limit_bytes=SMALL),
    )(parts, volume)


def step_kernel(grad_ref, smooth_ref, newton_ref, vol_ref, out_ref):
    mats, depth, pix = vol_ref.shape
    owners, copies, _, span = grad_ref.shape
    for owner in range(owners):
        own = slice(owner * span, (owner + 1) * span)
        grad = grad_ref[owner, 0].astype(F32)
        for copy in range(1, copies):
            grad = grad + grad_ref[owner, copy].astype(F32)
        steps = [grad[k * depth : (k + 1) * depth] + 0.5 * smooth_ref[k, :, own] for k in range(mats)]
        for m in range(mats):
            moved = newton_ref[m, 0, :, own].astype(F32) * steps[0]
            for k in range(1, mats):
                moved = moved + newton_ref[m, k, :, own].astype(F32) * steps[k]
            out_ref[m, :, own] = vol_ref[m, :, own] - moved


def newton_step(grad, smoothed, newton, volume):
    return pl.pallas_call(
        step_kernel,
        out_shape=jax.ShapeDtypeStruct(volume.shape, F32),
        in_specs=[VMEM] * 4,
        out_specs=VMEM,
        compiler_params=pltpu.CompilerParams(vmem_limit_bytes=SMALL),
    )(grad, smoothed, newton, volume)


def body(volume, projector, counts, atten, newton):
    depth, mats, pix = volume.shape
    owners, halves, groups, pairs, sides = (
        lax.axis_size(name) for name in ("x", "half", "row", "pair", "side")
    )
    slabs = pairs * sides
    views_all = projector.shape[0] * owners * halves * slabs
    rows, span = mats * depth, pix // owners
    vol = volume.transpose(1, 0, 2)
    x_all = lax.all_to_all(spread(vol, slabs), ("pair", "side"), 0, 0, tiled=True)
    x_all = x_all.reshape(slabs * rows, pix)
    near, binned, tiles = stage(atten, projector[0], counts[0], projector.shape[1] // 2)
    parts = project(tiles, x_all, near, projector[0], binned, owners, sides, slabs, mats)
    parts = parts.reshape(owners * sides, pairs, rows, span)
    parts = lax.all_to_all(parts, ("x", "side"), 0, 0, tiled=True)
    mine, edge = total_copies(parts, vol, float(views_all) ** (-0.5), owners * halves)
    ends = []
    for g in range(groups - 1):
        last, start = g * slabs + slabs - 1, (g + 1) * slabs
        ends += [(last, start), (start, last)]
    edge = lax.ppermute(edge, ("row", "pair", "side"), ends)
    mine = mine.reshape(owners * halves * pairs, rows, span)
    grad = lax.all_to_all(mine, ("x", "half", "pair"), 0, 0, tiled=True)
    grad = grad.reshape(owners, halves * pairs, rows, span)
    smoothed = smooth(vol, x_all, edge)
    updated = newton_step(grad, smoothed, newton.transpose(1, 2, 0, 3), vol)
    return updated.transpose(1, 0, 2)


def solution(mesh):
    views, groups, slabs = mesh.devices.shape
    mesh = jax.sharding.Mesh(
        mesh.devices.reshape(views // 2, 2, groups, slabs // 2, 2),
        ("x", "half", "row", "pair", "side"),
    )
    view, slice_axes = ("x", "half", "pair", "side"), ("row", "pair", "side")
    in_specs = (
        P(slice_axes, None, None),
        P(view, None, None),
        P(view, "row", None, None),
        P(),
        P(slice_axes, None, None, None),
    )
    out_specs = P(slice_axes, None, None)
    return jax.shard_map(body, mesh=mesh, in_specs=in_specs, out_specs=out_specs, check_vma=False)
```

```python
import functools

import jax
import jax.numpy as jnp
from jax import lax
from jax.experimental import pallas as pl
from jax.experimental.pallas import tpu as pltpu
from jax.sharding import PartitionSpec as P

PX = 1024
BF16 = jnp.bfloat16
F32 = jnp.float32
VMEM = pl.BlockSpec(memory_space=pltpu.VMEM)
SMEM = pl.BlockSpec(memory_space=pltpu.SMEM)
HBM = pl.BlockSpec(memory_space=pltpu.HBM)
SMALL = 8 * 1024 * 1024
MEDIUM = 49 * 1024 * 1024
LARGE = 49 * 1024 * 1024


def stage_kernel(
    vol_ref, atten_ref, counts_ref, proj_ref, own_ref, tiles_ref, binned_ref, near_ref, sem
):
    copy = pltpu.make_async_copy(proj_ref.at[: near_ref.shape[0]], near_ref, sem)
    copy.start()
    bins, mats = atten_ref.shape
    own_ref[...] = jnp.concatenate([vol_ref[m] for m in range(mats)], 0).astype(BF16)
    for b in range(bins):
        for m in range(mats):
            tiles_ref[b * mats + m] = jnp.full(tiles_ref.shape[1:], atten_ref[b, m], F32)
    for b in range(bins):
        binned_ref[b] = counts_ref[:, b, :].astype(F32)
    copy.wait()


def stage(volume, atten, counts, projector, held):
    slices, bins, cols = counts.shape
    mats, depth, pix = volume.shape
    return pl.pallas_call(
        stage_kernel,
        out_shape=[
            jax.ShapeDtypeStruct((mats * depth, pix), BF16),
            jax.ShapeDtypeStruct((atten.size, 8, 128), F32),
            jax.ShapeDtypeStruct((bins, slices, cols), F32),
            jax.ShapeDtypeStruct((held, pix), BF16),
        ],
        in_specs=[VMEM, SMEM, VMEM, HBM],
        out_specs=[VMEM] * 4,
        scratch_shapes=[pltpu.SemaphoreType.DMA(())],
        compiler_params=pltpu.CompilerParams(vmem_limit_bytes=LARGE),
    )(volume, atten, counts, projector)


def wide_tile(tile, wide):
    return jnp.concatenate([tile] * (wide // tile.shape[1]), 1)


def project_kernel(mats, bins, slabs, tiles_ref, x_ref, near_ref, proj_ref, counts_ref, out_ref, resid_ref, rest_ref, sems):
    rows, pix = x_ref.shape
    cols, held = proj_ref.shape[0], near_ref.shape[0]
    wide = 256
    copies = [
        pltpu.make_async_copy(
            proj_ref.at[at : at + wide], rest_ref.at[at - held : at - held + wide], sems.at[i]
        )
        for i, at in enumerate(range(held, cols, wide))
    ]
    for copy in copies:
        copy.start()
    per_slab = rows // slabs
    depth = per_slab // mats
    atten = [[wide_tile(tiles_ref[b * mats + m], wide) for m in range(mats)] for b in range(bins)]
    for at in range(0, cols, wide):
        if at >= held:
            copies[(at - held) // wide].wait()
        block = near_ref[at : at + wide] if at < held else rest_ref[at - held : at - held + wide]
        line = lax.dot_general(
            x_ref[...], block, (((1,), (1,)), ((), ())), preferred_element_type=F32
        )
        blocks = []
        for slab in range(slabs):
            lines = [line[slab * per_slab + m * depth :][:depth] for m in range(mats)]
            parts = [None] * mats
            for b in range(bins):
                power = atten[b][0] * lines[0]
                for m in range(1, mats):
                    power = power + atten[b][m] * lines[m]
                seen = counts_ref[b, slab * depth : (slab + 1) * depth, at : at + wide]
                diff = seen - jnp.exp(-power)
                for m in range(mats):
                    term = atten[b][m] * diff
                    parts[m] = term if parts[m] is None else parts[m] + term
            blocks += parts
        resid_ref[:, at : at + wide] = jnp.concatenate(blocks, 0).astype(BF16)
    owners, sides, _, _, span = out_ref.shape
    for owner in range(owners):
        own = slice(owner * span, (owner + 1) * span)
        back = jnp.dot(resid_ref[:, :held], near_ref[:, own], preferred_element_type=F32)
        back = back + jnp.dot(resid_ref[:, held:], rest_ref[:, own], preferred_element_type=F32)
        for slab in range(slabs):
            out_ref[owner, slab % sides, slab // sides] = back[
                slab * per_slab : (slab + 1) * per_slab
            ].astype(BF16)


def project(tiles, x_all, near, projector, counts, owners, sides, slabs, mats):
    rows, pix = x_all.shape
    cols = counts.shape[2]
    out = (owners, sides, slabs // sides, rows // slabs, pix // owners)
    return pl.pallas_call(
        functools.partial(project_kernel, mats, counts.shape[0], slabs),
        out_shape=jax.ShapeDtypeStruct(out, BF16),
        in_specs=[VMEM, VMEM, VMEM, HBM, VMEM],
        out_specs=VMEM,
        scratch_shapes=[
            pltpu.VMEM((rows, cols), BF16),
            pltpu.VMEM((cols - near.shape[0], pix), BF16),
            pltpu.SemaphoreType.DMA(((cols - near.shape[0]) // 256,)),
        ],
        compiler_params=pltpu.CompilerParams(vmem_limit_bytes=MEDIUM),
        cost_estimate=pl.CostEstimate(
            flops=4 * rows * cols * pix, bytes_accessed=2 * cols * pix, transcendentals=rows * cols
        ),
    )(tiles, x_all, near, projector, counts)


def next_pixel(field):
    column = lax.broadcasted_iota(jnp.int32, field.shape, 1) % PX
    return jnp.where(column == PX - 1, 0.0, pltpu.roll(field, field.shape[1] - 1, 1))


def next_row(field):
    return jnp.concatenate([field[:, PX:], jnp.zeros((field.shape[0], PX), F32)], 1)


def prev_pixel(flux):
    column = lax.broadcasted_iota(jnp.int32, flux.shape, 1) % PX
    return jnp.where(column == 0, 0.0, pltpu.roll(flux, 1, 1))


def prev_row(flux):
    return jnp.concatenate([jnp.zeros((flux.shape[0], PX), F32), flux[:, :-PX]], 1)


def slab_index():
    return lax.axis_index("pair") * lax.axis_size("side") + lax.axis_index("side")


def smooth_kernel(vol_ref, x_ref, edge_ref, out_ref):
    mats, depth, pix = vol_ref.shape
    slabs = x_ref.shape[0] // (mats * depth)
    slab = slab_index()
    first = jnp.logical_and(slab == 0, lax.axis_index("row") == 0)
    row = lax.broadcasted_iota(jnp.int32, (depth, pix), 0)
    vol, above, below = [], [], []
    for m in range(mats):
        vol.append(vol_ref[m])
        up = down = edge_ref[m : m + 1]
        for other in range(1, slabs):
            at = (other * mats + m) * depth
            up = jnp.where(slab == other - 1, x_ref[at : at + depth].astype(F32)[:1], up)
            at = ((other - 1) * mats + m) * depth
            down = jnp.where(slab == other, x_ref[at : at + depth].astype(F32)[-1:], down)
        above.append(jnp.where(row == depth - 1, up, pltpu.roll(vol[m], depth - 1, 0)))
        below.append(down)
    square = jnp.full((depth, pix), 0.25, F32)
    square_below = jnp.full((1, pix), 0.25, F32)
    diffs, steps = [], []
    for m in range(mats):
        dz, dy, dx = above[m] - vol[m], next_row(vol[m]) - vol[m], next_pixel(vol[m]) - vol[m]
        square = square + (dz * dz + dy * dy + dx * dx)
        diffs.append((dz, dy, dx))
        dz, dy, dx = vol[m][:1] - below[m], next_row(below[m]) - below[m], next_pixel(below[m]) - below[m]
        square_below = square_below + (dz * dz + dy * dy + dx * dx)
        steps.append(dz)
    scale = lax.rsqrt(square)
    scale_below = jnp.where(first, 0.0, lax.rsqrt(square_below))
    for m in range(mats):
        qz, qy, qx = (d * scale for d in diffs[m])
        prev_z = jnp.where(row == 0, steps[m] * scale_below, pltpu.roll(qz, 1, 0))
        out_ref[m] = prev_z - qz + (prev_row(qy) - qy) + (prev_pixel(qx) - qx)


def smooth(volume, x_all, edge):
    return pl.pallas_call(
        smooth_kernel,
        out_shape=jax.ShapeDtypeStruct(volume.shape, F32),
        in_specs=[VMEM, VMEM, VMEM],
        out_specs=VMEM,
        compiler_params=pltpu.CompilerParams(vmem_limit_bytes=SMALL),
        cost_estimate=pl.CostEstimate(
            flops=40 * volume.size, bytes_accessed=12 * volume.size, transcendentals=volume.size
        ),
    )(volume, x_all, edge)


def total_kernel(factor, part_ref, vol_ref, out_ref, edge_ref):
    total = jnp.sum(part_ref[...].astype(F32), axis=0) * factor
    total = total.astype(BF16)
    for copy in range(out_ref.shape[0]):
        out_ref[copy] = total
    slab = slab_index()
    for m in range(vol_ref.shape[0]):
        slab_m = vol_ref[m]
        edge_ref[m : m + 1] = jnp.where(slab == 0, slab_m[:1], slab_m[-1:])


def total_copies(parts, volume, factor, copies):
    mats, _, pix = volume.shape
    return pl.pallas_call(
        functools.partial(total_kernel, factor),
        out_shape=[
            jax.ShapeDtypeStruct((copies,) + parts.shape[1:], BF16),
            jax.ShapeDtypeStruct((mats, pix), F32),
        ],
        in_specs=[VMEM, VMEM],
        out_specs=[VMEM, VMEM],
        compiler_params=pltpu.CompilerParams(vmem_limit_bytes=SMALL),
    )(parts, volume)


def step_kernel(grad_ref, smooth_ref, newton_ref, vol_ref, out_ref):
    mats, depth, pix = vol_ref.shape
    owners, copies, _, span = grad_ref.shape
    for owner in range(owners):
        own = slice(owner * span, (owner + 1) * span)
        grad = grad_ref[owner, 0].astype(F32)
        for copy in range(1, copies):
            grad = grad + grad_ref[owner, copy].astype(F32)
        steps = [grad[k * depth : (k + 1) * depth] + 0.5 * smooth_ref[k, :, own] for k in range(mats)]
        for m in range(mats):
            moved = newton_ref[m, 0, :, own].astype(F32) * steps[0]
            for k in range(1, mats):
                moved = moved + newton_ref[m, k, :, own].astype(F32) * steps[k]
            out_ref[m, :, own] = vol_ref[m, :, own] - moved


def newton_step(grad, smoothed, newton, volume):
    return pl.pallas_call(
        step_kernel,
        out_shape=jax.ShapeDtypeStruct(volume.shape, F32),
        in_specs=[VMEM] * 4,
        out_specs=VMEM,
        compiler_params=pltpu.CompilerParams(vmem_limit_bytes=SMALL),
    )(grad, smoothed, newton, volume)


def body(volume, projector, counts, atten, newton):
    depth, mats, pix = volume.shape
    owners, halves, groups, pairs, sides = (
        lax.axis_size(name) for name in ("x", "half", "row", "pair", "side")
    )
    slabs = pairs * sides
    views_all = projector.shape[0] * owners * halves * slabs
    rows, span = mats * depth, pix // owners
    vol = volume.transpose(1, 0, 2)
    held = projector.shape[1] * 2 // 4
    own, tiles, binned, near = stage(vol, atten, counts[0], projector[0], held)
    x_all = lax.all_gather(own, ("pair", "side"), axis=0, tiled=True)
    parts = project(tiles, x_all, near, projector[0], binned, owners, sides, slabs, mats)
    parts = parts.reshape(owners * sides, pairs, rows, span)
    parts = lax.all_to_all(parts, ("x", "side"), 0, 0, tiled=True)
    mine, edge = total_copies(parts, vol, float(views_all) ** (-0.5), owners * halves)
    ends = []
    for g in range(groups - 1):
        last, start = g * slabs + slabs - 1, (g + 1) * slabs
        ends += [(last, start), (start, last)]
    edge = lax.ppermute(edge, ("row", "pair", "side"), ends)
    mine = mine.reshape(owners * halves * pairs, rows, span)
    grad = lax.all_to_all(mine, ("x", "half", "pair"), 0, 0, tiled=True)
    grad = grad.reshape(owners, halves * pairs, rows, span)
    smoothed = smooth(vol, x_all, edge)
    updated = newton_step(grad, smoothed, newton.transpose(1, 2, 0, 3), vol)
    return updated.transpose(1, 0, 2)


def solution(mesh):
    views, groups, slabs = mesh.devices.shape
    mesh = jax.sharding.Mesh(
        mesh.devices.reshape(views // 2, 2, groups, slabs // 2, 2),
        ("x", "half", "row", "pair", "side"),
    )
    view, slice_axes = ("x", "half", "pair", "side"), ("row", "pair", "side")
    in_specs = (
        P(slice_axes, None, None),
        P(view, None, None),
        P(view, "row", None, None),
        P(),
        P(slice_axes, None, None, None),
    )
    out_specs = P(slice_axes, None, None)
    return jax.shard_map(body, mesh=mesh, in_specs=in_specs, out_specs=out_specs, check_vma=False)
```

```python
import functools

import jax
import jax.numpy as jnp
from jax import lax
from jax.experimental import pallas as pl
from jax.experimental.pallas import tpu as pltpu
from jax.sharding import PartitionSpec as P

PX = 1024
BF16 = jnp.bfloat16
F32 = jnp.float32
VMEM = pl.BlockSpec(memory_space=pltpu.VMEM)
SMEM = pl.BlockSpec(memory_space=pltpu.SMEM)
HBM = pl.BlockSpec(memory_space=pltpu.HBM)
SMALL = 8 * 1024 * 1024
MEDIUM = 49 * 1024 * 1024
LARGE = 50 * 1024 * 1024
HUGE = 58 * 1024 * 1024


def spread_kernel(vol_ref, out_ref, near_ref, rounded_ref, sems):
    copy_in = pltpu.make_async_copy(vol_ref, near_ref, sems.at[0])
    copy_in.start()
    copy_in.wait()
    mats = near_ref.shape[0]
    rounded_ref[...] = jnp.concatenate([near_ref[m] for m in range(mats)], 0).astype(BF16)
    copies = [
        pltpu.make_async_copy(rounded_ref, out_ref.at[copy], sems.at[copy + 1])
        for copy in range(out_ref.shape[0])
    ]
    for copy in copies:
        copy.start()
    for copy in copies:
        copy.wait()


def spread(volume, copies):
    mats, depth, pix = volume.shape
    return pl.pallas_call(
        spread_kernel,
        out_shape=jax.ShapeDtypeStruct((copies, mats * depth, pix), BF16),
        in_specs=[HBM],
        out_specs=HBM,
        scratch_shapes=[
            pltpu.VMEM(volume.shape, F32),
            pltpu.VMEM((mats * depth, pix), BF16),
            pltpu.SemaphoreType.DMA((copies + 1,)),
        ],
        compiler_params=pltpu.CompilerParams(vmem_limit_bytes=HUGE),
    )(volume)


def stage_kernel(
    atten_ref, proj_ref, counts_ref, near_ref, binned_ref, tiles_ref, atten_near, counts_near, sems
):
    copy_atten = pltpu.make_async_copy(atten_ref, atten_near, sems.at[0])
    copy_counts = pltpu.make_async_copy(counts_ref, counts_near, sems.at[1])
    copy_proj = pltpu.make_async_copy(proj_ref.at[: near_ref.shape[0]], near_ref, sems.at[2])
    copy_atten.start()
    copy_counts.start()
    copy_proj.start()
    bins, mats = atten_ref.shape
    copy_atten.wait()
    for b in range(bins):
        for m in range(mats):
            tiles_ref[b * mats + m] = jnp.full(tiles_ref.shape[1:], atten_near[b, m], F32)
    copy_counts.wait()
    for b in range(bins):
        binned_ref[b] = counts_near[:, b, :].astype(F32)
    copy_proj.wait()


def stage(atten, projector, counts, held):
    slices, bins, cols = counts.shape
    return pl.pallas_call(
        stage_kernel,
        out_shape=[
            jax.ShapeDtypeStruct((held, projector.shape[1]), BF16),
            jax.ShapeDtypeStruct((bins, slices, cols), F32),
            jax.ShapeDtypeStruct((atten.size, 8, 128), F32),
        ],
        in_specs=[HBM, HBM, HBM],
        out_specs=[VMEM] * 3,
        scratch_shapes=[
            pltpu.SMEM(atten.shape, F32),
            pltpu.VMEM(counts.shape, BF16),
            pltpu.SemaphoreType.DMA((3,)),
        ],
        compiler_params=pltpu.CompilerParams(vmem_limit_bytes=LARGE),
        cost_estimate=pl.CostEstimate(flops=0, bytes_accessed=4 * projector.size, transcendentals=0),
    )(atten, projector, counts)


def wide_tile(tile, wide):
    return jnp.concatenate([tile] * (wide // tile.shape[1]), 1)


def project_kernel(mats, bins, slabs, tiles_ref, x_ref, near_ref, proj_ref, counts_ref, out_ref, resid_ref, rest_ref, sems):
    rows, pix = x_ref.shape
    cols, held = proj_ref.shape[0], near_ref.shape[0]
    wide = 512
    copies = [
        pltpu.make_async_copy(
            proj_ref.at[at : at + wide], rest_ref.at[at - held : at - held + wide], sems.at[i]
        )
        for i, at in enumerate(range(held, cols, wide))
    ]
    for copy in copies:
        copy.start()
    per_slab = rows // slabs
    depth = per_slab // mats
    atten = [[wide_tile(tiles_ref[b * mats + m], wide) for m in range(mats)] for b in range(bins)]
    for at in range(0, cols, wide):
        if at >= held:
            copies[(at - held) // wide].wait()
        block = near_ref[at : at + wide] if at < held else rest_ref[at - held : at - held + wide]
        line = lax.dot_general(
            x_ref[...], block, (((1,), (1,)), ((), ())), preferred_element_type=F32
        )
        blocks = []
        for slab in range(slabs):
            lines = [line[slab * per_slab + m * depth :][:depth] for m in range(mats)]
            parts = [None] * mats
            for b in range(bins):
                power = atten[b][0] * lines[0]
                for m in range(1, mats):
                    power = power + atten[b][m] * lines[m]
                seen = counts_ref[b, slab * depth : (slab + 1) * depth, at : at + wide]
                diff = seen - jnp.exp(-power)
                for m in range(mats):
                    term = atten[b][m] * diff
                    parts[m] = term if parts[m] is None else parts[m] + term
            blocks += parts
        resid_ref[:, at : at + wide] = jnp.concatenate(blocks, 0).astype(BF16)
    owners, sides, _, _, span = out_ref.shape
    for owner in range(owners):
        own = slice(owner * span, (owner + 1) * span)
        back = jnp.dot(resid_ref[:, :held], near_ref[:, own], preferred_element_type=F32)
        back = back + jnp.dot(resid_ref[:, held:], rest_ref[:, own], preferred_element_type=F32)
        for slab in range(slabs):
            out_ref[owner, slab % sides, slab // sides] = back[
                slab * per_slab : (slab + 1) * per_slab
            ].astype(BF16)


def project(tiles, x_all, near, projector, counts, owners, sides, slabs, mats):
    rows, pix = x_all.shape
    cols = counts.shape[2]
    out = (owners, sides, slabs // sides, rows // slabs, pix // owners)
    return pl.pallas_call(
        functools.partial(project_kernel, mats, counts.shape[0], slabs),
        out_shape=jax.ShapeDtypeStruct(out, BF16),
        in_specs=[VMEM, VMEM, VMEM, HBM, VMEM],
        out_specs=VMEM,
        scratch_shapes=[
            pltpu.VMEM((rows, cols), BF16),
            pltpu.VMEM((cols - near.shape[0], pix), BF16),
            pltpu.SemaphoreType.DMA(((cols - near.shape[0]) // 512,)),
        ],
        compiler_params=pltpu.CompilerParams(vmem_limit_bytes=MEDIUM),
        cost_estimate=pl.CostEstimate(
            flops=4 * rows * cols * pix, bytes_accessed=2 * cols * pix, transcendentals=rows * cols
        ),
    )(tiles, x_all, near, projector, counts)


def next_pixel(field):
    column = lax.broadcasted_iota(jnp.int32, field.shape, 1) % PX
    return jnp.where(column == PX - 1, 0.0, pltpu.roll(field, field.shape[1] - 1, 1))


def next_row(field):
    return jnp.concatenate([field[:, PX:], jnp.zeros((field.shape[0], PX), F32)], 1)


def prev_pixel(flux):
    column = lax.broadcasted_iota(jnp.int32, flux.shape, 1) % PX
    return jnp.where(column == 0, 0.0, pltpu.roll(flux, 1, 1))


def prev_row(flux):
    return jnp.concatenate([jnp.zeros((flux.shape[0], PX), F32), flux[:, :-PX]], 1)


def slab_index():
    return lax.axis_index("pair") * lax.axis_size("side") + lax.axis_index("side")


def smooth_kernel(vol_ref, x_ref, edge_ref, out_ref):
    mats, depth, pix = vol_ref.shape
    slabs = x_ref.shape[0] // (mats * depth)
    slab = slab_index()
    first = jnp.logical_and(slab == 0, lax.axis_index("row") == 0)
    row = lax.broadcasted_iota(jnp.int32, (depth, pix), 0)
    vol, above, below = [], [], []
    for m in range(mats):
        vol.append(vol_ref[m])
        up = down = edge_ref[m : m + 1]
        for other in range(1, slabs):
            at = (other * mats + m) * depth
            up = jnp.where(slab == other - 1, x_ref[at : at + depth].astype(F32)[:1], up)
            at = ((other - 1) * mats + m) * depth
            down = jnp.where(slab == other, x_ref[at : at + depth].astype(F32)[-1:], down)
        above.append(jnp.where(row == depth - 1, up, pltpu.roll(vol[m], depth - 1, 0)))
        below.append(down)
    square = jnp.full((depth, pix), 0.25, F32)
    square_below = jnp.full((1, pix), 0.25, F32)
    diffs, steps = [], []
    for m in range(mats):
        dz, dy, dx = above[m] - vol[m], next_row(vol[m]) - vol[m], next_pixel(vol[m]) - vol[m]
        square = square + (dz * dz + dy * dy + dx * dx)
        diffs.append((dz, dy, dx))
        dz, dy, dx = vol[m][:1] - below[m], next_row(below[m]) - below[m], next_pixel(below[m]) - below[m]
        square_below = square_below + (dz * dz + dy * dy + dx * dx)
        steps.append(dz)
    scale = lax.rsqrt(square)
    scale_below = jnp.where(first, 0.0, lax.rsqrt(square_below))
    for m in range(mats):
        qz, qy, qx = (d * scale for d in diffs[m])
        prev_z = jnp.where(row == 0, steps[m] * scale_below, pltpu.roll(qz, 1, 0))
        out_ref[m] = prev_z - qz + (prev_row(qy) - qy) + (prev_pixel(qx) - qx)


def smooth(volume, x_all, edge):
    return pl.pallas_call(
        smooth_kernel,
        out_shape=jax.ShapeDtypeStruct(volume.shape, F32),
        in_specs=[VMEM, VMEM, VMEM],
        out_specs=VMEM,
        compiler_params=pltpu.CompilerParams(vmem_limit_bytes=SMALL),
        cost_estimate=pl.CostEstimate(
            flops=40 * volume.size, bytes_accessed=12 * volume.size, transcendentals=volume.size
        ),
    )(volume, x_all, edge)


def total_kernel(factor, part_ref, vol_ref, out_ref, edge_ref):
    total = jnp.sum(part_ref[...].astype(F32), axis=0) * factor
    total = total.astype(BF16)
    for copy in range(out_ref.shape[0]):
        out_ref[copy] = total
    slab = slab_index()
    for m in range(vol_ref.shape[0]):
        slab_m = vol_ref[m]
        edge_ref[m : m + 1] = jnp.where(slab == 0, slab_m[:1], slab_m[-1:])


def total_copies(parts, volume, factor, copies):
    mats, _, pix = volume.shape
    return pl.pallas_call(
        functools.partial(total_kernel, factor),
        out_shape=[
            jax.ShapeDtypeStruct((copies,) + parts.shape[1:], BF16),
            jax.ShapeDtypeStruct((mats, pix), F32),
        ],
        in_specs=[VMEM, VMEM],
        out_specs=[VMEM, VMEM],
        compiler_params=pltpu.CompilerParams(vmem_limit_bytes=SMALL),
    )(parts, volume)


def step_kernel(grad_ref, smooth_ref, newton_ref, vol_ref, out_ref):
    mats, depth, pix = vol_ref.shape
    owners, copies, _, span = grad_ref.shape
    for owner in range(owners):
        own = slice(owner * span, (owner + 1) * span)
        grad = grad_ref[owner, 0].astype(F32)
        for copy in range(1, copies):
            grad = grad + grad_ref[owner, copy].astype(F32)
        steps = [grad[k * depth : (k + 1) * depth] + 0.5 * smooth_ref[k, :, own] for k in range(mats)]
        for m in range(mats):
            moved = newton_ref[m, 0, :, own].astype(F32) * steps[0]
            for k in range(1, mats):
                moved = moved + newton_ref[m, k, :, own].astype(F32) * steps[k]
            out_ref[m, :, own] = vol_ref[m, :, own] - moved


def newton_step(grad, smoothed, newton, volume):
    return pl.pallas_call(
        step_kernel,
        out_shape=jax.ShapeDtypeStruct(volume.shape, F32),
        in_specs=[VMEM] * 4,
        out_specs=VMEM,
        compiler_params=pltpu.CompilerParams(vmem_limit_bytes=SMALL),
    )(grad, smoothed, newton, volume)


def body(volume, projector, counts, atten, newton):
    depth, mats, pix = volume.shape
    owners, halves, groups, pairs, sides = (
        lax.axis_size(name) for name in ("x", "half", "row", "pair", "side")
    )
    slabs = pairs * sides
    views_all = projector.shape[0] * owners * halves * slabs
    rows, span = mats * depth, pix // owners
    vol = volume.transpose(1, 0, 2)
    x_all = lax.all_to_all(spread(vol, slabs), ("pair", "side"), 0, 0, tiled=True)
    x_all = x_all.reshape(slabs * rows, pix)
    near, binned, tiles = stage(atten, projector[0], counts[0], projector.shape[1] // 2)
    parts = project(tiles, x_all, near, projector[0], binned, owners, sides, slabs, mats)
    parts = parts.reshape(owners * sides, pairs, rows, span)
    parts = lax.all_to_all(parts, ("x", "side"), 0, 0, tiled=True)
    mine, edge = total_copies(parts, vol, float(views_all) ** (-0.5), owners * halves)
    ends = []
    for g in range(groups - 1):
        last, start = g * slabs + slabs - 1, (g + 1) * slabs
        ends += [(last, start), (start, last)]
    edge = lax.ppermute(edge, ("row", "pair", "side"), ends)
    mine = mine.reshape(owners * halves * pairs, rows, span)
    grad = lax.all_to_all(mine, ("x", "half", "pair"), 0, 0, tiled=True)
    grad = grad.reshape(owners, halves * pairs, rows, span)
    smoothed = smooth(vol, x_all, edge)
    updated = newton_step(grad, smoothed, newton.transpose(1, 2, 0, 3), vol)
    return updated.transpose(1, 0, 2)


def solution(mesh):
    views, groups, slabs = mesh.devices.shape
    mesh = jax.sharding.Mesh(
        mesh.devices.reshape(views // 2, 2, groups, slabs // 2, 2),
        ("x", "half", "row", "pair", "side"),
    )
    view, slice_axes = ("x", "half", "pair", "side"), ("row", "pair", "side")
    in_specs = (
        P(slice_axes, None, None),
        P(view, None, None),
        P(view, "row", None, None),
        P(),
        P(slice_axes, None, None, None),
    )
    out_specs = P(slice_axes, None, None)
    return jax.shard_map(body, mesh=mesh, in_specs=in_specs, out_specs=out_specs, check_vma=False)
```

```python
import functools

import jax
import jax.numpy as jnp
from jax import lax
from jax.experimental import pallas as pl
from jax.experimental.pallas import tpu as pltpu
from jax.sharding import PartitionSpec as P

PX = 1024
BF16 = jnp.bfloat16
F32 = jnp.float32
VMEM = pl.BlockSpec(memory_space=pltpu.VMEM)
SMEM = pl.BlockSpec(memory_space=pltpu.SMEM)
HBM = pl.BlockSpec(memory_space=pltpu.HBM)
SMALL = 8 * 1024 * 1024
MEDIUM = 49 * 1024 * 1024
LARGE = 50 * 1024 * 1024
HUGE = 58 * 1024 * 1024


def spread_kernel(vol_ref, out_ref, near_ref, rounded_ref, sems):
    copy_in = pltpu.make_async_copy(vol_ref, near_ref, sems.at[0])
    copy_in.start()
    copy_in.wait()
    mats = near_ref.shape[0]
    rounded_ref[...] = jnp.concatenate([near_ref[m] for m in range(mats)], 0).astype(BF16)
    copies = [
        pltpu.make_async_copy(rounded_ref, out_ref.at[copy], sems.at[copy + 1])
        for copy in range(out_ref.shape[0])
    ]
    for copy in copies:
        copy.start()
    for copy in copies:
        copy.wait()


def spread(volume, copies):
    mats, depth, pix = volume.shape
    return pl.pallas_call(
        spread_kernel,
        out_shape=jax.ShapeDtypeStruct((copies, mats * depth, pix), BF16),
        in_specs=[HBM],
        out_specs=HBM,
        scratch_shapes=[
            pltpu.VMEM(volume.shape, F32),
            pltpu.VMEM((mats * depth, pix), BF16),
            pltpu.SemaphoreType.DMA((copies + 1,)),
        ],
        compiler_params=pltpu.CompilerParams(vmem_limit_bytes=HUGE),
    )(volume)


def stage_kernel(
    atten_ref, proj_ref, counts_ref, near_ref, binned_ref, tiles_ref, atten_near, counts_near, sems
):
    copy_atten = pltpu.make_async_copy(atten_ref, atten_near, sems.at[0])
    copy_counts = pltpu.make_async_copy(counts_ref, counts_near, sems.at[1])
    copy_proj = pltpu.make_async_copy(proj_ref.at[: near_ref.shape[0]], near_ref, sems.at[2])
    copy_atten.start()
    copy_counts.start()
    copy_proj.start()
    bins, mats = atten_ref.shape
    copy_atten.wait()
    for b in range(bins):
        for m in range(mats):
            tiles_ref[b * mats + m] = jnp.full(tiles_ref.shape[1:], atten_near[b, m], F32)
    copy_counts.wait()
    for b in range(bins):
        binned_ref[b] = counts_near[:, b, :].astype(F32)
    copy_proj.wait()


def stage(atten, projector, counts, held):
    slices, bins, cols = counts.shape
    return pl.pallas_call(
        stage_kernel,
        out_shape=[
            jax.ShapeDtypeStruct((held, projector.shape[1]), BF16),
            jax.ShapeDtypeStruct((bins, slices, cols), F32),
            jax.ShapeDtypeStruct((atten.size, 8, 128), F32),
        ],
        in_specs=[HBM, HBM, HBM],
        out_specs=[VMEM] * 3,
        scratch_shapes=[
            pltpu.SMEM(atten.shape, F32),
            pltpu.VMEM(counts.shape, BF16),
            pltpu.SemaphoreType.DMA((3,)),
        ],
        compiler_params=pltpu.CompilerParams(vmem_limit_bytes=LARGE),
        cost_estimate=pl.CostEstimate(flops=0, bytes_accessed=4 * projector.size, transcendentals=0),
    )(atten, projector, counts)


def wide_tile(tile, wide):
    return jnp.concatenate([tile] * (wide // tile.shape[1]), 1)


def project_kernel(mats, bins, slabs, tiles_ref, x_ref, near_ref, proj_ref, counts_ref, out_ref, resid_ref, rest_ref, sems):
    rows, pix = x_ref.shape
    cols, held = proj_ref.shape[0], near_ref.shape[0]
    wide = 512
    copies = [
        pltpu.make_async_copy(
            proj_ref.at[at : at + wide], rest_ref.at[at - held : at - held + wide], sems.at[i]
        )
        for i, at in enumerate(range(held, cols, wide))
    ]
    for copy in copies:
        copy.start()
    per_slab = rows // slabs
    depth = per_slab // mats
    atten = [[wide_tile(tiles_ref[b * mats + m], wide) for m in range(mats)] for b in range(bins)]
    for at in range(0, cols, wide):
        if at >= held:
            copies[(at - held) // wide].wait()
        block = near_ref[at : at + wide] if at < held else rest_ref[at - held : at - held + wide]
        line = lax.dot_general(
            x_ref[...], block, (((1,), (1,)), ((), ())), preferred_element_type=F32
        )
        blocks = []
        for slab in range(slabs):
            lines = [line[slab * per_slab + m * depth :][:depth] for m in range(mats)]
            parts = [None] * mats
            for b in range(bins):
                power = atten[b][0] * lines[0]
                for m in range(1, mats):
                    power = power + atten[b][m] * lines[m]
                seen = counts_ref[b, slab * depth : (slab + 1) * depth, at : at + wide]
                diff = seen - jnp.exp(-power)
                for m in range(mats):
                    term = atten[b][m] * diff
                    parts[m] = term if parts[m] is None else parts[m] + term
            blocks += parts
        resid_ref[:, at : at + wide] = jnp.concatenate(blocks, 0).astype(BF16)
    owners, _, sides, _, span = out_ref.shape
    for owner in range(owners):
        own = slice(owner * span, (owner + 1) * span)
        back = jnp.dot(resid_ref[:, :held], near_ref[:, own], preferred_element_type=F32)
        back = back + jnp.dot(resid_ref[:, held:], rest_ref[:, own], preferred_element_type=F32)
        for slab in range(slabs):
            out_ref[owner, slab // sides, slab % sides] = back[
                slab * per_slab : (slab + 1) * per_slab
            ].astype(BF16)


def project(tiles, x_all, near, projector, counts, owners, sides, slabs, mats):
    rows, pix = x_all.shape
    cols = counts.shape[2]
    out = (owners, slabs // sides, sides, rows // slabs, pix // owners)
    return pl.pallas_call(
        functools.partial(project_kernel, mats, counts.shape[0], slabs),
        out_shape=jax.ShapeDtypeStruct(out, BF16),
        in_specs=[VMEM, VMEM, VMEM, HBM, VMEM],
        out_specs=VMEM,
        scratch_shapes=[
            pltpu.VMEM((rows, cols), BF16),
            pltpu.VMEM((cols - near.shape[0], pix), BF16),
            pltpu.SemaphoreType.DMA(((cols - near.shape[0]) // 512,)),
        ],
        compiler_params=pltpu.CompilerParams(vmem_limit_bytes=MEDIUM),
        cost_estimate=pl.CostEstimate(
            flops=4 * rows * cols * pix, bytes_accessed=2 * cols * pix, transcendentals=rows * cols
        ),
    )(tiles, x_all, near, projector, counts)


def next_pixel(field):
    column = lax.broadcasted_iota(jnp.int32, field.shape, 1) % PX
    return jnp.where(column == PX - 1, 0.0, pltpu.roll(field, field.shape[1] - 1, 1))


def next_row(field):
    return jnp.concatenate([field[:, PX:], jnp.zeros((field.shape[0], PX), F32)], 1)


def prev_pixel(flux):
    column = lax.broadcasted_iota(jnp.int32, flux.shape, 1) % PX
    return jnp.where(column == 0, 0.0, pltpu.roll(flux, 1, 1))


def prev_row(flux):
    return jnp.concatenate([jnp.zeros((flux.shape[0], PX), F32), flux[:, :-PX]], 1)


def slab_index():
    return lax.axis_index("pair") * lax.axis_size("side") + lax.axis_index("side")


def smooth_kernel(vol_ref, x_ref, edge_ref, out_ref):
    mats, depth, pix = vol_ref.shape
    slabs = x_ref.shape[0] // (mats * depth)
    slab = slab_index()
    first = jnp.logical_and(slab == 0, lax.axis_index("row") == 0)
    row = lax.broadcasted_iota(jnp.int32, (depth, pix), 0)
    vol, above, below = [], [], []
    for m in range(mats):
        vol.append(vol_ref[m])
        up = down = edge_ref[m : m + 1]
        for other in range(1, slabs):
            at = (other * mats + m) * depth
            up = jnp.where(slab == other - 1, x_ref[at : at + depth].astype(F32)[:1], up)
            at = ((other - 1) * mats + m) * depth
            down = jnp.where(slab == other, x_ref[at : at + depth].astype(F32)[-1:], down)
        above.append(jnp.where(row == depth - 1, up, pltpu.roll(vol[m], depth - 1, 0)))
        below.append(down)
    square = jnp.full((depth, pix), 0.25, F32)
    square_below = jnp.full((1, pix), 0.25, F32)
    diffs, steps = [], []
    for m in range(mats):
        dz, dy, dx = above[m] - vol[m], next_row(vol[m]) - vol[m], next_pixel(vol[m]) - vol[m]
        square = square + (dz * dz + dy * dy + dx * dx)
        diffs.append((dz, dy, dx))
        dz, dy, dx = vol[m][:1] - below[m], next_row(below[m]) - below[m], next_pixel(below[m]) - below[m]
        square_below = square_below + (dz * dz + dy * dy + dx * dx)
        steps.append(dz)
    scale = lax.rsqrt(square)
    scale_below = jnp.where(first, 0.0, lax.rsqrt(square_below))
    for m in range(mats):
        qz, qy, qx = (d * scale for d in diffs[m])
        prev_z = jnp.where(row == 0, steps[m] * scale_below, pltpu.roll(qz, 1, 0))
        out_ref[m] = prev_z - qz + (prev_row(qy) - qy) + (prev_pixel(qx) - qx)


def smooth(volume, x_all, edge):
    return pl.pallas_call(
        smooth_kernel,
        out_shape=jax.ShapeDtypeStruct(volume.shape, F32),
        in_specs=[VMEM, VMEM, VMEM],
        out_specs=VMEM,
        compiler_params=pltpu.CompilerParams(vmem_limit_bytes=SMALL),
        cost_estimate=pl.CostEstimate(
            flops=40 * volume.size, bytes_accessed=12 * volume.size, transcendentals=volume.size
        ),
    )(volume, x_all, edge)


def total_kernel(factor, part_ref, vol_ref, out_ref, edge_ref):
    total = jnp.sum(part_ref[...].astype(F32), axis=0) * factor
    total = total.astype(BF16)
    for copy in range(out_ref.shape[0]):
        out_ref[copy] = total
    slab = slab_index()
    for m in range(vol_ref.shape[0]):
        slab_m = vol_ref[m]
        edge_ref[m : m + 1] = jnp.where(slab == 0, slab_m[:1], slab_m[-1:])


def total_copies(parts, volume, factor, copies):
    mats, _, pix = volume.shape
    return pl.pallas_call(
        functools.partial(total_kernel, factor),
        out_shape=[
            jax.ShapeDtypeStruct((copies,) + parts.shape[1:], BF16),
            jax.ShapeDtypeStruct((mats, pix), F32),
        ],
        in_specs=[VMEM, VMEM],
        out_specs=[VMEM, VMEM],
        compiler_params=pltpu.CompilerParams(vmem_limit_bytes=SMALL),
    )(parts, volume)


def step_kernel(grad_ref, smooth_ref, newton_ref, vol_ref, out_ref):
    mats, depth, pix = vol_ref.shape
    owners, copies, _, span = grad_ref.shape
    for owner in range(owners):
        own = slice(owner * span, (owner + 1) * span)
        grad = grad_ref[owner, 0].astype(F32)
        for copy in range(1, copies):
            grad = grad + grad_ref[owner, copy].astype(F32)
        steps = [grad[k * depth : (k + 1) * depth] + 0.5 * smooth_ref[k, :, own] for k in range(mats)]
        for m in range(mats):
            moved = newton_ref[m, 0, :, own].astype(F32) * steps[0]
            for k in range(1, mats):
                moved = moved + newton_ref[m, k, :, own].astype(F32) * steps[k]
            out_ref[m, :, own] = vol_ref[m, :, own] - moved


def newton_step(grad, smoothed, newton, volume):
    return pl.pallas_call(
        step_kernel,
        out_shape=jax.ShapeDtypeStruct(volume.shape, F32),
        in_specs=[VMEM] * 4,
        out_specs=VMEM,
        compiler_params=pltpu.CompilerParams(vmem_limit_bytes=SMALL),
    )(grad, smoothed, newton, volume)


def body(volume, projector, counts, atten, newton):
    depth, mats, pix = volume.shape
    owners, halves, groups, pairs, sides = (
        lax.axis_size(name) for name in ("x", "half", "row", "pair", "side")
    )
    slabs = pairs * sides
    views_all = projector.shape[0] * owners * halves * slabs
    rows, span = mats * depth, pix // owners
    vol = volume.transpose(1, 0, 2)
    x_all = lax.all_to_all(spread(vol, slabs), ("pair", "side"), 0, 0, tiled=True)
    x_all = x_all.reshape(slabs * rows, pix)
    near, binned, tiles = stage(atten, projector[0], counts[0], projector.shape[1] // 2)
    parts = project(tiles, x_all, near, projector[0], binned, owners, sides, slabs, mats)
    parts = parts.reshape(owners * slabs, rows, span)
    parts = lax.all_to_all(parts, ("x", "pair", "side"), 0, 0, tiled=True)
    mine, edge = total_copies(parts, vol, float(views_all) ** (-0.5), owners * halves)
    ends = []
    for g in range(groups - 1):
        last, start = g * slabs + slabs - 1, (g + 1) * slabs
        ends += [(last, start), (start, last)]
    edge = lax.ppermute(edge, ("row", "pair", "side"), ends)
    grad = lax.all_to_all(mine, ("x", "half"), 0, 0, tiled=True)
    grad = grad.reshape(owners, halves, rows, span)
    smoothed = smooth(vol, x_all, edge)
    updated = newton_step(grad, smoothed, newton.transpose(1, 2, 0, 3), vol)
    return updated.transpose(1, 0, 2)


def solution(mesh):
    views, groups, slabs = mesh.devices.shape
    mesh = jax.sharding.Mesh(
        mesh.devices.reshape(views // 2, 2, groups, slabs // 2, 2),
        ("x", "half", "row", "pair", "side"),
    )
    view, slice_axes = ("x", "half", "pair", "side"), ("row", "pair", "side")
    in_specs = (
        P(slice_axes, None, None),
        P(view, None, None),
        P(view, "row", None, None),
        P(),
        P(slice_axes, None, None, None),
    )
    out_specs = P(slice_axes, None, None)
    return jax.shard_map(body, mesh=mesh, in_specs=in_specs, out_specs=out_specs, check_vma=False)
```

```python
import functools

import jax
import jax.numpy as jnp
from jax import lax
from jax.experimental import pallas as pl
from jax.experimental.pallas import tpu as pltpu
from jax.sharding import PartitionSpec as P

PX = 1024
BF16 = jnp.bfloat16
F32 = jnp.float32
VMEM = pl.BlockSpec(memory_space=pltpu.VMEM)
SMEM = pl.BlockSpec(memory_space=pltpu.SMEM)
HBM = pl.BlockSpec(memory_space=pltpu.HBM)
SMALL = 8 * 1024 * 1024
MEDIUM = 49 * 1024 * 1024
LARGE = 50 * 1024 * 1024
HUGE = 58 * 1024 * 1024


def spread_kernel(vol_ref, out_ref):
    mats = vol_ref.shape[0]
    rounded = jnp.concatenate([vol_ref[m] for m in range(mats)], 0).astype(BF16)
    for copy in range(out_ref.shape[0]):
        out_ref[copy] = rounded


def spread(volume, copies):
    mats, depth, pix = volume.shape
    return pl.pallas_call(
        spread_kernel,
        out_shape=jax.ShapeDtypeStruct((copies, mats * depth, pix), BF16),
        in_specs=[VMEM],
        out_specs=VMEM,
        compiler_params=pltpu.CompilerParams(vmem_limit_bytes=HUGE),
    )(volume)


def stage_kernel(atten_ref, proj_ref, counts_ref, near_ref, binned_ref, tiles_ref, sem):
    copy = pltpu.make_async_copy(proj_ref.at[: near_ref.shape[0]], near_ref, sem)
    copy.start()
    bins, mats = atten_ref.shape
    for b in range(bins):
        for m in range(mats):
            tiles_ref[b * mats + m] = jnp.full(tiles_ref.shape[1:], atten_ref[b, m], F32)
    for b in range(bins):
        binned_ref[b] = counts_ref[:, b, :].astype(F32)
    copy.wait()


def stage(atten, projector, counts, held):
    slices, bins, cols = counts.shape
    return pl.pallas_call(
        stage_kernel,
        out_shape=[
            jax.ShapeDtypeStruct((held, projector.shape[1]), BF16),
            jax.ShapeDtypeStruct((bins, slices, cols), F32),
            jax.ShapeDtypeStruct((atten.size, 8, 128), F32),
        ],
        in_specs=[SMEM, HBM, VMEM],
        out_specs=[VMEM] * 3,
        scratch_shapes=[pltpu.SemaphoreType.DMA(())],
        compiler_params=pltpu.CompilerParams(vmem_limit_bytes=LARGE),
        cost_estimate=pl.CostEstimate(flops=0, bytes_accessed=4 * projector.size, transcendentals=0),
    )(atten, projector, counts)


def wide_tile(tile, wide):
    return jnp.concatenate([tile] * (wide // tile.shape[1]), 1)


def project_kernel(mats, bins, slabs, tiles_ref, x_ref, near_ref, proj_ref, counts_ref, out_ref, resid_ref, rest_ref, sems):
    rows, pix = x_ref.shape
    cols, held = proj_ref.shape[0], near_ref.shape[0]
    wide = 512
    copies = [
        pltpu.make_async_copy(
            proj_ref.at[at : at + wide], rest_ref.at[at - held : at - held + wide], sems.at[i]
        )
        for i, at in enumerate(range(held, cols, wide))
    ]
    for copy in copies:
        copy.start()
    per_slab = rows // slabs
    depth = per_slab // mats
    atten = [[wide_tile(tiles_ref[b * mats + m], wide) for m in range(mats)] for b in range(bins)]
    for at in range(0, cols, wide):
        if at >= held:
            copies[(at - held) // wide].wait()
        block = near_ref[at : at + wide] if at < held else rest_ref[at - held : at - held + wide]
        line = lax.dot_general(
            x_ref[...], block, (((1,), (1,)), ((), ())), preferred_element_type=F32
        )
        blocks = []
        for slab in range(slabs):
            lines = [line[slab * per_slab + m * depth :][:depth] for m in range(mats)]
            parts = [None] * mats
            for b in range(bins):
                power = atten[b][0] * lines[0]
                for m in range(1, mats):
                    power = power + atten[b][m] * lines[m]
                seen = counts_ref[b, slab * depth : (slab + 1) * depth, at : at + wide]
                diff = seen - jnp.exp(-power)
                for m in range(mats):
                    term = atten[b][m] * diff
                    parts[m] = term if parts[m] is None else parts[m] + term
            blocks += parts
        resid_ref[:, at : at + wide] = jnp.concatenate(blocks, 0).astype(BF16)
    owners, sides, _, _, span = out_ref.shape
    for owner in range(owners):
        own = slice(owner * span, (owner + 1) * span)
        back = jnp.dot(resid_ref[:, :held], near_ref[:, own], preferred_element_type=F32)
        back = back + jnp.dot(resid_ref[:, held:], rest_ref[:, own], preferred_element_type=F32)
        for slab in range(slabs):
            out_ref[owner, slab % sides, slab // sides] = back[
                slab * per_slab : (slab + 1) * per_slab
            ].astype(BF16)


def project(tiles, x_all, near, projector, counts, owners, sides, slabs, mats):
    rows, pix = x_all.shape
    cols = counts.shape[2]
    out = (owners, sides, slabs // sides, rows // slabs, pix // owners)
    return pl.pallas_call(
        functools.partial(project_kernel, mats, counts.shape[0], slabs),
        out_shape=jax.ShapeDtypeStruct(out, BF16),
        in_specs=[VMEM, VMEM, VMEM, HBM, VMEM],
        out_specs=VMEM,
        scratch_shapes=[
            pltpu.VMEM((rows, cols), BF16),
            pltpu.VMEM((cols - near.shape[0], pix), BF16),
            pltpu.SemaphoreType.DMA(((cols - near.shape[0]) // 512,)),
        ],
        compiler_params=pltpu.CompilerParams(vmem_limit_bytes=MEDIUM),
        cost_estimate=pl.CostEstimate(
            flops=4 * rows * cols * pix, bytes_accessed=2 * cols * pix, transcendentals=rows * cols
        ),
    )(tiles, x_all, near, projector, counts)


def next_pixel(field):
    column = lax.broadcasted_iota(jnp.int32, field.shape, 1) % PX
    return jnp.where(column == PX - 1, 0.0, pltpu.roll(field, field.shape[1] - 1, 1))


def next_row(field):
    return jnp.concatenate([field[:, PX:], jnp.zeros((field.shape[0], PX), F32)], 1)


def prev_pixel(flux):
    column = lax.broadcasted_iota(jnp.int32, flux.shape, 1) % PX
    return jnp.where(column == 0, 0.0, pltpu.roll(flux, 1, 1))


def prev_row(flux):
    return jnp.concatenate([jnp.zeros((flux.shape[0], PX), F32), flux[:, :-PX]], 1)


def slab_index():
    return lax.axis_index("pair") * lax.axis_size("side") + lax.axis_index("side")


def smooth_kernel(vol_ref, x_ref, edge_ref, out_ref):
    mats, depth, pix = vol_ref.shape
    slabs = x_ref.shape[0] // (mats * depth)
    slab = slab_index()
    first = jnp.logical_and(slab == 0, lax.axis_index("row") == 0)
    row = lax.broadcasted_iota(jnp.int32, (depth, pix), 0)
    vol, above, below = [], [], []
    for m in range(mats):
        vol.append(vol_ref[m])
        up = down = edge_ref[m : m + 1]
        for other in range(1, slabs):
            at = (other * mats + m) * depth
            up = jnp.where(slab == other - 1, x_ref[at : at + depth].astype(F32)[:1], up)
            at = ((other - 1) * mats + m) * depth
            down = jnp.where(slab == other, x_ref[at : at + depth].astype(F32)[-1:], down)
        above.append(jnp.where(row == depth - 1, up, pltpu.roll(vol[m], depth - 1, 0)))
        below.append(down)
    square = jnp.full((depth, pix), 0.25, F32)
    square_below = jnp.full((1, pix), 0.25, F32)
    diffs, steps = [], []
    for m in range(mats):
        dz, dy, dx = above[m] - vol[m], next_row(vol[m]) - vol[m], next_pixel(vol[m]) - vol[m]
        square = square + (dz * dz + dy * dy + dx * dx)
        diffs.append((dz, dy, dx))
        dz, dy, dx = vol[m][:1] - below[m], next_row(below[m]) - below[m], next_pixel(below[m]) - below[m]
        square_below = square_below + (dz * dz + dy * dy + dx * dx)
        steps.append(dz)
    scale = lax.rsqrt(square)
    scale_below = jnp.where(first, 0.0, lax.rsqrt(square_below))
    for m in range(mats):
        qz, qy, qx = (d * scale for d in diffs[m])
        prev_z = jnp.where(row == 0, steps[m] * scale_below, pltpu.roll(qz, 1, 0))
        out_ref[m] = prev_z - qz + (prev_row(qy) - qy) + (prev_pixel(qx) - qx)


def smooth(volume, x_all, edge):
    return pl.pallas_call(
        smooth_kernel,
        out_shape=jax.ShapeDtypeStruct(volume.shape, F32),
        in_specs=[VMEM, VMEM, VMEM],
        out_specs=VMEM,
        compiler_params=pltpu.CompilerParams(vmem_limit_bytes=SMALL),
        cost_estimate=pl.CostEstimate(
            flops=40 * volume.size, bytes_accessed=12 * volume.size, transcendentals=volume.size
        ),
    )(volume, x_all, edge)


def total_kernel(factor, part_ref, vol_ref, out_ref, edge_ref):
    total = jnp.sum(part_ref[...].astype(F32), axis=0) * factor
    total = total.astype(BF16)
    for copy in range(out_ref.shape[0]):
        out_ref[copy] = total
    slab = slab_index()
    for m in range(vol_ref.shape[0]):
        slab_m = vol_ref[m]
        edge_ref[m : m + 1] = jnp.where(slab == 0, slab_m[:1], slab_m[-1:])


def total_copies(parts, volume, factor, copies):
    mats, _, pix = volume.shape
    return pl.pallas_call(
        functools.partial(total_kernel, factor),
        out_shape=[
            jax.ShapeDtypeStruct((copies,) + parts.shape[1:], BF16),
            jax.ShapeDtypeStruct((mats, pix), F32),
        ],
        in_specs=[VMEM, VMEM],
        out_specs=[VMEM, VMEM],
        compiler_params=pltpu.CompilerParams(vmem_limit_bytes=SMALL),
    )(parts, volume)


def step_kernel(grad_ref, smooth_ref, newton_ref, vol_ref, out_ref):
    mats, depth, pix = vol_ref.shape
    owners, copies, _, span = grad_ref.shape
    for owner in range(owners):
        own = slice(owner * span, (owner + 1) * span)
        grad = grad_ref[owner, 0].astype(F32)
        for copy in range(1, copies):
            grad = grad + grad_ref[owner, copy].astype(F32)
        steps = [grad[k * depth : (k + 1) * depth] + 0.5 * smooth_ref[k, :, own] for k in range(mats)]
        for m in range(mats):
            moved = newton_ref[m, 0, :, own].astype(F32) * steps[0]
            for k in range(1, mats):
                moved = moved + newton_ref[m, k, :, own].astype(F32) * steps[k]
            out_ref[m, :, own] = vol_ref[m, :, own] - moved


def newton_step(grad, smoothed, newton, volume):
    return pl.pallas_call(
        step_kernel,
        out_shape=jax.ShapeDtypeStruct(volume.shape, F32),
        in_specs=[VMEM] * 4,
        out_specs=VMEM,
        compiler_params=pltpu.CompilerParams(vmem_limit_bytes=SMALL),
    )(grad, smoothed, newton, volume)


def body(volume, projector, counts, atten, newton):
    depth, mats, pix = volume.shape
    owners, halves, groups, pairs, sides = (
        lax.axis_size(name) for name in ("x", "half", "row", "pair", "side")
    )
    slabs = pairs * sides
    views_all = projector.shape[0] * owners * halves * slabs
    rows, span = mats * depth, pix // owners
    vol = volume.transpose(1, 0, 2)
    x_all = lax.all_to_all(spread(vol, slabs), ("pair", "side"), 0, 0, tiled=True)
    x_all = x_all.reshape(slabs * rows, pix)
    near, binned, tiles = stage(atten, projector[0], counts[0], projector.shape[1] // 2)
    parts = project(tiles, x_all, near, projector[0], binned, owners, sides, slabs, mats)
    parts = parts.reshape(owners * sides, pairs, rows, span)
    parts = lax.all_to_all(parts, ("x", "side"), 0, 0, tiled=True)
    mine, edge = total_copies(parts, vol, float(views_all) ** (-0.5), owners * halves)
    ends = []
    for g in range(groups - 1):
        last, start = g * slabs + slabs - 1, (g + 1) * slabs
        ends += [(last, start), (start, last)]
    edge = lax.ppermute(edge, ("row", "pair", "side"), ends)
    mine = mine.reshape(owners * halves * pairs, rows, span)
    grad = lax.all_to_all(mine, ("x", "half", "pair"), 0, 0, tiled=True)
    grad = grad.reshape(owners, halves * pairs, rows, span)
    smoothed = smooth(vol, x_all, edge)
    updated = newton_step(grad, smoothed, newton.transpose(1, 2, 0, 3), vol)
    return updated.transpose(1, 0, 2)


def solution(mesh):
    views, groups, slabs = mesh.devices.shape
    mesh = jax.sharding.Mesh(
        mesh.devices.reshape(views // 2, 2, groups, slabs // 2, 2),
        ("x", "half", "row", "pair", "side"),
    )
    view, slice_axes = ("x", "half", "pair", "side"), ("row", "pair", "side")
    in_specs = (
        P(slice_axes, None, None),
        P(view, None, None),
        P(view, "row", None, None),
        P(),
        P(slice_axes, None, None, None),
    )
    out_specs = P(slice_axes, None, None)
    return jax.shard_map(body, mesh=mesh, in_specs=in_specs, out_specs=out_specs, check_vma=False)
```

```python
import functools

import jax
import jax.numpy as jnp
from jax import lax
from jax.experimental import pallas as pl
from jax.experimental.pallas import tpu as pltpu
from jax.sharding import PartitionSpec as P

PX = 1024
BF16 = jnp.bfloat16
F32 = jnp.float32
VMEM = pl.BlockSpec(memory_space=pltpu.VMEM)
SMEM = pl.BlockSpec(memory_space=pltpu.SMEM)
HBM = pl.BlockSpec(memory_space=pltpu.HBM)
SMALL = 8 * 1024 * 1024
MEDIUM = 49 * 1024 * 1024
LARGE = 50 * 1024 * 1024
HUGE = 58 * 1024 * 1024


def spread_kernel(vol_ref, out_ref):
    mats = vol_ref.shape[0]
    rounded = jnp.concatenate([vol_ref[m] for m in range(mats)], 0).astype(BF16)
    for copy in range(out_ref.shape[0]):
        out_ref[copy] = rounded


def spread(volume, copies):
    mats, depth, pix = volume.shape
    return pl.pallas_call(
        spread_kernel,
        out_shape=jax.ShapeDtypeStruct((copies, mats * depth, pix), BF16),
        in_specs=[VMEM],
        out_specs=VMEM,
        compiler_params=pltpu.CompilerParams(vmem_limit_bytes=HUGE),
    )(volume)


def stage_kernel(atten_ref, proj_ref, counts_ref, near_ref, binned_ref, tiles_ref, sem):
    copy = pltpu.make_async_copy(proj_ref.at[: near_ref.shape[0]], near_ref, sem)
    copy.start()
    bins, mats = atten_ref.shape
    for b in range(bins):
        for m in range(mats):
            tiles_ref[b * mats + m] = jnp.full(tiles_ref.shape[1:], atten_ref[b, m], F32)
    for b in range(bins):
        binned_ref[b] = counts_ref[:, b, :].astype(F32)
    copy.wait()


def stage(atten, projector, counts, held):
    slices, bins, cols = counts.shape
    return pl.pallas_call(
        stage_kernel,
        out_shape=[
            jax.ShapeDtypeStruct((held, projector.shape[1]), BF16),
            jax.ShapeDtypeStruct((bins, slices, cols), F32),
            jax.ShapeDtypeStruct((atten.size, 8, 128), F32),
        ],
        in_specs=[SMEM, HBM, VMEM],
        out_specs=[VMEM] * 3,
        scratch_shapes=[pltpu.SemaphoreType.DMA(())],
        compiler_params=pltpu.CompilerParams(vmem_limit_bytes=LARGE),
        cost_estimate=pl.CostEstimate(flops=0, bytes_accessed=4 * projector.size, transcendentals=0),
    )(atten, projector, counts)


def wide_tile(tile, wide):
    return jnp.concatenate([tile] * (wide // tile.shape[1]), 1)


def project_kernel(mats, bins, slabs, tiles_ref, x_ref, near_ref, proj_ref, counts_ref, out_ref, resid_ref, rest_ref, sems):
    rows, pix = x_ref.shape
    cols, held = proj_ref.shape[0], near_ref.shape[0]
    wide = 512
    copies = [
        pltpu.make_async_copy(
            proj_ref.at[at : at + wide], rest_ref.at[at - held : at - held + wide], sems.at[i]
        )
        for i, at in enumerate(range(held, cols, wide))
    ]
    for copy in copies:
        copy.start()
    per_slab = rows // slabs
    depth = per_slab // mats
    atten = [[wide_tile(tiles_ref[b * mats + m], wide) for m in range(mats)] for b in range(bins)]
    for at in range(0, cols, wide):
        if at >= held:
            copies[(at - held) // wide].wait()
        block = near_ref[at : at + wide] if at < held else rest_ref[at - held : at - held + wide]
        line = lax.dot_general(
            x_ref[...], block, (((1,), (1,)), ((), ())), preferred_element_type=F32
        )
        blocks = []
        for slab in range(slabs):
            lines = [line[slab * per_slab + m * depth :][:depth] for m in range(mats)]
            parts = [None] * mats
            for b in range(bins):
                power = atten[b][0] * lines[0]
                for m in range(1, mats):
                    power = power + atten[b][m] * lines[m]
                seen = counts_ref[b, slab * depth : (slab + 1) * depth, at : at + wide]
                diff = seen - jnp.exp(-power)
                for m in range(mats):
                    term = atten[b][m] * diff
                    parts[m] = term if parts[m] is None else parts[m] + term
            blocks += parts
        resid_ref[:, at : at + wide] = jnp.concatenate(blocks, 0).astype(BF16)
    owners, sides, _, _, span = out_ref.shape
    for owner in range(owners):
        own = slice(owner * span, (owner + 1) * span)
        back = jnp.dot(resid_ref[:, :held], near_ref[:, own], preferred_element_type=F32)
        back = back + jnp.dot(resid_ref[:, held:], rest_ref[:, own], preferred_element_type=F32)
        for slab in range(slabs):
            out_ref[owner, slab % sides, slab // sides] = back[
                slab * per_slab : (slab + 1) * per_slab
            ].astype(BF16)


def project(tiles, x_all, near, projector, counts, owners, sides, slabs, mats):
    rows, pix = x_all.shape
    cols = counts.shape[2]
    out = (owners, sides, slabs // sides, rows // slabs, pix // owners)
    return pl.pallas_call(
        functools.partial(project_kernel, mats, counts.shape[0], slabs),
        out_shape=jax.ShapeDtypeStruct(out, BF16),
        in_specs=[VMEM, VMEM, VMEM, HBM, VMEM],
        out_specs=VMEM,
        scratch_shapes=[
            pltpu.VMEM((rows, cols), BF16),
            pltpu.VMEM((cols - near.shape[0], pix), BF16),
            pltpu.SemaphoreType.DMA(((cols - near.shape[0]) // 512,)),
        ],
        compiler_params=pltpu.CompilerParams(vmem_limit_bytes=MEDIUM),
        cost_estimate=pl.CostEstimate(
            flops=4 * rows * cols * pix, bytes_accessed=2 * cols * pix, transcendentals=rows * cols
        ),
    )(tiles, x_all, near, projector, counts)


def next_pixel(field):
    column = lax.broadcasted_iota(jnp.int32, field.shape, 1) % PX
    return jnp.where(column == PX - 1, 0.0, pltpu.roll(field, field.shape[1] - 1, 1))


def next_row(field):
    return jnp.concatenate([field[:, PX:], jnp.zeros((field.shape[0], PX), F32)], 1)


def prev_pixel(flux):
    column = lax.broadcasted_iota(jnp.int32, flux.shape, 1) % PX
    return jnp.where(column == 0, 0.0, pltpu.roll(flux, 1, 1))


def prev_row(flux):
    return jnp.concatenate([jnp.zeros((flux.shape[0], PX), F32), flux[:, :-PX]], 1)


def slab_index():
    return lax.axis_index("pair") * lax.axis_size("side") + lax.axis_index("side")


def smooth_kernel(vol_ref, x_ref, edge_ref, out_ref):
    mats, depth, pix = vol_ref.shape
    slabs = x_ref.shape[0] // (mats * depth)
    slab = slab_index()
    first = jnp.logical_and(slab == 0, lax.axis_index("row") == 0)
    row = lax.broadcasted_iota(jnp.int32, (depth, pix), 0)
    vol, above, below = [], [], []
    for m in range(mats):
        vol.append(vol_ref[m])
        up = down = edge_ref[m : m + 1]
        for other in range(1, slabs):
            at = (other * mats + m) * depth
            up = jnp.where(slab == other - 1, x_ref[at : at + depth].astype(F32)[:1], up)
            at = ((other - 1) * mats + m) * depth
            down = jnp.where(slab == other, x_ref[at : at + depth].astype(F32)[-1:], down)
        above.append(jnp.where(row == depth - 1, up, pltpu.roll(vol[m], depth - 1, 0)))
        below.append(down)
    square = jnp.full((depth, pix), 0.25, F32)
    square_below = jnp.full((1, pix), 0.25, F32)
    diffs, steps = [], []
    for m in range(mats):
        dz, dy, dx = above[m] - vol[m], next_row(vol[m]) - vol[m], next_pixel(vol[m]) - vol[m]
        square = square + (dz * dz + dy * dy + dx * dx)
        diffs.append((dz, dy, dx))
        dz, dy, dx = vol[m][:1] - below[m], next_row(below[m]) - below[m], next_pixel(below[m]) - below[m]
        square_below = square_below + (dz * dz + dy * dy + dx * dx)
        steps.append(dz)
    scale = lax.rsqrt(square)
    scale_below = jnp.where(first, 0.0, lax.rsqrt(square_below))
    for m in range(mats):
        qz, qy, qx = (d * scale for d in diffs[m])
        prev_z = jnp.where(row == 0, steps[m] * scale_below, pltpu.roll(qz, 1, 0))
        out_ref[m] = prev_z - qz + (prev_row(qy) - qy) + (prev_pixel(qx) - qx)


def smooth(volume, x_all, edge):
    return pl.pallas_call(
        smooth_kernel,
        out_shape=jax.ShapeDtypeStruct(volume.shape, F32),
        in_specs=[VMEM, VMEM, VMEM],
        out_specs=VMEM,
        compiler_params=pltpu.CompilerParams(vmem_limit_bytes=SMALL),
        cost_estimate=pl.CostEstimate(
            flops=40 * volume.size, bytes_accessed=12 * volume.size, transcendentals=volume.size
        ),
    )(volume, x_all, edge)


def total_kernel(factor, part_ref, vol_ref, out_ref, edge_ref):
    total = jnp.sum(part_ref[...].astype(F32), axis=0) * factor
    total = total.astype(BF16)
    for half in range(out_ref.shape[0]):
        for owner in range(out_ref.shape[2]):
            out_ref[half, :, owner] = total
    slab = slab_index()
    for m in range(vol_ref.shape[0]):
        slab_m = vol_ref[m]
        edge_ref[m : m + 1] = jnp.where(slab == 0, slab_m[:1], slab_m[-1:])


def total_copies(parts, volume, factor, halves, owners):
    mats, _, pix = volume.shape
    return pl.pallas_call(
        functools.partial(total_kernel, factor),
        out_shape=[
            jax.ShapeDtypeStruct((halves, parts.shape[1], owners) + parts.shape[2:], BF16),
            jax.ShapeDtypeStruct((mats, pix), F32),
        ],
        in_specs=[VMEM, VMEM],
        out_specs=[VMEM, VMEM],
        compiler_params=pltpu.CompilerParams(vmem_limit_bytes=SMALL),
    )(parts, volume)


def step_kernel(grad_ref, smooth_ref, newton_ref, vol_ref, out_ref):
    mats, depth, pix = vol_ref.shape
    copies, owners, _, span = grad_ref.shape
    for owner in range(owners):
        own = slice(owner * span, (owner + 1) * span)
        grad = grad_ref[0, owner].astype(F32)
        for copy in range(1, copies):
            grad = grad + grad_ref[copy, owner].astype(F32)
        steps = [grad[k * depth : (k + 1) * depth] + 0.5 * smooth_ref[k, :, own] for k in range(mats)]
        for m in range(mats):
            moved = newton_ref[m, 0, :, own].astype(F32) * steps[0]
            for k in range(1, mats):
                moved = moved + newton_ref[m, k, :, own].astype(F32) * steps[k]
            out_ref[m, :, own] = vol_ref[m, :, own] - moved


def newton_step(grad, smoothed, newton, volume):
    return pl.pallas_call(
        step_kernel,
        out_shape=jax.ShapeDtypeStruct(volume.shape, F32),
        in_specs=[VMEM] * 4,
        out_specs=VMEM,
        compiler_params=pltpu.CompilerParams(vmem_limit_bytes=SMALL),
    )(grad, smoothed, newton, volume)


def body(volume, projector, counts, atten, newton):
    depth, mats, pix = volume.shape
    owners, halves, groups, pairs, sides = (
        lax.axis_size(name) for name in ("x", "half", "row", "pair", "side")
    )
    slabs = pairs * sides
    views_all = projector.shape[0] * owners * halves * slabs
    rows, span = mats * depth, pix // owners
    vol = volume.transpose(1, 0, 2)
    x_all = lax.all_to_all(spread(vol, slabs), ("pair", "side"), 0, 0, tiled=True)
    x_all = x_all.reshape(slabs * rows, pix)
    near, binned, tiles = stage(atten, projector[0], counts[0], projector.shape[1] // 2)
    parts = project(tiles, x_all, near, projector[0], binned, owners, sides, slabs, mats)
    parts = parts.reshape(owners * sides, pairs, rows, span)
    parts = lax.all_to_all(parts, ("x", "side"), 0, 0, tiled=True)
    mine, edge = total_copies(parts, vol, float(views_all) ** (-0.5), halves, owners)
    ends = []
    for g in range(groups - 1):
        last, start = g * slabs + slabs - 1, (g + 1) * slabs
        ends += [(last, start), (start, last)]
    edge = lax.ppermute(edge, ("row", "pair", "side"), ends)
    mine = mine.reshape(owners * halves * pairs, rows, span)
    grad = lax.all_to_all(mine, ("half", "pair", "x"), 0, 0, tiled=True)
    grad = grad.reshape(halves * pairs, owners, rows, span)
    smoothed = smooth(vol, x_all, edge)
    updated = newton_step(grad, smoothed, newton.transpose(1, 2, 0, 3), vol)
    return updated.transpose(1, 0, 2)


def solution(mesh):
    views, groups, slabs = mesh.devices.shape
    mesh = jax.sharding.Mesh(
        mesh.devices.reshape(views // 2, 2, groups, slabs // 2, 2),
        ("x", "half", "row", "pair", "side"),
    )
    view, slice_axes = ("x", "half", "pair", "side"), ("row", "pair", "side")
    in_specs = (
        P(slice_axes, None, None),
        P(view, None, None),
        P(view, "row", None, None),
        P(),
        P(slice_axes, None, None, None),
    )
    out_specs = P(slice_axes, None, None)
    return jax.shard_map(body, mesh=mesh, in_specs=in_specs, out_specs=out_specs, check_vma=False)
```

```python
import functools

import jax
import jax.numpy as jnp
from jax import lax
from jax.experimental import pallas as pl
from jax.experimental.pallas import tpu as pltpu
from jax.sharding import PartitionSpec as P

PX = 1024
BF16 = jnp.bfloat16
F32 = jnp.float32
VMEM = pl.BlockSpec(memory_space=pltpu.VMEM)
SMEM = pl.BlockSpec(memory_space=pltpu.SMEM)
HBM = pl.BlockSpec(memory_space=pltpu.HBM)
SMALL = 8 * 1024 * 1024
MEDIUM = 49 * 1024 * 1024
LARGE = 50 * 1024 * 1024
HUGE = 58 * 1024 * 1024


def spread_kernel(vol_ref, out_ref):
    mats = vol_ref.shape[0]
    rounded = jnp.concatenate([vol_ref[m] for m in range(mats)], 0).astype(BF16)
    for copy in range(out_ref.shape[0]):
        out_ref[copy] = rounded


def spread(volume, copies):
    mats, depth, pix = volume.shape
    return pl.pallas_call(
        spread_kernel,
        out_shape=jax.ShapeDtypeStruct((copies, mats * depth, pix), BF16),
        in_specs=[VMEM],
        out_specs=VMEM,
        compiler_params=pltpu.CompilerParams(vmem_limit_bytes=HUGE),
    )(volume)


def stage_kernel(atten_ref, proj_ref, counts_ref, near_ref, binned_ref, tiles_ref, sem):
    copy = pltpu.make_async_copy(proj_ref.at[: near_ref.shape[0]], near_ref, sem)
    copy.start()
    bins, mats = atten_ref.shape
    for b in range(bins):
        for m in range(mats):
            tiles_ref[b * mats + m] = jnp.full(tiles_ref.shape[1:], atten_ref[b, m], F32)
    for b in range(bins):
        binned_ref[b] = counts_ref[:, b, :].astype(F32)
    copy.wait()


def stage(atten, projector, counts, held):
    slices, bins, cols = counts.shape
    return pl.pallas_call(
        stage_kernel,
        out_shape=[
            jax.ShapeDtypeStruct((held, projector.shape[1]), BF16),
            jax.ShapeDtypeStruct((bins, slices, cols), F32),
            jax.ShapeDtypeStruct((atten.size, 8, 128), F32),
        ],
        in_specs=[SMEM, HBM, VMEM],
        out_specs=[VMEM] * 3,
        scratch_shapes=[pltpu.SemaphoreType.DMA(())],
        compiler_params=pltpu.CompilerParams(vmem_limit_bytes=LARGE),
        cost_estimate=pl.CostEstimate(flops=0, bytes_accessed=4 * projector.size, transcendentals=0),
    )(atten, projector, counts)


def wide_tile(tile, wide):
    return jnp.concatenate([tile] * (wide // tile.shape[1]), 1)


def project_kernel(mats, bins, slabs, tiles_ref, x_ref, near_ref, proj_ref, counts_ref, out_ref, resid_ref, rest_ref, sems):
    rows, pix = x_ref.shape
    cols, held = proj_ref.shape[0], near_ref.shape[0]
    wide = 512
    copies = [
        pltpu.make_async_copy(
            proj_ref.at[at : at + wide], rest_ref.at[at - held : at - held + wide], sems.at[i]
        )
        for i, at in enumerate(range(held, cols, wide))
    ]
    for copy in copies:
        copy.start()
    per_slab = rows // slabs
    depth = per_slab // mats
    atten = [[wide_tile(tiles_ref[b * mats + m], wide) for m in range(mats)] for b in range(bins)]
    for at in range(0, cols, wide):
        if at >= held:
            copies[(at - held) // wide].wait()
        block = near_ref[at : at + wide] if at < held else rest_ref[at - held : at - held + wide]
        line = lax.dot_general(
            x_ref[...], block, (((1,), (1,)), ((), ())), preferred_element_type=F32
        )
        blocks = []
        for slab in range(slabs):
            lines = [line[slab * per_slab + m * depth :][:depth] for m in range(mats)]
            parts = [None] * mats
            for b in range(bins):
                power = atten[b][0] * lines[0]
                for m in range(1, mats):
                    power = power + atten[b][m] * lines[m]
                seen = counts_ref[b, slab * depth : (slab + 1) * depth, at : at + wide]
                diff = seen - jnp.exp(-power)
                for m in range(mats):
                    term = atten[b][m] * diff
                    parts[m] = term if parts[m] is None else parts[m] + term
            blocks += parts
        resid_ref[:, at : at + wide] = jnp.concatenate(blocks, 0).astype(BF16)
    sides, owners, _, _, span = out_ref.shape
    for owner in range(owners):
        own = slice(owner * span, (owner + 1) * span)
        back = jnp.dot(resid_ref[:, :held], near_ref[:, own], preferred_element_type=F32)
        back = back + jnp.dot(resid_ref[:, held:], rest_ref[:, own], preferred_element_type=F32)
        for slab in range(slabs):
            out_ref[slab % sides, owner, slab // sides] = back[
                slab * per_slab : (slab + 1) * per_slab
            ].astype(BF16)


def project(tiles, x_all, near, projector, counts, owners, sides, slabs, mats):
    rows, pix = x_all.shape
    cols = counts.shape[2]
    out = (sides, owners, slabs // sides, rows // slabs, pix // owners)
    return pl.pallas_call(
        functools.partial(project_kernel, mats, counts.shape[0], slabs),
        out_shape=jax.ShapeDtypeStruct(out, BF16),
        in_specs=[VMEM, VMEM, VMEM, HBM, VMEM],
        out_specs=VMEM,
        scratch_shapes=[
            pltpu.VMEM((rows, cols), BF16),
            pltpu.VMEM((cols - near.shape[0], pix), BF16),
            pltpu.SemaphoreType.DMA(((cols - near.shape[0]) // 512,)),
        ],
        compiler_params=pltpu.CompilerParams(vmem_limit_bytes=MEDIUM),
        cost_estimate=pl.CostEstimate(
            flops=4 * rows * cols * pix, bytes_accessed=2 * cols * pix, transcendentals=rows * cols
        ),
    )(tiles, x_all, near, projector, counts)


def next_pixel(field):
    column = lax.broadcasted_iota(jnp.int32, field.shape, 1) % PX
    return jnp.where(column == PX - 1, 0.0, pltpu.roll(field, field.shape[1] - 1, 1))


def next_row(field):
    return jnp.concatenate([field[:, PX:], jnp.zeros((field.shape[0], PX), F32)], 1)


def prev_pixel(flux):
    column = lax.broadcasted_iota(jnp.int32, flux.shape, 1) % PX
    return jnp.where(column == 0, 0.0, pltpu.roll(flux, 1, 1))


def prev_row(flux):
    return jnp.concatenate([jnp.zeros((flux.shape[0], PX), F32), flux[:, :-PX]], 1)


def slab_index():
    return lax.axis_index("pair") * lax.axis_size("side") + lax.axis_index("side")


def smooth_kernel(vol_ref, x_ref, edge_ref, out_ref):
    mats, depth, pix = vol_ref.shape
    slabs = x_ref.shape[0] // (mats * depth)
    slab = slab_index()
    first = jnp.logical_and(slab == 0, lax.axis_index("row") == 0)
    row = lax.broadcasted_iota(jnp.int32, (depth, pix), 0)
    vol, above, below = [], [], []
    for m in range(mats):
        vol.append(vol_ref[m])
        up = down = edge_ref[m : m + 1]
        for other in range(1, slabs):
            at = (other * mats + m) * depth
            up = jnp.where(slab == other - 1, x_ref[at : at + depth].astype(F32)[:1], up)
            at = ((other - 1) * mats + m) * depth
            down = jnp.where(slab == other, x_ref[at : at + depth].astype(F32)[-1:], down)
        above.append(jnp.where(row == depth - 1, up, pltpu.roll(vol[m], depth - 1, 0)))
        below.append(down)
    square = jnp.full((depth, pix), 0.25, F32)
    square_below = jnp.full((1, pix), 0.25, F32)
    diffs, steps = [], []
    for m in range(mats):
        dz, dy, dx = above[m] - vol[m], next_row(vol[m]) - vol[m], next_pixel(vol[m]) - vol[m]
        square = square + (dz * dz + dy * dy + dx * dx)
        diffs.append((dz, dy, dx))
        dz, dy, dx = vol[m][:1] - below[m], next_row(below[m]) - below[m], next_pixel(below[m]) - below[m]
        square_below = square_below + (dz * dz + dy * dy + dx * dx)
        steps.append(dz)
    scale = lax.rsqrt(square)
    scale_below = jnp.where(first, 0.0, lax.rsqrt(square_below))
    for m in range(mats):
        qz, qy, qx = (d * scale for d in diffs[m])
        prev_z = jnp.where(row == 0, steps[m] * scale_below, pltpu.roll(qz, 1, 0))
        out_ref[m] = prev_z - qz + (prev_row(qy) - qy) + (prev_pixel(qx) - qx)


def smooth(volume, x_all, edge):
    return pl.pallas_call(
        smooth_kernel,
        out_shape=jax.ShapeDtypeStruct(volume.shape, F32),
        in_specs=[VMEM, VMEM, VMEM],
        out_specs=VMEM,
        compiler_params=pltpu.CompilerParams(vmem_limit_bytes=SMALL),
        cost_estimate=pl.CostEstimate(
            flops=40 * volume.size, bytes_accessed=12 * volume.size, transcendentals=volume.size
        ),
    )(volume, x_all, edge)


def total_kernel(factor, part_ref, vol_ref, out_ref, edge_ref):
    total = jnp.sum(part_ref[...].astype(F32), axis=0) * factor
    total = total.astype(BF16)
    for half in range(out_ref.shape[0]):
        for owner in range(out_ref.shape[2]):
            out_ref[half, :, owner] = total
    slab = slab_index()
    for m in range(vol_ref.shape[0]):
        slab_m = vol_ref[m]
        edge_ref[m : m + 1] = jnp.where(slab == 0, slab_m[:1], slab_m[-1:])


def total_copies(parts, volume, factor, halves, owners):
    mats, _, pix = volume.shape
    return pl.pallas_call(
        functools.partial(total_kernel, factor),
        out_shape=[
            jax.ShapeDtypeStruct((halves, parts.shape[1], owners) + parts.shape[2:], BF16),
            jax.ShapeDtypeStruct((mats, pix), F32),
        ],
        in_specs=[VMEM, VMEM],
        out_specs=[VMEM, VMEM],
        compiler_params=pltpu.CompilerParams(vmem_limit_bytes=SMALL),
    )(parts, volume)


def step_kernel(grad_ref, smooth_ref, newton_ref, vol_ref, out_ref):
    mats, depth, pix = vol_ref.shape
    copies, owners, _, span = grad_ref.shape
    for owner in range(owners):
        own = slice(owner * span, (owner + 1) * span)
        grad = grad_ref[0, owner].astype(F32)
        for copy in range(1, copies):
            grad = grad + grad_ref[copy, owner].astype(F32)
        steps = [grad[k * depth : (k + 1) * depth] + 0.5 * smooth_ref[k, :, own] for k in range(mats)]
        for m in range(mats):
            moved = newton_ref[m, 0, :, own].astype(F32) * steps[0]
            for k in range(1, mats):
                moved = moved + newton_ref[m, k, :, own].astype(F32) * steps[k]
            out_ref[m, :, own] = vol_ref[m, :, own] - moved


def newton_step(grad, smoothed, newton, volume):
    return pl.pallas_call(
        step_kernel,
        out_shape=jax.ShapeDtypeStruct(volume.shape, F32),
        in_specs=[VMEM] * 4,
        out_specs=VMEM,
        compiler_params=pltpu.CompilerParams(vmem_limit_bytes=SMALL),
    )(grad, smoothed, newton, volume)


def body(volume, projector, counts, atten, newton):
    depth, mats, pix = volume.shape
    owners, halves, groups, pairs, sides = (
        lax.axis_size(name) for name in ("x", "half", "row", "pair", "side")
    )
    slabs = pairs * sides
    views_all = projector.shape[0] * owners * halves * slabs
    rows, span = mats * depth, pix // owners
    vol = volume.transpose(1, 0, 2)
    x_all = lax.all_to_all(spread(vol, slabs), ("pair", "side"), 0, 0, tiled=True)
    x_all = x_all.reshape(slabs * rows, pix)
    near, binned, tiles = stage(atten, projector[0], counts[0], projector.shape[1] // 2)
    parts = project(tiles, x_all, near, projector[0], binned, owners, sides, slabs, mats)
    parts = parts.reshape(owners * sides, pairs, rows, span)
    parts = lax.all_to_all(parts, ("side", "x"), 0, 0, tiled=True)
    mine, edge = total_copies(parts, vol, float(views_all) ** (-0.5), halves, owners)
    ends = []
    for g in range(groups - 1):
        last, start = g * slabs + slabs - 1, (g + 1) * slabs
        ends += [(last, start), (start, last)]
    edge = lax.ppermute(edge, ("row", "pair", "side"), ends)
    mine = mine.reshape(owners * halves * pairs, rows, span)
    grad = lax.all_to_all(mine, ("half", "pair", "x"), 0, 0, tiled=True)
    grad = grad.reshape(halves * pairs, owners, rows, span)
    smoothed = smooth(vol, x_all, edge)
    updated = newton_step(grad, smoothed, newton.transpose(1, 2, 0, 3), vol)
    return updated.transpose(1, 0, 2)


def solution(mesh):
    views, groups, slabs = mesh.devices.shape
    mesh = jax.sharding.Mesh(
        mesh.devices.reshape(views // 2, 2, groups, slabs // 2, 2),
        ("x", "half", "row", "pair", "side"),
    )
    view, slice_axes = ("x", "half", "pair", "side"), ("row", "pair", "side")
    in_specs = (
        P(slice_axes, None, None),
        P(view, None, None),
        P(view, "row", None, None),
        P(),
        P(slice_axes, None, None, None),
    )
    out_specs = P(slice_axes, None, None)
    return jax.shard_map(body, mesh=mesh, in_specs=in_specs, out_specs=out_specs, check_vma=False)
```
